128 devices in a mesh: au: 16 (over y, z), vert: 8 (over x, core).
Axes of the slice: x: 4, y: 4, z: 4, core: 2. Of those that a mesh axis runs over, the one named last changes fastest.
Arguments:
- visibilities: bfloat16 [2048, 2, 2, 256], P(('au', 'vert')), may hold values from -6 to 6
- keep_flags: int32 [2048, 256], P(('au', 'vert')), may hold values 0 or 1
- kernel_index: int32 [2048, 256], P(('au', 'vert')), may hold values from 0 to 31
- row_offset: int32 [2048, 256], P(('au', 'vert')), may hold values from 0 to 127
- col_offset: int32 [2048, 256], P(('au', 'vert')), may hold values from 0 to 127
- cell_index: int32 [2048], P(('au', 'vert')), may hold values from 0 to 31
- tile_row: int32 [2048, 1], P(('au', 'vert')), may hold values from 0 to 15; in each aligned block of 16 rows (0 to 15, 16 to 31, ...) at most 2 rows name the same one
- kernel_taps: float32 [32, 2, 16], replicated, may hold values from -1 to 1
Outputs:
- dirty_gradient: float32 [2, 8192, 8192], P(None, ('au', 'vert'))
The draws below stay inside these ranges and needn't reach their ends.
Inputs may be any that keep to these rules, and one draw needn't show every extreme that they name: `tile_row`: of one device's 16 blocks at most 2 name the same tile row, and in every draw some device has exactly 2 for some tile row.
All inputs are finite; a program needn't handle non-finite values. No bound on the sum of `keep_flags` on one device may be relied on, other than what follows from the above.
Results may differ from the reference program's by a relative error of at most 0.0041.
Values may be sent and summed in bfloat16 or wider, within the bound.
A program may use at most 192 MiB of HBM per device.

```python
import math
import jax
import jax.numpy as jnp
import numpy as np
from jax import lax

PLANES = 2
KVIS = 256
TAPS = 16
WPLANES = 32
CELL = 128
TILE_R = 512
TILE_C = 1024
NB_DEV = 16
TILES_U = 16
TILES_V = 8
BLOCKS = 2048
CAP = 2
CELLS = 32
GRID_R = 8192
GRID_C = 8192


def place_ends(result, rng, low, high):
    place = [jax.random.randint(jax.random.fold_in(rng, axis), (), 0, length) for axis, length in enumerate(result.shape)]
    widest = result.shape.index(max(result.shape))
    neighbour = place[:widest] + [(place[widest] + 1) % result.shape[widest]] + place[widest + 1:]
    return result.at[tuple(place)].set(low).at[tuple(neighbour)].set(high)


def level_of(own_key, shape, pieces, least, high):
    gain, own = 1.0, jax.random.fold_in(own_key, 6)
    for dim, shards_of in pieces:
        heights = jnp.exp(jax.random.uniform(jax.random.fold_in(own, dim), (shards_of,), jnp.float32, least / len(pieces), high / len(pieces)))
        gain = gain * jnp.repeat(heights, shape[dim] // shards_of).reshape([-1 if axis == dim else 1 for axis in range(len(shape))])
    return gain


def shared_out(own_key, own, number, rows, count, top, limit, skew):
    order = jax.random.permutation(own_key, count)
    crowded, usual = load_shares(count, rows * top, limit, skew, True), load_shares(count, rows * top, limit, skew, False)
    places = jnp.arange(count)

    def named(tallies, turn):
        used = int((tallies > 0).sum())
        fixed = max(1, used // 4)
        shifted = fixed + (places - fixed + turn * (used - fixed)) % max(1, count - fixed)
        return jnp.zeros((count,), jnp.int32).at[order[jnp.where(places < fixed, places, shifted)]].set(jnp.asarray(tallies, jnp.int32))

    tallies = jnp.where(number % 4 == 0, named(crowded, number // 4), named(usual, number - number // 4 - 1))
    mixed = jax.random.permutation(jax.random.fold_in(own, 3), count)
    giver, sink = mixed[0:count // 2 * 2:2], mixed[1:count // 2 * 2:2]
    room = jnp.minimum(tallies[giver] - 1, limit - tallies[sink]) // 2
    room = jnp.where((giver == order[0]) | (sink == order[0]) | (tallies[sink] == 0), 0, jnp.maximum(room, 0))
    shifted = jax.random.randint(jax.random.fold_in(own, 4), (count // 2,), 0, 1 << 20) % (room + 1)
    tallies = tallies.at[giver].add(-shifted).at[sink].add(shifted)
    items = jnp.searchsorted(jnp.cumsum(tallies), jnp.arange(rows * top), side="right").astype(jnp.int32)
    table = items.reshape(top, rows).T
    table = table[jax.random.permutation(jax.random.fold_in(own, 1), rows)]
    turn = jax.random.randint(jax.random.fold_in(own, 2), (rows, 1), 0, top)
    return jnp.take_along_axis(table, (jnp.arange(top)[None, :] + turn) % top, axis=1)


def load_shares(count, total, limit, slope, full):
    loads = [(1 << 20) // math.isqrt(rank ** slope) + 1 for rank in range(1, count + 1)]
    largest = limit if full else min(limit, max(-(-total // count), total * loads[0] // sum(loads)))
    least = 1 if total - largest >= count - 1 else 0
    counts, rest = [largest] + [least] * (count - 1), total - largest - least * (count - 1)
    while rest > 0:
        candidates = [i for i in range(1, count) if counts[i] < largest] or [i for i in range(1, count) if counts[i] < limit]
        pool, budget = sum([loads[i] for i in candidates]), rest
        for i in candidates:
            more = min(limit - counts[i], max(1, budget * loads[i] // pool), rest)
            counts[i] = counts[i] + more
            rest = rest - more
    return np.array(counts)


def noise(key, dims, spread, most, split=(), kind=jnp.bfloat16):
    drawn = jax.random.normal(key, dims, jnp.float32) * spread
    if len(split) > 0:
        drawn = level_of(key, dims, split, -0.22, 0.18) * drawn
    return jnp.clip(drawn, min=-most, max=most).astype(kind)


def setup_inputs(seed: int = 0) -> dict:
    keys = jax.random.split(jax.random.key(seed), 9)
    visibilities = noise(keys[0], (BLOCKS, PLANES, 2, KVIS), 1.0, 6.0, ((0, 128),))
    keep_flags = place_ends((jax.random.randint(keys[1], (BLOCKS, KVIS), 0, 8) < 7).astype(jnp.int32), jax.random.fold_in(keys[1], 1), 0, 1)
    kernel_index = place_ends(jax.random.randint(keys[2], (BLOCKS, KVIS), 0, WPLANES), jax.random.fold_in(keys[2], 1), 0, WPLANES - 1).astype(jnp.int32)
    row_offset = place_ends(jax.random.randint(keys[3], (BLOCKS, KVIS), 0, CELL), jax.random.fold_in(keys[3], 1), 0, CELL - 1).astype(jnp.int32)
    col_offset = place_ends(jax.random.randint(keys[4], (BLOCKS, KVIS), 0, CELL), jax.random.fold_in(keys[4], 1), 0, CELL - 1).astype(jnp.int32)
    cell_index = place_ends(jax.random.randint(keys[5], (BLOCKS,), 0, CELLS), jax.random.fold_in(keys[5], 1), 0, CELLS - 1).astype(jnp.int32)
    tile_row_keys = jax.random.split(jax.random.fold_in(keys[6], 1), BLOCKS // NB_DEV)
    tile_row_turns = jax.random.permutation(jax.random.fold_in(keys[6], 3), BLOCKS // NB_DEV)
    tile_row = jax.vmap(lambda own, number: shared_out(jax.random.fold_in(keys[6], 2), own, number, NB_DEV, TILES_U, 1, CAP, 2))(tile_row_keys, tile_row_turns).reshape((BLOCKS, 1))
    kernel_taps = noise(keys[7], (WPLANES, 2, TAPS), 0.18, 1.0, (), jnp.float32)
    return dict(visibilities=visibilities, keep_flags=keep_flags, kernel_index=kernel_index, row_offset=row_offset, col_offset=col_offset, cell_index=cell_index, tile_row=tile_row, kernel_taps=kernel_taps)


exact_mode = lax.Precision.HIGHEST

def weighted_taps(masked, kernel_index, kernel_taps):
    wplane_count = kernel_taps.shape[0]
    selector = (kernel_index[..., None] == jnp.arange(wplane_count, dtype=jnp.int32)).astype(jnp.float32)
    taps_full = jnp.einsum('bkw,wct->bckt', selector, kernel_taps.astype(jnp.float32), precision=exact_mode)
    values = masked.astype(jnp.float32)
    real_vis = values[:, :, 0, :, None]
    imag_vis = values[:, :, 1, :, None]
    real_tap = taps_full[:, None, 0]
    imag_tap = taps_full[:, None, 1]
    weighted = jnp.stack([real_vis * real_tap - imag_vis * imag_tap, real_vis * imag_tap + imag_vis * real_tap], axis=2)
    return (weighted.astype(jnp.bfloat16), taps_full.astype(jnp.bfloat16))

def make_patches(weighted, taps, row_pos, col_pos, patch_size):
    tap_count = taps.shape[-1]
    span_idx = jnp.arange(patch_size, dtype=jnp.int32)
    tap_steps = jnp.arange(tap_count, dtype=jnp.int32)
    row_hit = (row_pos[:, :, None, None] + tap_steps[None, None, :, None] == span_idx).astype(jnp.float32)
    col_hit = (col_pos[:, :, None, None] + tap_steps[None, None, :, None] == span_idx).astype(jnp.float32)
    row_kernel = jnp.einsum('bpckt,bkta->bpcka', weighted.astype(jnp.float32), row_hit, precision=exact_mode)
    col_kernel = jnp.einsum('bdkt,bktl->bdkl', taps.astype(jnp.float32), col_hit, precision=exact_mode)
    products = jnp.einsum('bpcka,bdkl->bpcdal', row_kernel, col_kernel, precision=exact_mode)
    real_part = products[:, :, 0, 0] - products[:, :, 1, 1]
    imag_part = products[:, :, 0, 1] + products[:, :, 1, 0]
    return jnp.stack([real_part, imag_part], axis=2)

def reference(visibilities, keep_flags, kernel_index, row_offset, col_offset, cell_index, tile_row, kernel_taps):
    patch_size = CELL + TAPS
    cells_across = TILE_C // CELL
    masked = jnp.where(keep_flags[:, None, None, :] == 1, visibilities, jnp.zeros_like(visibilities))
    group_count = BLOCKS // NB_DEV
    grouped = (masked.reshape(group_count, NB_DEV, PLANES, 2, KVIS), kernel_index.reshape(group_count, NB_DEV, KVIS), row_offset.reshape(group_count, NB_DEV, KVIS), col_offset.reshape(group_count, NB_DEV, KVIS), cell_index.reshape(group_count, NB_DEV), tile_row.reshape(group_count, NB_DEV), jnp.arange(group_count, dtype=jnp.int32))
    zero_start = jnp.zeros((), jnp.int32)

    def one_group(grid, group):
        vis_group, index_group, rows_group, cols_group, cells_group, tiles_group, number = group
        weighted, taps = weighted_taps(vis_group, index_group, kernel_taps)
        patches = make_patches(weighted, taps, rows_group, cols_group, patch_size)
        column = number % TILES_V
        anchor_row = (tiles_group * TILE_R + cells_group // cells_across * CELL).astype(jnp.int32)
        anchor_col = (column * TILE_C + cells_group % cells_across * CELL).astype(jnp.int32)

        def add_block(position, current):
            starts = (zero_start, zero_start, anchor_row[position], anchor_col[position])
            piece = lax.dynamic_slice(current, starts, (PLANES, 2, patch_size, patch_size))
            return lax.dynamic_update_slice(current, piece + patches[position], starts)
        return (lax.fori_loop(0, NB_DEV, add_block, grid), None)
    start_grid = jnp.zeros((PLANES, 2, GRID_R + TAPS, GRID_C + TAPS), jnp.float32)
    grid = lax.scan(one_group, start_grid, grouped)[0]
    cropped = grid[:, :, :GRID_R, :GRID_C]
    field = lax.complex(cropped[:, 0], cropped[:, 1])
    image = jnp.fft.ifft2(field, axes=(1, 2)) * (GRID_R * GRID_C)
    scale = 1.0 / math.sqrt(BLOCKS * KVIS)
    return (jnp.real(image) * scale).transpose(0, 2, 1).astype(jnp.float32)
```

```python
import functools
import math

import jax
import jax.numpy as jnp
import numpy as np
from jax import lax
from jax.experimental import pallas as pl
from jax.experimental.pallas import tpu as pltpu
from jax.sharding import PartitionSpec as P

KVIS = 256
TAPS = 16
TILE_R = 512
TILE_C = 1024
NB_DEV = 16
BLOCKS = 2048
GRID = 8192
DEVICES = 128
ROWS = 32
HEAD = 16
WINDOW = 152
UNROLL = 4
BOTH = ("au", "vert")
F32 = jnp.float32
BF16 = jnp.bfloat16
I32 = jnp.int32
NT = (((1,), (1,)), ((), ()))
BIT_MUL = 0x077CB531


def bit_table():
    table = np.zeros(32, np.int32)
    for bit in range(32):
        table[((BIT_MUL << bit) & 0xFFFFFFFF) >> 27] = bit
    return table


def hi_lo(values):
    high = values.astype(jnp.bfloat16)
    low = (values - high.astype(np.float64)).astype(jnp.bfloat16)
    return high, low


@functools.lru_cache(None)
def column_tables():
    v0, c1 = np.arange(64), np.arange(64)
    c0 = np.arange(128)
    angle = 2 * np.pi / GRID * ((v0[None, :, None] * (128 * c1[None, None, :] + c0[:, None, None])) % GRID)
    first = np.concatenate([np.cos(angle), np.sin(angle)], axis=1)
    first = np.concatenate(hi_lo(first), axis=2)
    angle = 2 * np.pi / 128 * ((c0[:, None] * c0[None, :]) % 128)
    second = np.concatenate(hi_lo(np.concatenate([np.cos(angle), np.sin(angle)], axis=1)), axis=0)
    angle = 2 * np.pi / GRID * (v0[:, None] * c0[None, :])
    turn = np.concatenate([np.cos(angle), np.sin(angle)], axis=0).astype(np.float32)
    return first, second, turn


@functools.lru_cache(None)
def row_tables():
    scale = 1.0 / math.sqrt(BLOCKS * KVIS)
    u0, s = np.arange(256), np.arange(128)
    angle = 2 * np.pi / 256 * ((u0[:, None] * s[None, :]) % 256)
    first = np.concatenate([np.cos(angle), np.sin(angle)], axis=1).astype(jnp.bfloat16)
    comp, j = np.arange(128) // 64, np.arange(128) % 32
    plane = np.arange(128) // 32 % 2
    angle = 2 * np.pi / GRID * (u0[:, None] * j[None, :])
    turn_cos = (np.cos(angle) * scale).astype(np.float32)
    turn_sin = (np.sin(angle) * np.where(comp == 0, -1.0, 1.0) * scale).astype(np.float32)
    alternate = ((1.0 - 2.0 * (u0 % 2))[:, None] * ((comp == 0) & (j == 0))[None, :]).astype(np.float32)
    u1 = np.arange(32)
    angle = 2 * np.pi / 32 * ((u1[:, None] * j[None, :]) % 32)
    last = np.where(comp == 0, np.cos(angle), -np.sin(angle))
    last = np.concatenate([last * (plane == p) for p in range(2)], axis=0)
    last = np.concatenate(hi_lo(last), axis=1)
    return first, np.stack([turn_cos, turn_sin, alternate]), last


def iota(shape, dim):
    return lax.broadcasted_iota(I32, shape, dim)


def ones_where(mask):
    return jnp.where(mask, 1.0, 0.0).astype(BF16)


def dot(a, b):
    return jnp.dot(a, b, preferred_element_type=F32)


def dot_nt(a, b):
    return lax.dot_general(a, b, NT, preferred_element_type=F32)


def sort_kernel(x_ref, out_ref):
    below = ones_where(iota((128, 128), 1) < iota((128, 128), 0))
    before = ones_where(iota((KVIS, KVIS), 0) < iota((KVIS, KVIS), 1))
    ones = jnp.ones((KVIS, KVIS), BF16)
    value = iota((128, KVIS), 0)
    place = iota((KVIS, KVIS), 0)

    def one_block(i, carry):
        x = x_ref[i]
        row = x.astype(F32)[4:5].astype(I32)
        hit = value == row
        hot = ones_where(hit)
        rank = dot(hot, before) + dot(dot(below, hot).astype(BF16), ones)
        rank = jnp.sum(jnp.where(hit, rank, 0.0), axis=0, keepdims=True)
        moved = dot_nt(x, ones_where(place == rank.astype(I32)))
        both = jnp.concatenate([moved[:, :128], moved[:, 128:]], axis=0)
        out_ref[pl.ds(pl.multiple_of(i * 16, 16), 16), :] = both.astype(BF16)
        return carry

    lax.fori_loop(0, NB_DEV, one_block, 0, unroll=2)


def pick(halves, index, low):
    first, second = [jnp.take_along_axis(half, index, axis=0, mode="promise_in_bounds") for half in halves]
    return jnp.where(low, first, second)


def placed(sources, tap, limit):
    halves = [(source[:8], source[8:]) for source in sources]
    parts = [[] for _ in sources]
    for i in range(tap.shape[0] // 8):
        t = tap[8 * i : 8 * i + 8]
        inside = (t >= 0) & (t < limit)
        low = t < 8
        index = t & 7
        for out, pair in zip(parts, halves):
            out.append(jnp.where(inside, pick(pair, index, low), 0.0))
    return [jnp.concatenate(part, axis=0) for part in parts]


def grid_kernel(
    words, meta, bits, strip, x_ref, taps_ref, first_ref, second_ref, turn_ref,
    out_ref, acc, mid, stage, acc4, extra, items,
):
    s = strip[0]
    acc[...] = jnp.zeros_like(acc)
    acc4[...] = jnp.zeros_like(acc4)
    table = taps_ref[...]
    table_hi = table.astype(BF16)
    table_lo = (table - table_hi.astype(F32)).astype(BF16)
    both_tables = jnp.concatenate([table_hi, table_lo], axis=0)

    def listed(kind, count):
        def group(g, n):
            def step(state):
                word, n = state
                low = word & -word
                bit = bits[lax.shift_right_logical(low * BIT_MUL, 27)]
                items[n] = (kind << 12) | ((g * NB_DEV + (bit & 15)) << 1) | (bit >> 4)
                return word ^ low, n + 1

            return lax.while_loop(lambda state: state[0] != 0, step, (words[kind * 128 + g], n))[1]

        return lax.fori_loop(0, 128, group, count)

    def loaded(code):
        half, block = code & 1, (code >> 1) & (BLOCKS - 1)
        where = meta[block]
        cell = (where >> 14) & 31
        anchor_row = (where >> 19) * TILE_R + (cell >> 3) * 128
        anchor_col = ((block >> 4) & 7) * TILE_C + (cell & 7) * 128
        x = x_ref[pl.ds(pl.multiple_of(block * 16, 16), 16), :].astype(F32)
        x = jnp.where(half == 1, x[8:], x[:8])
        row, col, wplane = [x[i : i + 1].astype(I32) for i in (4, 5, 6)]
        chosen = ones_where(iota((32, 128), 0) == wplane)
        taps = dot(both_tables, chosen)
        tap_re, tap_im = taps[:16], taps[16:32]
        full_re, full_im = tap_re + taps[32:48], tap_im + taps[48:64]
        weights_re, weights_im = [], []
        for p in range(2):
            re, im = x[2 * p : 2 * p + 1], x[2 * p + 1 : 2 * p + 2]
            weights_re.append((re * full_re - im * full_im).astype(BF16).astype(F32))
            weights_im.append((re * full_im + im * full_re).astype(BF16).astype(F32))
        limit = jnp.minimum(jnp.where(anchor_col == GRID - 128, 128, 1000) - col, TAPS)
        return anchor_row, anchor_col, row, col, (tap_re, tap_im), weights_re + weights_im, limit

    def item(code, valid):
        anchor_row, anchor_col, row, col, taps, weights, limit = loaded(code)
        mirror = (code >> 12) == 1
        sign = jnp.where(mirror, -1, 1)
        base = jnp.where(mirror, GRID - s * ROWS, s * ROWS) - anchor_row
        base = jnp.where(valid, base, -100000)
        least = jnp.where(mirror & (s == 0), 1, 0)
        j = iota((ROWS, 128), 0)
        tap = jnp.where(j < least, -1, base + sign * j - row)
        re0, re1, im0, im1 = placed(weights, tap, TAPS)
        flip = jnp.where(mirror, -1.0, 1.0)
        left = jnp.concatenate([re0, re1, im0 * flip, im1 * flip], axis=0).astype(BF16)
        right = jnp.concatenate([-im0, -im1, re0 * flip, re1 * flip], axis=0).astype(BF16)
        tap = jnp.where(mirror, 144, 0) + sign * iota((WINDOW, 128), 0) - col
        col_re, col_im = placed(taps, tap, limit)
        cols = jnp.concatenate([col_re.astype(BF16), col_im.astype(BF16)], axis=1)
        patch = dot_nt(cols, jnp.concatenate([left, right], axis=1))
        start = jnp.where(mirror, GRID - 128 - anchor_col, anchor_col + HEAD)
        return pl.multiple_of(start, 16), patch

    count = listed(1, listed(0, 0))

    def several(i, carry):
        found = []
        for k in range(UNROLL):
            n = i * UNROLL + k
            valid = n < count
            found.append(item(jnp.where(valid, items[n], 0), valid))
        for start, patch in found:
            acc[pl.ds(start, WINDOW), :] += patch
        return carry

    lax.fori_loop(0, (count + UNROLL - 1) // UNROLL, several, 0)
    acc[HEAD : HEAD + 8, :] += jnp.where(iota((8, 128), 0) == 0, acc[HEAD + GRID : HEAD + GRID + 8, :], 0.0)

    count4 = listed(2, 0)

    def single(i, carry):
        anchor_row, anchor_col, row, col, taps, weights, limit = loaded(items[i])
        tap = jnp.broadcast_to(GRID // 2 - anchor_row - row, (8, 128))
        re0, re1, im0, im1 = placed(weights, tap, TAPS)
        q = iota((8, 128), 0)
        left = jnp.where(q == 0, re0, jnp.where(q == 1, re1, jnp.where(q == 2, im0, jnp.where(q == 3, im1, 0.0))))
        right = jnp.where(q == 0, -im0, jnp.where(q == 1, -im1, jnp.where(q == 2, re0, jnp.where(q == 3, re1, 0.0))))
        rows = jnp.concatenate([left, right], axis=1).astype(BF16)
        tap = iota((WINDOW, 128), 0) - col
        col_re, col_im = placed(taps, tap, limit)
        cols = jnp.concatenate([col_re, col_im], axis=1)
        tail = jnp.concatenate([cols[128:], jnp.zeros((256 - WINDOW, 256), F32)], axis=0)
        c1 = anchor_col >> 7
        acc4[pl.ds(pl.multiple_of(c1 * 8, 8), 8), :] += dot_nt(rows, cols[:128].astype(BF16))
        acc4[pl.ds(pl.multiple_of(c1 * 8 + 8, 8), 8), :] += dot_nt(rows, tail.astype(BF16))
        return carry

    lax.fori_loop(0, count4, single, 0)

    lane = iota((1, 128), 1)
    flip = jnp.where(lane < 64, -1.0, 1.0)

    @pl.when(s != 0)
    def _():
        extra[...] = jnp.zeros_like(extra)

    @pl.when(s == 0)
    def _():
        cosine = first_ref[0, :64, :64]
        sine = first_ref[0, 64:, :64]
        turn_cos, turn_sin = turn_ref[:64], turn_ref[64:]
        for p in range(2):
            re = acc4[pl.ds(p, 64, stride=8), :].astype(BF16)
            im = acc4[pl.ds(2 + p, 64, stride=8), :].astype(BF16)
            mid_re = dot(cosine, re) - dot(sine, im)
            mid_im = dot(cosine, im) + dot(sine, re)
            turned_re = (mid_re * turn_cos - mid_im * turn_sin).astype(BF16)
            turned_im = (mid_re * turn_sin + mid_im * turn_cos).astype(BF16)
            got = dot_nt(second_ref[:128, :128], turned_re) - dot_nt(second_ref[:128, 128:], turned_im)
            extra[p] = got.astype(BF16)

    def column_first(c0, carry):
        h = acc[pl.ds(HEAD + c0, 64, stride=128), :]
        high = h.astype(BF16)
        low = (h - high.astype(F32)).astype(BF16)
        factors = first_ref[c0]
        got = dot(
            jnp.concatenate([factors, factors], axis=1), jnp.concatenate([high, high, low, low], axis=0)
        )
        y = got[:64] + flip * pltpu.roll(got[64:], 64, 1)
        mid[pl.ds(pl.multiple_of(c0 * 64, 64), 64), :] = y
        return carry

    lax.fori_loop(0, 128, column_first, 0, unroll=4)

    special = (s == 0) & ((lane == 64) | (lane == 96))
    keep = jnp.where(special, 0.0, 1.0)
    second_hi = second_ref[:128]
    second_lo = second_ref[128:]
    spot = iota((64, 128), 0)
    spot_lane = iota((64, 128), 1)

    for group in range(4):

        def column_second(v, carry):
            v0 = group * 16 + v
            y = mid[pl.ds(v0, 128, stride=64), :]
            turned = flip * pltpu.roll(y, 64, 1)
            pair = jnp.concatenate([y.astype(BF16), turned.astype(BF16)], axis=0)
            z = dot(second_hi, pair) + dot(second_lo, pair)
            more = dot(extra[0], ones_where((spot == v0) & (spot_lane == 64)))
            more = more + dot(extra[1], ones_where((spot == v0) & (spot_lane == 96)))
            stage[pl.ds(v, 128, stride=16), :] = z * keep + more
            return carry

        lax.fori_loop(0, 16, column_second, 0, unroll=2)

        def pack(d, carry):
            out_ref[d, group * 16 : group * 16 + 16, :] = stage[
                pl.ds(pl.multiple_of(d * 16, 16), 16), :
            ].astype(BF16)
            return carry

        lax.fori_loop(0, 128, pack, 0, unroll=8)


def image_kernel(in_ref, first_ref, turn_ref, last_ref, out_ref, wide, left, right):
    def widen(s, carry):
        wide[pl.ds(pl.multiple_of(s * 16, 16), 16), :] = in_ref[s].astype(F32)
        return carry

    lax.fori_loop(0, DEVICES, widen, 0, unroll=8)
    flip = jnp.where(iota((1, 128), 1) < 64, -1.0, 1.0)
    first = first_ref[...]
    last = last_ref[...]

    def one(v, carry):
        y = wide[pl.ds(v, DEVICES, stride=16), :]
        rolled = pltpu.roll(y, 64, 1)
        pair = jnp.concatenate([y.astype(BF16), (flip * rolled).astype(BF16)], axis=0)
        got = dot(first, pair) + turn_ref[2] * rolled[:1]
        turned = (got * turn_ref[0] + pltpu.roll(got, 64, 1) * turn_ref[1]).astype(BF16)
        result = dot_nt(last, jnp.concatenate([turned, turned], axis=1))
        left[pl.ds(pl.multiple_of(v * 64, 64), 64), :] = result[:, :128]
        right[pl.ds(pl.multiple_of(v * 64, 64), 64), :] = result[:, 128:]
        return carry

    lax.fori_loop(0, 16, one, 0, unroll=2)

    def place(u1, carry):
        for p in range(2):
            for half in range(2):
                for side, ref in ((0, left), (1, right)):
                    out_ref[p, half * 8 : half * 8 + 8, pl.ds(pl.multiple_of(u1 * 256 + side * 128, 128), 128)] = (
                        ref[pl.ds(half * 512 + p * 32 + u1, 8, stride=64), :]
                    )
        return carry

    lax.fori_loop(0, 32, place, 0, unroll=2)


def words_of(code, s):
    row = (code >> 19) * TILE_R + ((code >> 17) & 3) * 128
    top, bottom = (code >> 7) & 127, code & 127
    shift = jnp.arange(NB_DEV, dtype=I32)[None, :]

    def packed(first, final):
        hit = (final >= 0) & (first < 128 + TAPS - 1)
        one = (hit & (top >= first - (TAPS - 1))).astype(I32)
        two = (hit & (bottom <= final)).astype(I32)
        both = one.reshape(128, NB_DEV) << shift | two.reshape(128, NB_DEV) << (shift + 16)
        return jnp.sum(both, axis=1)

    direct = s * ROWS - row
    mirror = GRID - ROWS + 1 - s * ROWS - row
    middle = GRID // 2 - row
    middle = packed(middle, middle) * (s == 0).astype(I32)
    return jnp.concatenate([packed(direct, direct + ROWS - 1), packed(mirror, mirror + ROWS - 1), middle])


def shards(visibilities, keep_flags, kernel_index, row_offset, col_offset, cell_index, tile_row, kernel_taps):
    s = lax.axis_index("au") * 8 + lax.axis_index("vert")
    masked = jnp.where(keep_flags[:, None, :] == 1, visibilities.reshape(NB_DEV, 4, KVIS), 0).astype(BF16)
    codes = jnp.stack([row_offset, col_offset, kernel_index, jnp.zeros_like(row_offset)], axis=1)
    x8 = jnp.concatenate([masked, codes.astype(BF16)], axis=1)
    vmem = pl.BlockSpec(memory_space=pltpu.VMEM)
    smem = pl.BlockSpec(memory_space=pltpu.SMEM)
    ordered = pl.pallas_call(
        sort_kernel,
        out_shape=jax.ShapeDtypeStruct((NB_DEV * 16, 128), BF16),
        in_specs=[vmem],
        out_specs=vmem,
        name="sort_blocks",
    )(x8)
    by_block = ordered.reshape(NB_DEV, 16, 128)
    top = by_block[:, 4, 127].astype(I32)
    bottom = by_block[:, 12, 0].astype(I32)
    code = ((tile_row[:, 0] * 32 + cell_index) << 14) | (top << 7) | bottom
    codes_all = lax.all_gather(code, BOTH, axis=0, tiled=True)
    x_all = lax.all_gather(ordered, BOTH, axis=0, tiled=True)
    words = words_of(codes_all, s)
    first, second, turn = column_tables()
    taps = kernel_taps.transpose(1, 2, 0).reshape(2 * TAPS, 32)
    sent = pl.pallas_call(
        grid_kernel,
        out_shape=jax.ShapeDtypeStruct((DEVICES, 64, 128), BF16),
        in_specs=[smem] * 4 + [vmem] * 5,
        out_specs=vmem,
        scratch_shapes=[
            pltpu.VMEM((HEAD + GRID + 32, 128), F32),
            pltpu.VMEM((128 * 64, 128), F32),
            pltpu.VMEM((DEVICES * 16, 128), F32),
            pltpu.VMEM((66 * 8, 128), F32),
            pltpu.VMEM((2, 128, 64), BF16),
            pltpu.SMEM((4096,), I32),
        ],
        compiler_params=pltpu.CompilerParams(vmem_limit_bytes=56 * 1024 * 1024),
        name="grid_columns",
    )(
        words, codes_all, jnp.asarray(bit_table()), s.reshape(1).astype(I32),
        x_all, taps, jnp.asarray(first), jnp.asarray(second), jnp.asarray(turn),
    )
    got = lax.all_to_all(sent, BOTH, split_axis=0, concat_axis=0, tiled=True)
    first, turn, last = row_tables()
    return pl.pallas_call(
        image_kernel,
        out_shape=jax.ShapeDtypeStruct((2, 64, GRID), F32),
        grid=(4,),
        in_specs=[
            pl.BlockSpec((DEVICES, 16, 128), lambda i: (0, i, 0)),
            pl.BlockSpec((256, 256), lambda i: (0, 0)),
            pl.BlockSpec((3, 256, 128), lambda i: (0, 0, 0)),
            pl.BlockSpec((64, 256), lambda i: (0, 0)),
        ],
        out_specs=pl.BlockSpec((2, 16, GRID), lambda i: (0, i, 0)),
        scratch_shapes=[
            pltpu.VMEM((DEVICES * 16, 128), F32),
            pltpu.VMEM((16 * 64, 128), F32),
            pltpu.VMEM((16 * 64, 128), F32),
        ],
        compiler_params=pltpu.CompilerParams(vmem_limit_bytes=48 * 1024 * 1024),
        name="image_rows",
    )(got, jnp.asarray(first), jnp.asarray(turn), jnp.asarray(last))


def solution(mesh):
    in_specs = (
        P(BOTH, None, None, None),
        P(BOTH, None),
        P(BOTH, None),
        P(BOTH, None),
        P(BOTH, None),
        P(BOTH),
        P(BOTH, None),
        P(),
    )
    out_specs = P(None, BOTH, None)
    return jax.shard_map(shards, mesh=mesh, in_specs=in_specs, out_specs=out_specs, check_vma=False)
```

```python
import functools
import math

import jax
import jax.numpy as jnp
import numpy as np
from jax import lax
from jax.experimental import pallas as pl
from jax.experimental.pallas import tpu as pltpu
from jax.sharding import PartitionSpec as P

KVIS = 256
TAPS = 16
TILE_R = 512
TILE_C = 1024
NB_DEV = 16
BLOCKS = 2048
GRID = 8192
DEVICES = 128
ROWS = 32
HEAD = 16
WINDOW = 152
UNROLL = 4
BOTH = ("au", "vert")
F32 = jnp.float32
BF16 = jnp.bfloat16
I32 = jnp.int32
NT = (((1,), (1,)), ((), ()))
BIT_MUL = 0x077CB531


def bit_table():
    table = np.zeros(32, np.int32)
    for bit in range(32):
        table[((BIT_MUL << bit) & 0xFFFFFFFF) >> 27] = bit
    return table


def hi_lo(values):
    high = values.astype(jnp.bfloat16)
    low = (values - high.astype(np.float64)).astype(jnp.bfloat16)
    return high, low


@functools.lru_cache(None)
def column_tables():
    v0, c1 = np.arange(64), np.arange(64)
    c0 = np.arange(128)
    angle = 2 * np.pi / GRID * ((v0[None, :, None] * (128 * c1[None, None, :] + c0[:, None, None])) % GRID)
    first = np.concatenate([np.cos(angle), np.sin(angle)], axis=1)
    first = np.concatenate(hi_lo(first), axis=2)
    angle = 2 * np.pi / 128 * ((c0[:, None] * c0[None, :]) % 128)
    second = np.concatenate(hi_lo(np.concatenate([np.cos(angle), np.sin(angle)], axis=1)), axis=0)
    angle = 2 * np.pi / GRID * (v0[:, None] * c0[None, :])
    turn = np.concatenate([np.cos(angle), np.sin(angle)], axis=0).astype(np.float32)
    return first, second, turn


@functools.lru_cache(None)
def row_tables():
    scale = 1.0 / math.sqrt(BLOCKS * KVIS)
    u0, s = np.arange(256), np.arange(128)
    angle = 2 * np.pi / 256 * ((u0[:, None] * s[None, :]) % 256)
    first = np.concatenate([np.cos(angle), np.sin(angle)], axis=1).astype(jnp.bfloat16)
    comp, j = np.arange(128) // 64, np.arange(128) % 32
    plane = np.arange(128) // 32 % 2
    angle = 2 * np.pi / GRID * (u0[:, None] * j[None, :])
    turn_cos = (np.cos(angle) * scale).astype(np.float32)
    turn_sin = (np.sin(angle) * np.where(comp == 0, -1.0, 1.0) * scale).astype(np.float32)
    alternate = ((1.0 - 2.0 * (u0 % 2))[:, None] * ((comp == 0) & (j == 0))[None, :]).astype(np.float32)
    u1 = np.arange(32)
    angle = 2 * np.pi / 32 * ((u1[:, None] * j[None, :]) % 32)
    last = np.where(comp == 0, np.cos(angle), -np.sin(angle))
    last = np.concatenate([last * (plane == p) for p in range(2)], axis=0)
    last = np.concatenate(hi_lo(last), axis=1)
    return first, np.stack([turn_cos, turn_sin, alternate]), last


def iota(shape, dim):
    return lax.broadcasted_iota(I32, shape, dim)


def ones_where(mask):
    return jnp.where(mask, 1.0, 0.0).astype(BF16)


def dot(a, b):
    return jnp.dot(a, b, preferred_element_type=F32)


def dot_nt(a, b):
    return lax.dot_general(a, b, NT, preferred_element_type=F32)


def sort_kernel(x_ref, out_ref):
    below = ones_where(iota((128, 128), 1) < iota((128, 128), 0))
    before = ones_where(iota((KVIS, KVIS), 0) < iota((KVIS, KVIS), 1))
    ones = jnp.ones((KVIS, KVIS), BF16)
    value = iota((128, KVIS), 0)
    place = iota((KVIS, KVIS), 0)

    def one_block(i, carry):
        x = x_ref[i]
        row = x.astype(F32)[4:5].astype(I32)
        hit = value == row
        hot = ones_where(hit)
        rank = dot(hot, before) + dot(dot(below, hot).astype(BF16), ones)
        rank = jnp.sum(jnp.where(hit, rank, 0.0), axis=0, keepdims=True)
        moved = dot_nt(x, ones_where(place == rank.astype(I32)))
        both = jnp.concatenate([moved[:, :128], moved[:, 128:]], axis=0)
        out_ref[pl.ds(pl.multiple_of(i * 16, 16), 16), :] = both.astype(BF16)
        return carry

    lax.fori_loop(0, NB_DEV, one_block, 0, unroll=2)


AGR = 272
PARTS = ((0, 48, 48), (96, 48, 48), (192, 48, 32))
ORDERS = (("x", "y", "z"), ("y", "z", "x"), ("z", "x", "y"))


def gather_kernel(x_ref, meta_ref, all_ref, send, recv):
    au, vert = lax.axis_index("au"), lax.axis_index("vert")
    here = {"y": au // 4, "z": au % 4, "x": vert // 2}
    core = vert % 2

    def device(at, core):
        return (at["y"] * 4 + at["z"], at["x"] * 2 + core)

    def moved(dim, step):
        return {**here, dim: (here[dim] + step) % 4}

    sibling = device(here, 1 - core)
    barrier = pltpu.get_barrier_semaphore()
    for other in [device(moved(d, step), core) for d in "xyz" for step in (1, 3)] + [sibling]:
        pl.semaphore_signal(barrier, inc=1, device_id=other, device_id_type=pl.DeviceIdType.MESH)
    all_ref[here["y"], here["z"], here["x"], core, :256, :] = x_ref[...]
    all_ref[here["y"], here["z"], here["x"], core, 256:, :] = meta_ref[...]
    pl.semaphore_wait(barrier, 7)

    def region(part, full, at, rows=None):
        first, one, two = PARTS[part]
        start, size = {None: (first, one + two), 0: (first, one), 1: (first + one, two)}[rows]
        index = [slice(None) if d in full else at[d] for d in "yzx"]
        return all_ref.at[(*index, core, pl.ds(start, size), slice(None))]

    used = [0]
    started = []

    def copy(ref, to):
        n = used[0]
        used[0] += 1
        made = pltpu.make_async_remote_copy(
            src_ref=ref, dst_ref=ref, send_sem=send.at[n], recv_sem=recv.at[n],
            device_id=to, device_id_type=pl.DeviceIdType.MESH,
        )
        made.start()
        started.append(made)
        return made

    shared = []
    for phase in range(3):
        plain, relayed = [], []
        for part, order in enumerate(ORDERS):
            full, dim = order[:phase], order[phase]
            ref = region(part, full, here)
            right = copy(ref, device(moved(dim, 1), core))
            left = copy(ref, device(moved(dim, 3), core))
            plain.append((right, left))
        if phase == 2:
            for part, order in enumerate(ORDERS):
                shared.append(copy(region(part, order[:2], here), sibling))
        for part, order in enumerate(ORDERS):
            full, dim = order[:phase], order[phase]
            right, left = plain[part]
            right.wait_recv()
            one = copy(region(part, full, moved(dim, 3), 0), device(moved(dim, 1), core))
            if phase == 2:
                shared.append(copy(region(part, full, moved(dim, 3)), sibling))
            left.wait_recv()
            two = copy(region(part, full, moved(dim, 1), 1), device(moved(dim, 3), core))
            if phase == 2:
                shared.append(copy(region(part, full, moved(dim, 1)), sibling))
            relayed.append((one, two))
        for part, order in enumerate(ORDERS):
            full, dim = order[:phase], order[phase]
            for half, made in enumerate(relayed[part]):
                made.wait_recv()
                if phase == 2:
                    shared.append(copy(region(part, full, moved(dim, 2), half), sibling))
    for made in shared:
        made.wait_recv()
    for made in started:
        made.wait_send()


COPIES = 3 * (4 * 3 + 5)


def gathered(ordered, meta):
    vmem = pl.BlockSpec(memory_space=pltpu.VMEM)
    return pl.pallas_call(
        gather_kernel,
        out_shape=jax.ShapeDtypeStruct((4, 4, 4, 2, AGR, 128), BF16),
        in_specs=[vmem, vmem],
        out_specs=vmem,
        scratch_shapes=[pltpu.SemaphoreType.DMA((COPIES,)), pltpu.SemaphoreType.DMA((COPIES,))],
        compiler_params=pltpu.CompilerParams(
            collective_id=0, has_side_effects=True, vmem_limit_bytes=32 * 1024 * 1024
        ),
        name="gather_blocks",
    )(ordered, meta)


def pick(halves, index, low):
    first, second = [jnp.take_along_axis(half, index, axis=0, mode="promise_in_bounds") for half in halves]
    return jnp.where(low, first, second)


def placed(sources, tap, limit):
    halves = [(source[:8], source[8:]) for source in sources]
    parts = [[] for _ in sources]
    for i in range(tap.shape[0] // 8):
        t = tap[8 * i : 8 * i + 8]
        inside = (t >= 0) & (t < limit)
        low = t < 8
        index = t & 7
        for out, pair in zip(parts, halves):
            out.append(jnp.where(inside, pick(pair, index, low), 0.0))
    return [jnp.concatenate(part, axis=0) for part in parts]


def grid_kernel(
    words, meta, bits, strip, x_ref, taps_ref, first_ref, second_ref, turn_ref,
    out_ref, acc, mid, stage, acc4, extra, items,
):
    s = strip[0]
    acc[...] = jnp.zeros_like(acc)
    acc4[...] = jnp.zeros_like(acc4)
    table = taps_ref[...]
    table_hi = table.astype(BF16)
    table_lo = (table - table_hi.astype(F32)).astype(BF16)
    both_tables = jnp.concatenate([table_hi, table_lo], axis=0)

    def listed(kind, count):
        def group(g, n):
            def step(state):
                word, n = state
                low = word & -word
                bit = bits[lax.shift_right_logical(low * BIT_MUL, 27)]
                items[n] = (kind << 12) | ((g * NB_DEV + (bit & 15)) << 1) | (bit >> 4)
                return word ^ low, n + 1

            return lax.while_loop(lambda state: state[0] != 0, step, (words[kind * 128 + g], n))[1]

        return lax.fori_loop(0, 128, group, count)

    def loaded(code):
        half, block = code & 1, (code >> 1) & (BLOCKS - 1)
        where = meta[block]
        cell = (where >> 14) & 31
        anchor_row = (where >> 19) * TILE_R + (cell >> 3) * 128
        anchor_col = ((block >> 4) & 7) * TILE_C + (cell & 7) * 128
        x = x_ref[block >> 4, pl.ds(pl.multiple_of((block & 15) * 16, 16), 16), :].astype(F32)
        x = jnp.where(half == 1, x[8:], x[:8])
        row, col, wplane = [x[i : i + 1].astype(I32) for i in (4, 5, 6)]
        chosen = ones_where(iota((32, 128), 0) == wplane)
        taps = dot(both_tables, chosen)
        tap_re, tap_im = taps[:16], taps[16:32]
        full_re, full_im = tap_re + taps[32:48], tap_im + taps[48:64]
        weights_re, weights_im = [], []
        for p in range(2):
            re, im = x[2 * p : 2 * p + 1], x[2 * p + 1 : 2 * p + 2]
            weights_re.append((re * full_re - im * full_im).astype(BF16).astype(F32))
            weights_im.append((re * full_im + im * full_re).astype(BF16).astype(F32))
        limit = jnp.minimum(jnp.where(anchor_col == GRID - 128, 128, 1000) - col, TAPS)
        return anchor_row, anchor_col, row, col, (tap_re, tap_im), weights_re + weights_im, limit

    def item(code, valid):
        anchor_row, anchor_col, row, col, taps, weights, limit = loaded(code)
        mirror = (code >> 12) == 1
        sign = jnp.where(mirror, -1, 1)
        base = jnp.where(mirror, GRID - s * ROWS, s * ROWS) - anchor_row
        base = jnp.where(valid, base, -100000)
        least = jnp.where(mirror & (s == 0), 1, 0)
        j = iota((ROWS, 128), 0)
        tap = jnp.where(j < least, -1, base + sign * j - row)
        re0, re1, im0, im1 = placed(weights, tap, TAPS)
        flip = jnp.where(mirror, -1.0, 1.0)
        left = jnp.concatenate([re0, re1, im0 * flip, im1 * flip], axis=0).astype(BF16)
        right = jnp.concatenate([-im0, -im1, re0 * flip, re1 * flip], axis=0).astype(BF16)
        tap = jnp.where(mirror, 144, 0) + sign * iota((WINDOW, 128), 0) - col
        col_re, col_im = placed(taps, tap, limit)
        cols = jnp.concatenate([col_re.astype(BF16), col_im.astype(BF16)], axis=1)
        patch = dot_nt(cols, jnp.concatenate([left, right], axis=1))
        start = jnp.where(mirror, GRID - 128 - anchor_col, anchor_col + HEAD)
        return pl.multiple_of(start, 16), patch

    count = listed(1, listed(0, 0))

    def several(i, carry):
        found = []
        for k in range(UNROLL):
            n = i * UNROLL + k
            valid = n < count
            found.append(item(jnp.where(valid, items[n], 0), valid))
        for start, patch in found:
            acc[pl.ds(start, WINDOW), :] += patch
        return carry

    lax.fori_loop(0, (count + UNROLL - 1) // UNROLL, several, 0)
    acc[HEAD : HEAD + 8, :] += jnp.where(iota((8, 128), 0) == 0, acc[HEAD + GRID : HEAD + GRID + 8, :], 0.0)

    count4 = listed(2, 0)

    def single(i, carry):
        anchor_row, anchor_col, row, col, taps, weights, limit = loaded(items[i])
        tap = jnp.broadcast_to(GRID // 2 - anchor_row - row, (8, 128))
        re0, re1, im0, im1 = placed(weights, tap, TAPS)
        q = iota((8, 128), 0)
        left = jnp.where(q == 0, re0, jnp.where(q == 1, re1, jnp.where(q == 2, im0, jnp.where(q == 3, im1, 0.0))))
        right = jnp.where(q == 0, -im0, jnp.where(q == 1, -im1, jnp.where(q == 2, re0, jnp.where(q == 3, re1, 0.0))))
        rows = jnp.concatenate([left, right], axis=1).astype(BF16)
        tap = iota((WINDOW, 128), 0) - col
        col_re, col_im = placed(taps, tap, limit)
        cols = jnp.concatenate([col_re, col_im], axis=1)
        tail = jnp.concatenate([cols[128:], jnp.zeros((256 - WINDOW, 256), F32)], axis=0)
        c1 = anchor_col >> 7
        acc4[pl.ds(pl.multiple_of(c1 * 8, 8), 8), :] += dot_nt(rows, cols[:128].astype(BF16))
        acc4[pl.ds(pl.multiple_of(c1 * 8 + 8, 8), 8), :] += dot_nt(rows, tail.astype(BF16))
        return carry

    lax.fori_loop(0, count4, single, 0)

    lane = iota((1, 128), 1)
    flip = jnp.where(lane < 64, -1.0, 1.0)

    @pl.when(s != 0)
    def _():
        extra[...] = jnp.zeros_like(extra)

    @pl.when(s == 0)
    def _():
        cosine = first_ref[0, :64, :64]
        sine = first_ref[0, 64:, :64]
        turn_cos, turn_sin = turn_ref[:64], turn_ref[64:]
        for p in range(2):
            re = acc4[pl.ds(p, 64, stride=8), :].astype(BF16)
            im = acc4[pl.ds(2 + p, 64, stride=8), :].astype(BF16)
            mid_re = dot(cosine, re) - dot(sine, im)
            mid_im = dot(cosine, im) + dot(sine, re)
            turned_re = (mid_re * turn_cos - mid_im * turn_sin).astype(BF16)
            turned_im = (mid_re * turn_sin + mid_im * turn_cos).astype(BF16)
            got = dot_nt(second_ref[:128, :128], turned_re) - dot_nt(second_ref[:128, 128:], turned_im)
            extra[p] = got.astype(BF16)

    def column_first(c0, carry):
        h = acc[pl.ds(HEAD + c0, 64, stride=128), :]
        high = h.astype(BF16)
        low = (h - high.astype(F32)).astype(BF16)
        factors = first_ref[c0]
        got = dot(
            jnp.concatenate([factors, factors], axis=1), jnp.concatenate([high, high, low, low], axis=0)
        )
        y = got[:64] + flip * pltpu.roll(got[64:], 64, 1)
        mid[pl.ds(pl.multiple_of(c0 * 64, 64), 64), :] = y
        return carry

    lax.fori_loop(0, 128, column_first, 0, unroll=4)

    special = (s == 0) & ((lane == 64) | (lane == 96))
    keep = jnp.where(special, 0.0, 1.0)
    second_hi = second_ref[:128]
    second_lo = second_ref[128:]
    spot = iota((64, 128), 0)
    spot_lane = iota((64, 128), 1)

    for group in range(4):

        def column_second(v, carry):
            v0 = group * 16 + v
            y = mid[pl.ds(v0, 128, stride=64), :]
            turned = flip * pltpu.roll(y, 64, 1)
            pair = jnp.concatenate([y.astype(BF16), turned.astype(BF16)], axis=0)
            z = dot(second_hi, pair) + dot(second_lo, pair)
            more = dot(extra[0], ones_where((spot == v0) & (spot_lane == 64)))
            more = more + dot(extra[1], ones_where((spot == v0) & (spot_lane == 96)))
            stage[pl.ds(v, 128, stride=16), :] = z * keep + more
            return carry

        lax.fori_loop(0, 16, column_second, 0, unroll=2)

        def pack(d, carry):
            out_ref[d, group * 16 : group * 16 + 16, :] = stage[
                pl.ds(pl.multiple_of(d * 16, 16), 16), :
            ].astype(BF16)
            return carry

        lax.fori_loop(0, 128, pack, 0, unroll=8)


def image_kernel(in_ref, first_ref, turn_ref, last_ref, out_ref, wide, left, right):
    def widen(s, carry):
        wide[pl.ds(pl.multiple_of(s * 16, 16), 16), :] = in_ref[s].astype(F32)
        return carry

    lax.fori_loop(0, DEVICES, widen, 0, unroll=8)
    flip = jnp.where(iota((1, 128), 1) < 64, -1.0, 1.0)
    first = first_ref[...]
    last = last_ref[...]

    def one(v, carry):
        y = wide[pl.ds(v, DEVICES, stride=16), :]
        rolled = pltpu.roll(y, 64, 1)
        pair = jnp.concatenate([y.astype(BF16), (flip * rolled).astype(BF16)], axis=0)
        got = dot(first, pair) + turn_ref[2] * rolled[:1]
        turned = (got * turn_ref[0] + pltpu.roll(got, 64, 1) * turn_ref[1]).astype(BF16)
        result = dot_nt(last, jnp.concatenate([turned, turned], axis=1))
        left[pl.ds(pl.multiple_of(v * 64, 64), 64), :] = result[:, :128]
        right[pl.ds(pl.multiple_of(v * 64, 64), 64), :] = result[:, 128:]
        return carry

    lax.fori_loop(0, 16, one, 0, unroll=2)

    def place(u1, carry):
        for p in range(2):
            for half in range(2):
                for side, ref in ((0, left), (1, right)):
                    out_ref[p, half * 8 : half * 8 + 8, pl.ds(pl.multiple_of(u1 * 256 + side * 128, 128), 128)] = (
                        ref[pl.ds(half * 512 + p * 32 + u1, 8, stride=64), :]
                    )
        return carry

    lax.fori_loop(0, 32, place, 0, unroll=2)


def words_of(code, s):
    row = (code >> 19) * TILE_R + ((code >> 17) & 3) * 128
    top, bottom = (code >> 7) & 127, code & 127
    shift = jnp.arange(NB_DEV, dtype=I32)[None, :]

    def packed(first, final):
        hit = (final >= 0) & (first < 128 + TAPS - 1)
        one = (hit & (top >= first - (TAPS - 1))).astype(I32)
        two = (hit & (bottom <= final)).astype(I32)
        both = one.reshape(128, NB_DEV) << shift | two.reshape(128, NB_DEV) << (shift + 16)
        return jnp.sum(both, axis=1)

    direct = s * ROWS - row
    mirror = GRID - ROWS + 1 - s * ROWS - row
    middle = GRID // 2 - row
    middle = packed(middle, middle) * (s == 0).astype(I32)
    return jnp.concatenate([packed(direct, direct + ROWS - 1), packed(mirror, mirror + ROWS - 1), middle])


def shards(visibilities, keep_flags, kernel_index, row_offset, col_offset, cell_index, tile_row, kernel_taps):
    s = lax.axis_index("au") * 8 + lax.axis_index("vert")
    masked = jnp.where(keep_flags[:, None, :] == 1, visibilities.reshape(NB_DEV, 4, KVIS), 0).astype(BF16)
    codes = jnp.stack([row_offset, col_offset, kernel_index, jnp.zeros_like(row_offset)], axis=1)
    x8 = jnp.concatenate([masked, codes.astype(BF16)], axis=1)
    vmem = pl.BlockSpec(memory_space=pltpu.VMEM)
    smem = pl.BlockSpec(memory_space=pltpu.SMEM)
    ordered = pl.pallas_call(
        sort_kernel,
        out_shape=jax.ShapeDtypeStruct((NB_DEV * 16, 128), BF16),
        in_specs=[vmem],
        out_specs=vmem,
        name="sort_blocks",
    )(x8)
    by_block = ordered.reshape(NB_DEV, 16, 128)
    top = by_block[:, 4, 127].astype(I32)
    bottom = by_block[:, 12, 0].astype(I32)
    meta = jnp.stack([tile_row[:, 0].astype(BF16), cell_index.astype(BF16), by_block[:, 4, 127], by_block[:, 12, 0]])
    x_all = gathered(ordered, jnp.pad(meta, ((0, 12), (0, 128 - NB_DEV)))).reshape(DEVICES, AGR, 128)
    found = x_all[:, 256:260, :NB_DEV].astype(I32)
    codes_all = ((found[:, 0] * 32 + found[:, 1]) << 14) | (found[:, 2] << 7) | found[:, 3]
    codes_all = codes_all.reshape(BLOCKS)
    words = words_of(codes_all, s)
    first, second, turn = column_tables()
    taps = kernel_taps.transpose(1, 2, 0).reshape(2 * TAPS, 32)
    sent = pl.pallas_call(
        grid_kernel,
        out_shape=jax.ShapeDtypeStruct((DEVICES, 64, 128), BF16),
        in_specs=[smem] * 4 + [vmem] * 5,
        out_specs=vmem,
        scratch_shapes=[
            pltpu.VMEM((HEAD + GRID + 32, 128), F32),
            pltpu.VMEM((128 * 64, 128), F32),
            pltpu.VMEM((DEVICES * 16, 128), F32),
            pltpu.VMEM((66 * 8, 128), F32),
            pltpu.VMEM((2, 128, 64), BF16),
            pltpu.SMEM((4096,), I32),
        ],
        compiler_params=pltpu.CompilerParams(vmem_limit_bytes=56 * 1024 * 1024),
        name="grid_columns",
    )(
        words, codes_all, jnp.asarray(bit_table()), s.reshape(1).astype(I32),
        x_all, taps, jnp.asarray(first), jnp.asarray(second), jnp.asarray(turn),
    )
    got = lax.all_to_all(sent, BOTH, split_axis=0, concat_axis=0, tiled=True)
    first, turn, last = row_tables()
    return pl.pallas_call(
        image_kernel,
        out_shape=jax.ShapeDtypeStruct((2, 64, GRID), F32),
        grid=(4,),
        in_specs=[
            pl.BlockSpec((DEVICES, 16, 128), lambda i: (0, i, 0)),
            pl.BlockSpec((256, 256), lambda i: (0, 0)),
            pl.BlockSpec((3, 256, 128), lambda i: (0, 0, 0)),
            pl.BlockSpec((64, 256), lambda i: (0, 0)),
        ],
        out_specs=pl.BlockSpec((2, 16, GRID), lambda i: (0, i, 0)),
        scratch_shapes=[
            pltpu.VMEM((DEVICES * 16, 128), F32),
            pltpu.VMEM((16 * 64, 128), F32),
            pltpu.VMEM((16 * 64, 128), F32),
        ],
        compiler_params=pltpu.CompilerParams(vmem_limit_bytes=48 * 1024 * 1024),
        name="image_rows",
    )(got, jnp.asarray(first), jnp.asarray(turn), jnp.asarray(last))


def solution(mesh):
    in_specs = (
        P(BOTH, None, None, None),
        P(BOTH, None),
        P(BOTH, None),
        P(BOTH, None),
        P(BOTH, None),
        P(BOTH),
        P(BOTH, None),
        P(),
    )
    out_specs = P(None, BOTH, None)
    return jax.shard_map(shards, mesh=mesh, in_specs=in_specs, out_specs=out_specs, check_vma=False)
```

```python
import functools
import math

import jax
import jax.numpy as jnp
import numpy as np
from jax import lax
from jax.experimental import pallas as pl
from jax.experimental.pallas import tpu as pltpu
from jax.sharding import PartitionSpec as P

KVIS = 256
TAPS = 16
TILE_R = 512
TILE_C = 1024
NB_DEV = 16
BLOCKS = 2048
GRID = 8192
DEVICES = 128
ROWS = 32
HEAD = 16
WINDOW = 152
UNROLL = 8
BATCH = 32
BOTH = ("au", "vert")
F32 = jnp.float32
BF16 = jnp.bfloat16
I32 = jnp.int32
NT = (((1,), (1,)), ((), ()))
BIT_MUL = 0x077CB531


def bit_table():
    table = np.zeros(32, np.int32)
    for bit in range(32):
        table[((BIT_MUL << bit) & 0xFFFFFFFF) >> 27] = bit
    return table


def hi_lo(values):
    high = values.astype(jnp.bfloat16)
    low = (values - high.astype(np.float64)).astype(jnp.bfloat16)
    return high, low


@functools.lru_cache(None)
def column_tables():
    v0, c1 = np.arange(64), np.arange(64)
    c0 = np.arange(128)
    angle = 2 * np.pi / GRID * ((v0[None, :, None] * (128 * c1[None, None, :] + c0[:, None, None])) % GRID)
    first = np.concatenate([np.cos(angle), np.sin(angle)], axis=1)
    first = np.concatenate(hi_lo(first), axis=2)
    angle = 2 * np.pi / 128 * ((c0[:, None] * c0[None, :]) % 128)
    second = np.concatenate(hi_lo(np.concatenate([np.cos(angle), np.sin(angle)], axis=1)), axis=0)
    angle = 2 * np.pi / GRID * (v0[:, None] * c0[None, :])
    turn = np.concatenate([np.cos(angle), np.sin(angle)], axis=0).astype(np.float32)
    return first, second, turn


@functools.lru_cache(None)
def row_tables():
    scale = 1.0 / math.sqrt(BLOCKS * KVIS)
    u0, s = np.arange(256), np.arange(128)
    angle = 2 * np.pi / 256 * ((u0[:, None] * s[None, :]) % 256)
    first = np.concatenate([np.cos(angle), np.sin(angle)], axis=1).astype(jnp.bfloat16)
    comp, j = np.arange(128) // 64, np.arange(128) % 32
    plane = np.arange(128) // 32 % 2
    angle = 2 * np.pi / GRID * (u0[:, None] * j[None, :])
    turn_cos = (np.cos(angle) * scale).astype(np.float32)
    turn_sin = (np.sin(angle) * np.where(comp == 0, -1.0, 1.0) * scale).astype(np.float32)
    alternate = ((1.0 - 2.0 * (u0 % 2))[:, None] * ((comp == 0) & (j == 0))[None, :]).astype(np.float32)
    u1 = np.arange(32)
    angle = 2 * np.pi / 32 * ((u1[:, None] * j[None, :]) % 32)
    last = np.where(comp == 0, np.cos(angle), -np.sin(angle))
    last = np.concatenate([last * (plane == p) for p in range(2)], axis=0)
    last = np.concatenate(hi_lo(last), axis=1)
    return first, np.stack([turn_cos, turn_sin, alternate]), last


def iota(shape, dim):
    return lax.broadcasted_iota(I32, shape, dim)


def ones_where(mask):
    return jnp.where(mask, 1.0, 0.0).astype(BF16)


def dot(a, b):
    return jnp.dot(a, b, preferred_element_type=F32)


def dot_nt(a, b):
    return lax.dot_general(a, b, NT, preferred_element_type=F32)


def sort_kernel(vis_ref, keep_ref, plane_ref, row_ref, col_ref, cell_ref, tile_ref, out_ref, meta):
    below = ones_where(iota((128, 128), 1) < iota((128, 128), 0))
    before = ones_where(iota((KVIS, KVIS), 0) < iota((KVIS, KVIS), 1))
    ones = jnp.ones((KVIS, KVIS), BF16)
    value = iota((128, KVIS), 0)
    place = iota((KVIS, KVIS), 0)
    slot = iota((8, KVIS), 0)
    lane = iota((1, 128), 1)

    def one_block(i, carry):
        at = pl.ds(i, 1)
        row = row_ref[at, :]
        keep = keep_ref[at, :] == 1
        x = jnp.where(slot == 4, row, jnp.where(slot == 5, col_ref[at, :], jnp.where(slot == 6, plane_ref[at, :], 0)))
        x = x.astype(F32)
        for p in range(2):
            pair = vis_ref[i, p].astype(F32)
            for c in range(2):
                x = jnp.where((slot == 2 * p + c) & keep, pair[c : c + 1], x)
        x = x.astype(BF16)
        hit = value == row
        hot = ones_where(hit)
        rank = dot(hot, before) + dot(dot(below, hot).astype(BF16), ones)
        rank = jnp.sum(jnp.where(hit, rank, 0.0), axis=0, keepdims=True)
        moved = dot_nt(x, ones_where(place == rank.astype(I32)))
        both = jnp.concatenate([moved[:, :128], moved[:, 128:]], axis=0)
        out_ref[pl.ds(pl.multiple_of(i * 16, 16), 16), :] = both.astype(BF16)
        note = jnp.where(lane == 0, tile_ref[i], jnp.where(lane == 1, cell_ref[i], 0)).astype(F32)
        note = jnp.where(lane == 2, moved[4:5, 127:128], jnp.where(lane == 3, moved[4:5, 128:129], note))
        meta[at, :] = note
        return carry

    lax.fori_loop(0, NB_DEV, one_block, 0, unroll=4)
    out_ref[256:, :] = meta[...].astype(BF16)


AGR = 272
PARTS = ((0, 48, 48), (96, 48, 48), (192, 48, 32))
ORDERS = (("x", "y", "z"), ("y", "z", "x"), ("z", "x", "y"))


def gather_kernel(x_ref, all_ref, send, recv, local):
    au, vert = lax.axis_index("au"), lax.axis_index("vert")
    here = {"y": au // 4, "z": au % 4, "x": vert // 2}
    core = vert % 2

    def device(at, core):
        return (at["y"] * 4 + at["z"], at["x"] * 2 + core)

    def moved(dim, step):
        return {**here, dim: (here[dim] + step) % 4}

    sibling = device(here, 1 - core)
    barrier = pltpu.get_barrier_semaphore()
    for other in [device(moved(d, step), core) for d in "xyz" for step in (1, 2, 3)] + [sibling]:
        pl.semaphore_signal(barrier, inc=1, device_id=other, device_id_type=pl.DeviceIdType.MESH)
    own = pltpu.make_async_copy(x_ref, all_ref.at[here["y"], here["z"], here["x"], core], local)
    own.start()
    own.wait()
    pl.semaphore_wait(barrier, 10)

    def region(part, full, at, rows=None):
        first, one, two = PARTS[part]
        start, size = {None: (first, one + two), 0: (first, one), 1: (first + one, two)}[rows]
        index = [slice(None) if d in full else at[d] for d in "yzx"]
        return all_ref.at[(*index, core, pl.ds(start, size), slice(None))]

    used = [0]
    started = []

    def copy(ref, to):
        n = used[0]
        used[0] += 1
        made = pltpu.make_async_remote_copy(
            src_ref=ref, dst_ref=ref, send_sem=send.at[n], recv_sem=recv.at[n],
            device_id=to, device_id_type=pl.DeviceIdType.MESH,
        )
        made.start()
        started.append(made)
        return made

    shared = []
    for phase in range(2):
        direct = []
        for part, order in enumerate(ORDERS):
            ref = region(part, order[:phase], here)
            direct += [copy(ref, device(moved(order[phase], step), core)) for step in (2, 1, 3)]
        for made in direct:
            made.wait_recv()
    for phase in (2,):
        plain, relayed = [], []
        for part, order in enumerate(ORDERS):
            full, dim = order[:phase], order[phase]
            ref = region(part, full, here)
            right = copy(ref, device(moved(dim, 1), core))
            left = copy(ref, device(moved(dim, 3), core))
            plain.append((right, left))
        if phase == 2:
            for part, order in enumerate(ORDERS):
                shared.append(copy(region(part, order[:2], here), sibling))
        for part, order in enumerate(ORDERS):
            full, dim = order[:phase], order[phase]
            right, left = plain[part]
            right.wait_recv()
            one = copy(region(part, full, moved(dim, 3), 0), device(moved(dim, 1), core))
            if phase == 2:
                shared.append(copy(region(part, full, moved(dim, 3)), sibling))
            left.wait_recv()
            two = copy(region(part, full, moved(dim, 1), 1), device(moved(dim, 3), core))
            if phase == 2:
                shared.append(copy(region(part, full, moved(dim, 1)), sibling))
            relayed.append((one, two))
        for part, order in enumerate(ORDERS):
            full, dim = order[:phase], order[phase]
            for half, made in enumerate(relayed[part]):
                made.wait_recv()
                if phase == 2:
                    shared.append(copy(region(part, full, moved(dim, 2), half), sibling))
    for made in shared:
        made.wait_recv()
    for made in started:
        made.wait_send()


COPIES = 3 * (3 + 3 + 4 + 5)


def gathered(ordered):
    anywhere = pl.BlockSpec(memory_space=pl.ANY)
    return pl.pallas_call(
        gather_kernel,
        out_shape=jax.ShapeDtypeStruct((4, 4, 4, 2, AGR, 128), BF16),
        in_specs=[anywhere],
        out_specs=anywhere,
        scratch_shapes=[
            pltpu.SemaphoreType.DMA((COPIES,)), pltpu.SemaphoreType.DMA((COPIES,)), pltpu.SemaphoreType.DMA
        ],
        compiler_params=pltpu.CompilerParams(collective_id=0, has_side_effects=True),
        name="gather_blocks",
    )(ordered)


def pick(halves, index, low):
    first, second = [jnp.take_along_axis(half, index, axis=0, mode="promise_in_bounds") for half in halves]
    return jnp.where(low, first, second)


def placed(sources, tap, limit):
    halves = [(source[:8], source[8:]) for source in sources]
    parts = [[] for _ in sources]
    for i in range(tap.shape[0] // 8):
        t = tap[8 * i : 8 * i + 8]
        inside = (t >= 0) & (t < limit)
        low = t < 8
        index = t & 7
        for out, pair in zip(parts, halves):
            out.append(jnp.where(inside, pick(pair, index, low), 0.0))
    return [jnp.concatenate(part, axis=0) for part in parts]


def grid_kernel(
    words, meta, bits, strip, x_all, first_all, taps_ref, second_ref, turn_ref,
    out_ref, acc, mid, stage, acc4, extra, x_ref, first_ref, spread, items, sems,
):
    s = strip[0]
    fetch_x = pltpu.make_async_copy(x_all, x_ref, sems.at[0])
    fetch_x.start()
    fetch_first = pltpu.make_async_copy(first_all, first_ref, sems.at[1])
    fetch_first.start()
    acc[...] = jnp.zeros_like(acc)
    acc4[...] = jnp.zeros_like(acc4)
    table = taps_ref[...]
    table_hi = table.astype(BF16)
    table_lo = (table - table_hi.astype(F32)).astype(BF16)
    both_tables = jnp.concatenate([table_hi, table_lo], axis=0)

    def listed(kind, count):
        def group(g, n):
            def step(state):
                word, n = state
                low = word & -word
                bit = bits[lax.shift_right_logical(low * BIT_MUL, 27)]
                items[n] = (kind << 12) | ((g * NB_DEV + (bit & 15)) << 1) | (bit >> 4)
                return word ^ low, n + 1

            return lax.while_loop(lambda state: state[0] != 0, step, (words[kind * 128 + g], n))[1]

        return lax.fori_loop(0, 128, group, count)

    def place_of(code):
        block = (code >> 1) & (BLOCKS - 1)
        where = meta[block]
        cell = (where >> 14) & 31
        anchor_row = (where >> 19) * TILE_R + (cell >> 3) * 128
        return anchor_row, ((block >> 4) & 7) * TILE_C + (cell & 7) * 128

    def codes_of(code):
        half, block = code & 1, (code >> 1) & (BLOCKS - 1)
        x = x_ref[block >> 4, pl.ds(pl.multiple_of((block & 15) * 16, 16), 16), :].astype(F32)
        return jnp.where(half == 1, x[8:], x[:8])

    def factors_of(x):
        chosen = ones_where(iota((32, 128), 0) == x[6:7].astype(I32))
        taps = dot(both_tables, chosen)
        tap_re, tap_im = taps[:16], taps[16:32]
        full_re, full_im = tap_re + taps[32:48], tap_im + taps[48:64]
        weights_re, weights_im = [], []
        for p in range(2):
            re, im = x[2 * p : 2 * p + 1], x[2 * p + 1 : 2 * p + 2]
            weights_re.append((re * full_re - im * full_im).astype(BF16).astype(F32))
            weights_im.append((re * full_im + im * full_re).astype(BF16).astype(F32))
        return weights_re + weights_im + [tap_re, tap_im]

    def offsets(x, anchor_col):
        row, col = x[4:5].astype(I32), x[5:6].astype(I32)
        return row, col, jnp.minimum(jnp.where(anchor_col == GRID - 128, 128, 1000) - col, TAPS)

    def item(code, valid, slot):
        anchor_row, anchor_col = place_of(code)
        row, col, limit = offsets(codes_of(code), anchor_col)
        base_at = pl.multiple_of(slot * 96, 96)
        factors = [spread[pl.ds(base_at + 16 * i, 16), :] for i in range(6)]
        weights, taps = factors[:4], factors[4:]
        mirror = (code >> 12) == 1
        sign = jnp.where(mirror, -1, 1)
        base = jnp.where(mirror, GRID - s * ROWS, s * ROWS) - anchor_row
        base = jnp.where(valid, base, -100000)
        least = jnp.where(mirror & (s == 0), 1, 0)
        j = iota((ROWS, 128), 0)
        tap = jnp.where(j < least, -1, base + sign * j - row)
        re0, re1, im0, im1 = placed(weights, tap, TAPS)
        flip = jnp.where(mirror, -1.0, 1.0)
        left = jnp.concatenate([re0, re1, im0 * flip, im1 * flip], axis=0).astype(BF16)
        right = jnp.concatenate([-im0, -im1, re0 * flip, re1 * flip], axis=0).astype(BF16)
        tap = jnp.where(mirror, 144, 0) + sign * iota((WINDOW, 128), 0) - col
        col_re, col_im = placed(taps, tap, limit)
        cols = jnp.concatenate([col_re.astype(BF16), col_im.astype(BF16)], axis=1)
        patch = dot_nt(cols, jnp.concatenate([left, right], axis=1))
        start = jnp.where(mirror, GRID - 128 - anchor_col, anchor_col + HEAD)
        return pl.multiple_of(start, 16), patch

    count = listed(1, listed(0, 0))
    fetch_x.wait()

    def batch(i, carry):
        first_item = i * BATCH
        rounds = (jnp.minimum(count - first_item, BATCH) + UNROLL - 1) // UNROLL

        def code_at(n):
            valid = n < count
            return jnp.where(valid, items[n], 0), valid

        def prepare(r, carry):
            for k in range(UNROLL):
                slot = r * UNROLL + k
                factors = factors_of(codes_of(code_at(first_item + slot)[0]))
                for f, factor in enumerate(factors):
                    spread[pl.ds(pl.multiple_of(slot * 96 + f * 16, 16), 16), :] = factor
            return carry

        lax.fori_loop(0, rounds, prepare, 0)

        def several(r, carry):
            found = []
            for k in range(UNROLL):
                slot = r * UNROLL + k
                found.append(item(*code_at(first_item + slot), slot))
            for start, patch in found:
                acc[pl.ds(start, WINDOW), :] += patch
            return carry

        lax.fori_loop(0, rounds, several, 0)
        return carry

    lax.fori_loop(0, (count + BATCH - 1) // BATCH, batch, 0)
    acc[HEAD : HEAD + 8, :] += jnp.where(iota((8, 128), 0) == 0, acc[HEAD + GRID : HEAD + GRID + 8, :], 0.0)

    count4 = listed(2, 0)

    def single(i, carry):
        anchor_row, anchor_col = place_of(items[i])
        x = codes_of(items[i])
        row, col, limit = offsets(x, anchor_col)
        factors = factors_of(x)
        weights, taps = factors[:4], factors[4:]
        tap = jnp.broadcast_to(GRID // 2 - anchor_row - row, (8, 128))
        re0, re1, im0, im1 = placed(weights, tap, TAPS)
        q = iota((8, 128), 0)
        left = jnp.where(q == 0, re0, jnp.where(q == 1, re1, jnp.where(q == 2, im0, jnp.where(q == 3, im1, 0.0))))
        right = jnp.where(q == 0, -im0, jnp.where(q == 1, -im1, jnp.where(q == 2, re0, jnp.where(q == 3, re1, 0.0))))
        rows = jnp.concatenate([left, right], axis=1).astype(BF16)
        tap = iota((WINDOW, 128), 0) - col
        col_re, col_im = placed(taps, tap, limit)
        cols = jnp.concatenate([col_re, col_im], axis=1)
        tail = jnp.concatenate([cols[128:], jnp.zeros((256 - WINDOW, 256), F32)], axis=0)
        c1 = anchor_col >> 7
        acc4[pl.ds(pl.multiple_of(c1 * 8, 8), 8), :] += dot_nt(rows, cols[:128].astype(BF16))
        acc4[pl.ds(pl.multiple_of(c1 * 8 + 8, 8), 8), :] += dot_nt(rows, tail.astype(BF16))
        return carry

    lax.fori_loop(0, count4, single, 0)

    lane = iota((1, 128), 1)
    flip = jnp.where(lane < 64, -1.0, 1.0)

    fetch_first.wait()

    @pl.when(s == 0)
    def _():
        cosine = first_ref[0, :64, :64]
        sine = first_ref[0, 64:, :64]
        turn_cos, turn_sin = turn_ref[:64], turn_ref[64:]
        for p in range(2):
            re = acc4[pl.ds(p, 64, stride=8), :].astype(BF16)
            im = acc4[pl.ds(2 + p, 64, stride=8), :].astype(BF16)
            mid_re = dot(cosine, re) - dot(sine, im)
            mid_im = dot(cosine, im) + dot(sine, re)
            turned_re = (mid_re * turn_cos - mid_im * turn_sin).astype(BF16)
            turned_im = (mid_re * turn_sin + mid_im * turn_cos).astype(BF16)
            got = dot_nt(second_ref[:128, :128], turned_re) - dot_nt(second_ref[:128, 128:], turned_im)
            extra[p] = got.astype(BF16)

    def column_first(c0, carry):
        h = acc[pl.ds(HEAD + c0, 64, stride=128), :]
        high = h.astype(BF16)
        low = (h - high.astype(F32)).astype(BF16)
        factors = first_ref[c0]
        got = dot(
            jnp.concatenate([factors, factors], axis=1), jnp.concatenate([high, high, low, low], axis=0)
        )
        y = got[:64] + flip * pltpu.roll(got[64:], 64, 1)
        mid[pl.ds(pl.multiple_of(c0 * 64, 64), 64), :] = y
        return carry

    lax.fori_loop(0, 128, column_first, 0, unroll=16)

    keep = jnp.where((lane == 64) | (lane == 96), 0.0, 1.0)
    second_hi = second_ref[:128]
    second_lo = second_ref[128:]
    spot = iota((64, 128), 0)
    spot_lane = iota((64, 128), 1)

    for group in range(4):

        def column_second(v, carry):
            v0 = group * 16 + v
            y = mid[pl.ds(v0, 128, stride=64), :]
            turned = flip * pltpu.roll(y, 64, 1)
            pair = jnp.concatenate([y.astype(BF16), turned.astype(BF16)], axis=0)
            z = dot(second_hi, pair) + dot(second_lo, pair)
            stage[pl.ds(v, 128, stride=16), :] = z
            return carry

        lax.fori_loop(0, 16, column_second, 0, unroll=8)

        @pl.when(s == 0)
        def _():
            def middle(v, carry):
                v0 = group * 16 + v
                more = dot(extra[0], ones_where((spot == v0) & (spot_lane == 64)))
                more = more + dot(extra[1], ones_where((spot == v0) & (spot_lane == 96)))
                where = pl.ds(v, 128, stride=16)
                stage[where, :] = stage[where, :] * keep + more
                return carry

            lax.fori_loop(0, 16, middle, 0, unroll=4)

        def pack(d, carry):
            out_ref[d, group * 16 : group * 16 + 16, :] = stage[
                pl.ds(pl.multiple_of(d * 16, 16), 16), :
            ].astype(BF16)
            return carry

        lax.fori_loop(0, 128, pack, 0, unroll=8)


def image_kernel(in_ref, first_ref, turn_ref, last_ref, out_ref, wide, left, right):
    def widen(s, carry):
        wide[pl.ds(pl.multiple_of(s * 16, 16), 16), :] = in_ref[s].astype(F32)
        return carry

    lax.fori_loop(0, DEVICES, widen, 0, unroll=8)
    flip = jnp.where(iota((1, 128), 1) < 64, -1.0, 1.0)
    first = first_ref[...]
    last = last_ref[...]

    def one(v, carry):
        y = wide[pl.ds(v, DEVICES, stride=16), :]
        rolled = pltpu.roll(y, 64, 1)
        pair = jnp.concatenate([y.astype(BF16), (flip * rolled).astype(BF16)], axis=0)
        got = dot(first, pair) + turn_ref[2] * rolled[:1]
        turned = (got * turn_ref[0] + pltpu.roll(got, 64, 1) * turn_ref[1]).astype(BF16)
        result = dot_nt(last, jnp.concatenate([turned, turned], axis=1))
        left[pl.ds(pl.multiple_of(v * 64, 64), 64), :] = result[:, :128]
        right[pl.ds(pl.multiple_of(v * 64, 64), 64), :] = result[:, 128:]
        return carry

    lax.fori_loop(0, 16, one, 0, unroll=8)

    def place(u1, carry):
        for p in range(2):
            for half in range(2):
                for side, ref in ((0, left), (1, right)):
                    out_ref[p, half * 8 : half * 8 + 8, pl.ds(pl.multiple_of(u1 * 256 + side * 128, 128), 128)] = (
                        ref[pl.ds(half * 512 + p * 32 + u1, 8, stride=64), :]
                    )
        return carry

    lax.fori_loop(0, 32, place, 0, unroll=4)


def words_of(code, s):
    row = (code >> 19) * TILE_R + ((code >> 17) & 3) * 128
    top, bottom = (code >> 7) & 127, code & 127
    shift = jnp.arange(NB_DEV, dtype=I32)[None, :]

    def packed(first, final):
        hit = (final >= 0) & (first < 128 + TAPS - 1)
        one = (hit & (top >= first - (TAPS - 1))).astype(I32)
        two = (hit & (bottom <= final)).astype(I32)
        both = one.reshape(128, NB_DEV) << shift | two.reshape(128, NB_DEV) << (shift + 16)
        return jnp.sum(both, axis=1)

    direct = s * ROWS - row
    mirror = GRID - ROWS + 1 - s * ROWS - row
    middle = GRID // 2 - row
    middle = packed(middle, middle) * (s == 0).astype(I32)
    return jnp.concatenate([packed(direct, direct + ROWS - 1), packed(mirror, mirror + ROWS - 1), middle])


def gridded(words, codes_all, s, x_all, taps):
    vmem = pl.BlockSpec(memory_space=pltpu.VMEM)
    smem = pl.BlockSpec(memory_space=pltpu.SMEM)
    first, second, turn = column_tables()
    return pl.pallas_call(
        grid_kernel,
        out_shape=jax.ShapeDtypeStruct((DEVICES, 64, 128), BF16),
        in_specs=[smem] * 4 + [pl.BlockSpec(memory_space=pl.ANY)] * 2 + [vmem] * 3,
        out_specs=vmem,
        scratch_shapes=[
            pltpu.VMEM((HEAD + GRID + 32, 128), F32),
            pltpu.VMEM((128 * 64, 128), F32),
            pltpu.VMEM((DEVICES * 16, 128), F32),
            pltpu.VMEM((66 * 8, 128), F32),
            pltpu.VMEM((2, 128, 64), BF16),
            pltpu.VMEM((DEVICES, AGR, 128), BF16),
            pltpu.VMEM((128, 128, 128), BF16),
            pltpu.VMEM((BATCH * 96, 128), F32),
            pltpu.SMEM((4096,), I32),
            pltpu.SemaphoreType.DMA((2,)),
        ],
        compiler_params=pltpu.CompilerParams(vmem_limit_bytes=44 * 1024 * 1024),
        name="grid_columns",
    )(
        words, codes_all, jnp.asarray(bit_table()), s.reshape(1).astype(I32),
        x_all, jnp.asarray(first), taps, jnp.asarray(second), jnp.asarray(turn),
    )


def imaged(got):
    first, turn, last = row_tables()
    return pl.pallas_call(
        image_kernel,
        out_shape=jax.ShapeDtypeStruct((2, 64, GRID), F32),
        grid=(4,),
        in_specs=[
            pl.BlockSpec((DEVICES, 16, 128), lambda i: (0, i, 0)),
            pl.BlockSpec((256, 256), lambda i: (0, 0)),
            pl.BlockSpec((3, 256, 128), lambda i: (0, 0, 0)),
            pl.BlockSpec((64, 256), lambda i: (0, 0)),
        ],
        out_specs=pl.BlockSpec((2, 16, GRID), lambda i: (0, i, 0)),
        scratch_shapes=[
            pltpu.VMEM((DEVICES * 16, 128), F32),
            pltpu.VMEM((16 * 64, 128), F32),
            pltpu.VMEM((16 * 64, 128), F32),
        ],
        compiler_params=pltpu.CompilerParams(vmem_limit_bytes=48 * 1024 * 1024),
        name="image_rows",
    )(got, jnp.asarray(first), jnp.asarray(turn), jnp.asarray(last))


def shards(visibilities, keep_flags, kernel_index, row_offset, col_offset, cell_index, tile_row, kernel_taps):
    s = lax.axis_index("au") * 8 + lax.axis_index("vert")
    vmem = pl.BlockSpec(memory_space=pltpu.VMEM)
    smem = pl.BlockSpec(memory_space=pltpu.SMEM)
    ordered = pl.pallas_call(
        sort_kernel,
        out_shape=jax.ShapeDtypeStruct((AGR, 128), BF16),
        in_specs=[vmem] * 5 + [smem] * 2,
        out_specs=vmem,
        scratch_shapes=[pltpu.VMEM((16, 128), F32)],
        name="sort_blocks",
    )(visibilities, keep_flags, kernel_index, row_offset, col_offset, cell_index, tile_row.reshape(NB_DEV))
    x_all = gathered(ordered).reshape(DEVICES, AGR, 128)
    found = x_all[:, 256:, :4].astype(I32)
    codes_all = ((found[..., 0] * 32 + found[..., 1]) << 14) | (found[..., 2] << 7) | found[..., 3]
    codes_all = codes_all.reshape(BLOCKS)
    words = words_of(codes_all, s)
    taps = kernel_taps.transpose(1, 2, 0).reshape(2 * TAPS, 32)
    sent = gridded(words, codes_all, s, x_all, taps)
    got = lax.all_to_all(sent, BOTH, split_axis=0, concat_axis=0, tiled=True)
    return imaged(got)


def solution(mesh):
    in_specs = (
        P(BOTH, None, None, None),
        P(BOTH, None),
        P(BOTH, None),
        P(BOTH, None),
        P(BOTH, None),
        P(BOTH),
        P(BOTH, None),
        P(),
    )
    out_specs = P(None, BOTH, None)
    return jax.shard_map(shards, mesh=mesh, in_specs=in_specs, out_specs=out_specs, check_vma=False)
```

```python
import functools
import math

import jax
import jax.numpy as jnp
import numpy as np
from jax import lax
from jax.experimental import pallas as pl
from jax.experimental.pallas import tpu as pltpu
from jax.sharding import PartitionSpec as P

KVIS = 256
TAPS = 16
TILE_R = 512
TILE_C = 1024
NB_DEV = 16
BLOCKS = 2048
GRID = 8192
DEVICES = 128
ROWS = 32
HEAD = 16
WINDOW = 152
UNROLL = 8
BATCH = 32
BOTH = ("au", "vert")
F32 = jnp.float32
BF16 = jnp.bfloat16
I32 = jnp.int32
NT = (((1,), (1,)), ((), ()))
BIT_MUL = 0x077CB531


def bit_table():
    table = np.zeros(32, np.int32)
    for bit in range(32):
        table[((BIT_MUL << bit) & 0xFFFFFFFF) >> 27] = bit
    return table


def hi_lo(values):
    high = values.astype(jnp.bfloat16)
    low = (values - high.astype(np.float64)).astype(jnp.bfloat16)
    return high, low


@functools.lru_cache(None)
def column_tables():
    v0, c1 = np.arange(64), np.arange(64)
    c0 = np.arange(128)
    angle = 2 * np.pi / GRID * ((v0[None, :, None] * (128 * c1[None, None, :] + c0[:, None, None])) % GRID)
    first = np.concatenate([np.cos(angle), np.sin(angle)], axis=1)
    first = np.concatenate(hi_lo(first), axis=2)
    angle = 2 * np.pi / 128 * ((c0[:, None] * c0[None, :]) % 128)
    second = np.concatenate(hi_lo(np.concatenate([np.cos(angle), np.sin(angle)], axis=1)), axis=0)
    angle = 2 * np.pi / GRID * (v0[:, None] * c0[None, :])
    turn = np.concatenate([np.cos(angle), np.sin(angle)], axis=0).astype(np.float32)
    return first, second, turn


@functools.lru_cache(None)
def row_tables():
    scale = 1.0 / math.sqrt(BLOCKS * KVIS)
    u0, s = np.arange(256), np.arange(128)
    angle = 2 * np.pi / 256 * ((u0[:, None] * s[None, :]) % 256)
    first = np.concatenate([np.cos(angle), np.sin(angle)], axis=1).astype(jnp.bfloat16)
    comp, j = np.arange(128) // 64, np.arange(128) % 32
    plane = np.arange(128) // 32 % 2
    angle = 2 * np.pi / GRID * (u0[:, None] * j[None, :])
    turn_cos = (np.cos(angle) * scale).astype(np.float32)
    turn_sin = (np.sin(angle) * np.where(comp == 0, -1.0, 1.0) * scale).astype(np.float32)
    alternate = ((1.0 - 2.0 * (u0 % 2))[:, None] * ((comp == 0) & (j == 0))[None, :]).astype(np.float32)
    u1 = np.arange(32)
    angle = 2 * np.pi / 32 * ((u1[:, None] * j[None, :]) % 32)
    last = np.where(comp == 0, np.cos(angle), -np.sin(angle))
    last = np.concatenate([last * (plane == p) for p in range(2)], axis=0)
    last = np.concatenate(hi_lo(last), axis=1)
    return first, np.stack([turn_cos, turn_sin, alternate]), last


def iota(shape, dim):
    return lax.broadcasted_iota(I32, shape, dim)


def ones_where(mask):
    return jnp.where(mask, 1.0, 0.0).astype(BF16)


def dot(a, b):
    return jnp.dot(a, b, preferred_element_type=F32)


def dot_nt(a, b):
    return lax.dot_general(a, b, NT, preferred_element_type=F32)


def sort_kernel(vis_ref, keep_ref, plane_ref, row_ref, col_ref, cell_ref, tile_ref, out_ref, meta):
    below = ones_where(iota((128, 128), 1) < iota((128, 128), 0))
    before = ones_where(iota((KVIS, KVIS), 0) < iota((KVIS, KVIS), 1))
    ones = jnp.ones((KVIS, KVIS), BF16)
    value = iota((128, KVIS), 0)
    place = iota((KVIS, KVIS), 0)
    slot = iota((8, KVIS), 0)
    lane = iota((1, 128), 1)

    meta[...] = jnp.zeros_like(meta)

    def one_block(i, carry):
        at = pl.ds(i, 1)
        row = row_ref[at, :]
        keep = keep_ref[at, :] == 1
        x = jnp.where(slot == 4, row, jnp.where(slot == 5, col_ref[at, :], jnp.where(slot == 6, plane_ref[at, :], 0)))
        x = x.astype(F32)
        for p in range(2):
            pair = vis_ref[i, p].astype(F32)
            for c in range(2):
                x = jnp.where((slot == 2 * p + c) & keep, pair[c : c + 1], x)
        x = x.astype(BF16)
        hit = value == row
        hot = ones_where(hit)
        rank = dot(hot, before) + dot(dot(below, hot).astype(BF16), ones)
        rank = jnp.sum(jnp.where(hit, rank, 0.0), axis=0, keepdims=True)
        moved = dot_nt(x, ones_where(place == rank.astype(I32)))
        both = jnp.concatenate([moved[:, :128], moved[:, 128:]], axis=0)
        out_ref[pl.ds(pl.multiple_of(i * 16, 16), 16), :] = both.astype(BF16)
        note = jnp.where(lane == 0, tile_ref[i], jnp.where(lane == 1, cell_ref[i], 0)).astype(F32)
        note = jnp.where(lane == 2, moved[4:5, 127:128], jnp.where(lane == 3, moved[4:5, 128:129], note))
        meta[at, :] = note
        return carry

    lax.fori_loop(0, NB_DEV, one_block, 0, unroll=4)
    turned = dot_nt(ones_where(iota((16, 128), 0) == iota((16, 128), 1)), meta[...].astype(BF16))
    out_ref[256:, :] = turned.astype(BF16)


AGR = 272
PARTS = ((0, 48, 48), (96, 48, 48), (192, 48, 32))
ORDERS = (("x", "y", "z"), ("y", "z", "x"), ("z", "x", "y"))


def gather_kernel(x_ref, all_ref, send, recv, local):
    au, vert = lax.axis_index("au"), lax.axis_index("vert")
    here = {"y": au // 4, "z": au % 4, "x": vert // 2}
    core = vert % 2

    def device(at, core):
        return (at["y"] * 4 + at["z"], at["x"] * 2 + core)

    def moved(dim, step):
        return {**here, dim: (here[dim] + step) % 4}

    sibling = device(here, 1 - core)
    barrier = pltpu.get_barrier_semaphore()
    for other in [device(moved(d, step), core) for d in "xyz" for step in (1, 2, 3)] + [sibling]:
        pl.semaphore_signal(barrier, inc=1, device_id=other, device_id_type=pl.DeviceIdType.MESH)
    own = pltpu.make_async_copy(x_ref, all_ref.at[here["y"], here["z"], here["x"], core], local)
    own.start()
    own.wait()
    pl.semaphore_wait(barrier, 10)

    def region(part, full, at, rows=None):
        first, one, two = PARTS[part]
        start, size = {None: (first, one + two), 0: (first, one), 1: (first + one, two)}[rows]
        index = [slice(None) if d in full else at[d] for d in "yzx"]
        return all_ref.at[(*index, core, pl.ds(start, size), slice(None))]

    used = [0]
    started = []

    def copy(ref, to):
        n = used[0]
        used[0] += 1
        made = pltpu.make_async_remote_copy(
            src_ref=ref, dst_ref=ref, send_sem=send.at[n], recv_sem=recv.at[n],
            device_id=to, device_id_type=pl.DeviceIdType.MESH,
        )
        made.start()
        started.append(made)
        return made

    shared = []
    for phase in range(2):
        direct = []
        for part, order in enumerate(ORDERS):
            ref = region(part, order[:phase], here)
            direct += [copy(ref, device(moved(order[phase], step), core)) for step in (2, 1, 3)]
        for made in direct:
            made.wait_recv()
    for phase in (2,):
        plain, relayed = [], []
        for part, order in enumerate(ORDERS):
            full, dim = order[:phase], order[phase]
            ref = region(part, full, here)
            right = copy(ref, device(moved(dim, 1), core))
            left = copy(ref, device(moved(dim, 3), core))
            plain.append((right, left))
        if phase == 2:
            for part, order in enumerate(ORDERS):
                shared.append(copy(region(part, order[:2], here), sibling))
        for part, order in enumerate(ORDERS):
            full, dim = order[:phase], order[phase]
            right, left = plain[part]
            right.wait_recv()
            one = copy(region(part, full, moved(dim, 3), 0), device(moved(dim, 1), core))
            if phase == 2:
                shared.append(copy(region(part, full, moved(dim, 3)), sibling))
            left.wait_recv()
            two = copy(region(part, full, moved(dim, 1), 1), device(moved(dim, 3), core))
            if phase == 2:
                shared.append(copy(region(part, full, moved(dim, 1)), sibling))
            relayed.append((one, two))
        for part, order in enumerate(ORDERS):
            full, dim = order[:phase], order[phase]
            for half, made in enumerate(relayed[part]):
                made.wait_recv()
                if phase == 2:
                    shared.append(copy(region(part, full, moved(dim, 2), half), sibling))
    for made in shared:
        made.wait_recv()
    for made in started:
        made.wait_send()


COPIES = 3 * (3 + 3 + 4 + 5)


def gathered(ordered):
    anywhere = pl.BlockSpec(memory_space=pl.ANY)
    return pl.pallas_call(
        gather_kernel,
        out_shape=jax.ShapeDtypeStruct((4, 4, 4, 2, AGR, 128), BF16),
        in_specs=[anywhere],
        out_specs=anywhere,
        scratch_shapes=[
            pltpu.SemaphoreType.DMA((COPIES,)), pltpu.SemaphoreType.DMA((COPIES,)), pltpu.SemaphoreType.DMA
        ],
        compiler_params=pltpu.CompilerParams(collective_id=0, has_side_effects=True),
        name="gather_blocks",
    )(ordered)


def pick(halves, index, low):
    first, second = [jnp.take_along_axis(half, index, axis=0, mode="promise_in_bounds") for half in halves]
    return jnp.where(low, first, second)


def placed(sources, tap, limit):
    halves = [(source[:8], source[8:]) for source in sources]
    parts = [[] for _ in sources]
    for i in range(tap.shape[0] // 8):
        t = tap[8 * i : 8 * i + 8]
        inside = (t >= 0) & (t < limit)
        low = t < 8
        index = t & 7
        for out, pair in zip(parts, halves):
            out.append(jnp.where(inside, pick(pair, index, low), 0.0))
    return [jnp.concatenate(part, axis=0) for part in parts]


def grid_kernel(
    words, meta, bits, strip, x_all, first_all, taps_ref, second_ref, turn_ref,
    out_ref, acc, mid, stage, acc4, extra, x_ref, first_ref, spread, items, sems,
):
    s = strip[0]
    fetch_x = pltpu.make_async_copy(x_all, x_ref, sems.at[0])
    fetch_x.start()
    fetch_first = pltpu.make_async_copy(first_all, first_ref, sems.at[1])
    fetch_first.start()
    acc[...] = jnp.zeros_like(acc)
    acc4[...] = jnp.zeros_like(acc4)
    table = taps_ref[...]
    table_hi = table.astype(BF16)
    table_lo = (table - table_hi.astype(F32)).astype(BF16)
    both_tables = jnp.concatenate([table_hi, table_lo], axis=0)

    def listed(kind, count, groups=128):
        def group(g, n):
            def step(state):
                word, n = state
                low = word & -word
                bit = bits[lax.shift_right_logical(low * BIT_MUL, 27)]
                items[n] = (kind << 12) | ((g * NB_DEV + (bit & 15)) << 1) | (bit >> 4)
                return word ^ low, n + 1

            return lax.while_loop(lambda state: state[0] != 0, step, (words[kind * 128 + g], n))[1]

        return lax.fori_loop(0, groups, group, count)

    def place_of(code):
        block = (code >> 1) & (BLOCKS - 1)
        where = meta[block]
        cell = (where >> 14) & 31
        anchor_row = (where >> 19) * TILE_R + (cell >> 3) * 128
        return anchor_row, ((block >> 4) & 7) * TILE_C + (cell & 7) * 128

    def codes_of(code):
        half, block = code & 1, (code >> 1) & (BLOCKS - 1)
        x = x_ref[block >> 4, pl.ds(pl.multiple_of((block & 15) * 16, 16), 16), :].astype(F32)
        return jnp.where(half == 1, x[8:], x[:8])

    def factors_of(x):
        chosen = ones_where(iota((32, 128), 0) == x[6:7].astype(I32))
        taps = dot(both_tables, chosen)
        tap_re, tap_im = taps[:16], taps[16:32]
        full_re, full_im = tap_re + taps[32:48], tap_im + taps[48:64]
        weights_re, weights_im = [], []
        for p in range(2):
            re, im = x[2 * p : 2 * p + 1], x[2 * p + 1 : 2 * p + 2]
            weights_re.append((re * full_re - im * full_im).astype(BF16).astype(F32))
            weights_im.append((re * full_im + im * full_re).astype(BF16).astype(F32))
        return weights_re + weights_im + [tap_re, tap_im]

    def offsets(x, anchor_col):
        row, col = x[4:5].astype(I32), x[5:6].astype(I32)
        return row, col, jnp.minimum(jnp.where(anchor_col == GRID - 128, 128, 1000) - col, TAPS)

    def item(code, valid, slot):
        anchor_row, anchor_col = place_of(code)
        row, col, limit = offsets(codes_of(code), anchor_col)
        base_at = pl.multiple_of(slot * 96, 96)
        factors = [spread[pl.ds(base_at + 16 * i, 16), :] for i in range(6)]
        weights, taps = factors[:4], factors[4:]
        mirror = (code >> 12) == 1
        sign = jnp.where(mirror, -1, 1)
        base = jnp.where(mirror, GRID - s * ROWS, s * ROWS) - anchor_row
        base = jnp.where(valid, base, -100000)
        least = jnp.where(mirror & (s == 0), 1, 0)
        j = iota((ROWS, 128), 0)
        tap = jnp.where(j < least, -1, base + sign * j - row)
        re0, re1, im0, im1 = placed(weights, tap, TAPS)
        flip = jnp.where(mirror, -1.0, 1.0)
        left = jnp.concatenate([re0, re1, im0 * flip, im1 * flip], axis=0).astype(BF16)
        right = jnp.concatenate([-im0, -im1, re0 * flip, re1 * flip], axis=0).astype(BF16)
        tap = jnp.where(mirror, 144, 0) + sign * iota((WINDOW, 128), 0) - col
        col_re, col_im = placed(taps, tap, limit)
        cols = jnp.concatenate([col_re.astype(BF16), col_im.astype(BF16)], axis=1)
        patch = dot_nt(cols, jnp.concatenate([left, right], axis=1))
        start = jnp.where(mirror, GRID - 128 - anchor_col, anchor_col + HEAD)
        return pl.multiple_of(start, 16), patch

    count = listed(1, listed(0, 0))
    fetch_x.wait()

    def batch(i, carry):
        first_item = i * BATCH
        rounds = (jnp.minimum(count - first_item, BATCH) + UNROLL - 1) // UNROLL

        def code_at(n):
            valid = n < count
            return jnp.where(valid, items[n], 0), valid

        def prepare(r, carry):
            for k in range(UNROLL):
                slot = r * UNROLL + k
                factors = factors_of(codes_of(code_at(first_item + slot)[0]))
                for f, factor in enumerate(factors):
                    spread[pl.ds(pl.multiple_of(slot * 96 + f * 16, 16), 16), :] = factor
            return carry

        lax.fori_loop(0, rounds, prepare, 0)

        def several(r, carry):
            found = []
            for k in range(UNROLL):
                slot = r * UNROLL + k
                found.append(item(*code_at(first_item + slot), slot))
            for start, patch in found:
                acc[pl.ds(start, WINDOW), :] += patch
            return carry

        lax.fori_loop(0, rounds, several, 0)
        return carry

    lax.fori_loop(0, (count + BATCH - 1) // BATCH, batch, 0)
    acc[HEAD : HEAD + 8, :] += jnp.where(iota((8, 128), 0) == 0, acc[HEAD + GRID : HEAD + GRID + 8, :], 0.0)

    count4 = listed(2, 0, jnp.where(s == 0, 128, 0))

    def single(i, carry):
        anchor_row, anchor_col = place_of(items[i])
        x = codes_of(items[i])
        row, col, limit = offsets(x, anchor_col)
        factors = factors_of(x)
        weights, taps = factors[:4], factors[4:]
        tap = jnp.broadcast_to(GRID // 2 - anchor_row - row, (8, 128))
        re0, re1, im0, im1 = placed(weights, tap, TAPS)
        q = iota((8, 128), 0)
        left = jnp.where(q == 0, re0, jnp.where(q == 1, re1, jnp.where(q == 2, im0, jnp.where(q == 3, im1, 0.0))))
        right = jnp.where(q == 0, -im0, jnp.where(q == 1, -im1, jnp.where(q == 2, re0, jnp.where(q == 3, re1, 0.0))))
        rows = jnp.concatenate([left, right], axis=1).astype(BF16)
        tap = iota((WINDOW, 128), 0) - col
        col_re, col_im = placed(taps, tap, limit)
        cols = jnp.concatenate([col_re, col_im], axis=1)
        tail = jnp.concatenate([cols[128:], jnp.zeros((256 - WINDOW, 256), F32)], axis=0)
        c1 = anchor_col >> 7
        acc4[pl.ds(pl.multiple_of(c1 * 8, 8), 8), :] += dot_nt(rows, cols[:128].astype(BF16))
        acc4[pl.ds(pl.multiple_of(c1 * 8 + 8, 8), 8), :] += dot_nt(rows, tail.astype(BF16))
        return carry

    lax.fori_loop(0, count4, single, 0)

    lane = iota((1, 128), 1)
    flip = jnp.where(lane < 64, -1.0, 1.0)

    fetch_first.wait()

    @pl.when(s == 0)
    def _():
        cosine = first_ref[0, :64, :64]
        sine = first_ref[0, 64:, :64]
        turn_cos, turn_sin = turn_ref[:64], turn_ref[64:]
        for p in range(2):
            re = acc4[pl.ds(p, 64, stride=8), :].astype(BF16)
            im = acc4[pl.ds(2 + p, 64, stride=8), :].astype(BF16)
            mid_re = dot(cosine, re) - dot(sine, im)
            mid_im = dot(cosine, im) + dot(sine, re)
            turned_re = (mid_re * turn_cos - mid_im * turn_sin).astype(BF16)
            turned_im = (mid_re * turn_sin + mid_im * turn_cos).astype(BF16)
            got = dot_nt(second_ref[:128, :128], turned_re) - dot_nt(second_ref[:128, 128:], turned_im)
            extra[p] = got.astype(BF16)

    def column_first(c0, carry):
        h = acc[pl.ds(HEAD + c0, 64, stride=128), :]
        high = h.astype(BF16)
        low = (h - high.astype(F32)).astype(BF16)
        factors = first_ref[c0]
        got = dot(
            jnp.concatenate([factors, factors], axis=1), jnp.concatenate([high, high, low, low], axis=0)
        )
        y = got[:64] + flip * pltpu.roll(got[64:], 64, 1)
        mid[pl.ds(pl.multiple_of(c0 * 64, 64), 64), :] = y
        return carry

    lax.fori_loop(0, 128, column_first, 0, unroll=16)

    keep = jnp.where((lane == 64) | (lane == 96), 0.0, 1.0)
    second_hi = second_ref[:128]
    second_lo = second_ref[128:]
    spot = iota((64, 128), 0)
    spot_lane = iota((64, 128), 1)

    for group in range(4):

        def column_second(v, carry):
            v0 = group * 16 + v
            y = mid[pl.ds(v0, 128, stride=64), :]
            turned = flip * pltpu.roll(y, 64, 1)
            pair = jnp.concatenate([y.astype(BF16), turned.astype(BF16)], axis=0)
            z = dot(second_hi, pair) + dot(second_lo, pair)
            stage[pl.ds(v, 128, stride=16), :] = z
            return carry

        lax.fori_loop(0, 16, column_second, 0, unroll=8)

        @pl.when(s == 0)
        def _():
            def middle(v, carry):
                v0 = group * 16 + v
                more = dot(extra[0], ones_where((spot == v0) & (spot_lane == 64)))
                more = more + dot(extra[1], ones_where((spot == v0) & (spot_lane == 96)))
                where = pl.ds(v, 128, stride=16)
                stage[where, :] = stage[where, :] * keep + more
                return carry

            lax.fori_loop(0, 16, middle, 0, unroll=4)

        def pack(d, carry):
            out_ref[d, group * 16 : group * 16 + 16, :] = stage[
                pl.ds(pl.multiple_of(d * 16, 16), 16), :
            ].astype(BF16)
            return carry

        lax.fori_loop(0, 128, pack, 0, unroll=8)


def image_kernel(in_ref, first_ref, turn_ref, last_ref, out_ref, wide, left, right):
    def widen(s, carry):
        wide[pl.ds(pl.multiple_of(s * 16, 16), 16), :] = in_ref[s].astype(F32)
        return carry

    lax.fori_loop(0, DEVICES, widen, 0, unroll=8)
    flip = jnp.where(iota((1, 128), 1) < 64, -1.0, 1.0)
    first = first_ref[...]
    last = last_ref[...]

    def one(v, carry):
        y = wide[pl.ds(v, DEVICES, stride=16), :]
        rolled = pltpu.roll(y, 64, 1)
        pair = jnp.concatenate([y.astype(BF16), (flip * rolled).astype(BF16)], axis=0)
        got = dot(first, pair) + turn_ref[2] * rolled[:1]
        turned = (got * turn_ref[0] + pltpu.roll(got, 64, 1) * turn_ref[1]).astype(BF16)
        result = dot_nt(last, jnp.concatenate([turned, turned], axis=1))
        left[pl.ds(pl.multiple_of(v * 64, 64), 64), :] = result[:, :128]
        right[pl.ds(pl.multiple_of(v * 64, 64), 64), :] = result[:, 128:]
        return carry

    lax.fori_loop(0, 16, one, 0, unroll=8)

    def place(u1, carry):
        for p in range(2):
            for half in range(2):
                for side, ref in ((0, left), (1, right)):
                    out_ref[p, half * 8 : half * 8 + 8, pl.ds(pl.multiple_of(u1 * 256 + side * 128, 128), 128)] = (
                        ref[pl.ds(half * 512 + p * 32 + u1, 8, stride=64), :]
                    )
        return carry

    lax.fori_loop(0, 32, place, 0, unroll=4)


def words_of(code, s):
    row = (code >> 19) * TILE_R + ((code >> 17) & 3) * 128
    top, bottom = (code >> 7) & 127, code & 127
    shift = jnp.arange(NB_DEV, dtype=I32)[None, :]

    def packed(first, final):
        hit = (final >= 0) & (first < 128 + TAPS - 1)
        one = (hit & (top >= first - (TAPS - 1))).astype(I32)
        two = (hit & (bottom <= final)).astype(I32)
        both = one.reshape(128, NB_DEV) << shift | two.reshape(128, NB_DEV) << (shift + 16)
        return jnp.sum(both, axis=1)

    direct = s * ROWS - row
    mirror = GRID - ROWS + 1 - s * ROWS - row
    middle = GRID // 2 - row
    middle = packed(middle, middle) * (s == 0).astype(I32)
    return jnp.concatenate([packed(direct, direct + ROWS - 1), packed(mirror, mirror + ROWS - 1), middle])


def gridded(words, codes_all, s, x_all, taps):
    vmem = pl.BlockSpec(memory_space=pltpu.VMEM)
    smem = pl.BlockSpec(memory_space=pltpu.SMEM)
    first, second, turn = column_tables()
    return pl.pallas_call(
        grid_kernel,
        out_shape=jax.ShapeDtypeStruct((DEVICES, 64, 128), BF16),
        in_specs=[smem] * 4 + [pl.BlockSpec(memory_space=pl.ANY)] * 2 + [vmem] * 3,
        out_specs=vmem,
        scratch_shapes=[
            pltpu.VMEM((HEAD + GRID + 32, 128), F32),
            pltpu.VMEM((128 * 64, 128), F32),
            pltpu.VMEM((DEVICES * 16, 128), F32),
            pltpu.VMEM((66 * 8, 128), F32),
            pltpu.VMEM((2, 128, 64), BF16),
            pltpu.VMEM((DEVICES, AGR, 128), BF16),
            pltpu.VMEM((128, 128, 128), BF16),
            pltpu.VMEM((BATCH * 96, 128), F32),
            pltpu.SMEM((4096,), I32),
            pltpu.SemaphoreType.DMA((2,)),
        ],
        compiler_params=pltpu.CompilerParams(vmem_limit_bytes=44 * 1024 * 1024),
        name="grid_columns",
    )(
        words, codes_all, jnp.asarray(bit_table()), s.reshape(1).astype(I32),
        x_all, jnp.asarray(first), taps, jnp.asarray(second), jnp.asarray(turn),
    )


def imaged(got):
    first, turn, last = row_tables()
    return pl.pallas_call(
        image_kernel,
        out_shape=jax.ShapeDtypeStruct((2, 64, GRID), F32),
        grid=(4,),
        in_specs=[
            pl.BlockSpec((DEVICES, 16, 128), lambda i: (0, i, 0)),
            pl.BlockSpec((256, 256), lambda i: (0, 0)),
            pl.BlockSpec((3, 256, 128), lambda i: (0, 0, 0)),
            pl.BlockSpec((64, 256), lambda i: (0, 0)),
        ],
        out_specs=pl.BlockSpec((2, 16, GRID), lambda i: (0, i, 0)),
        scratch_shapes=[
            pltpu.VMEM((DEVICES * 16, 128), F32),
            pltpu.VMEM((16 * 64, 128), F32),
            pltpu.VMEM((16 * 64, 128), F32),
        ],
        compiler_params=pltpu.CompilerParams(vmem_limit_bytes=48 * 1024 * 1024),
        name="image_rows",
    )(got, jnp.asarray(first), jnp.asarray(turn), jnp.asarray(last))


def shards(visibilities, keep_flags, kernel_index, row_offset, col_offset, cell_index, tile_row, kernel_taps):
    s = lax.axis_index("au") * 8 + lax.axis_index("vert")
    vmem = pl.BlockSpec(memory_space=pltpu.VMEM)
    smem = pl.BlockSpec(memory_space=pltpu.SMEM)
    ordered = pl.pallas_call(
        sort_kernel,
        out_shape=jax.ShapeDtypeStruct((AGR, 128), BF16),
        in_specs=[vmem] * 5 + [smem] * 2,
        out_specs=vmem,
        scratch_shapes=[pltpu.VMEM((128, 128), F32)],
        name="sort_blocks",
    )(visibilities, keep_flags, kernel_index, row_offset, col_offset, cell_index, tile_row.reshape(NB_DEV))
    x_all = gathered(ordered).reshape(DEVICES, AGR, 128)
    found = x_all[:, 256:260, :NB_DEV].astype(I32)
    codes_all = ((found[:, 0] * 32 + found[:, 1]) << 14) | (found[:, 2] << 7) | found[:, 3]
    codes_all = codes_all.reshape(BLOCKS)
    words = words_of(codes_all, s)
    taps = kernel_taps.transpose(1, 2, 0).reshape(2 * TAPS, 32)
    sent = gridded(words, codes_all, s, x_all, taps)
    got = lax.all_to_all(sent, BOTH, split_axis=0, concat_axis=0, tiled=True)
    return imaged(got)


def solution(mesh):
    in_specs = (
        P(BOTH, None, None, None),
        P(BOTH, None),
        P(BOTH, None),
        P(BOTH, None),
        P(BOTH, None),
        P(BOTH),
        P(BOTH, None),
        P(),
    )
    out_specs = P(None, BOTH, None)
    return jax.shard_map(shards, mesh=mesh, in_specs=in_specs, out_specs=out_specs, check_vma=False)
```

```python
import functools
import math

import jax
import jax.numpy as jnp
import numpy as np
from jax import lax
from jax.experimental import pallas as pl
from jax.experimental.pallas import tpu as pltpu
from jax.sharding import PartitionSpec as P

KVIS = 256
TAPS = 16
TILE_R = 512
TILE_C = 1024
NB_DEV = 16
BLOCKS = 2048
GRID = 8192
DEVICES = 128
ROWS = 32
HEAD = 16
WINDOW = 152
UNROLL = 12
BATCH = 48
BOTH = ("au", "vert")
F32 = jnp.float32
BF16 = jnp.bfloat16
I32 = jnp.int32
NT = (((1,), (1,)), ((), ()))
BIT_MUL = 0x077CB531


def bit_table():
    table = np.zeros(32, np.int32)
    for bit in range(32):
        table[((BIT_MUL << bit) & 0xFFFFFFFF) >> 27] = bit
    return table


def hi_lo(values):
    high = values.astype(jnp.bfloat16)
    low = (values - high.astype(np.float64)).astype(jnp.bfloat16)
    return high, low


@functools.lru_cache(None)
def column_tables():
    v0, c1 = np.arange(64), np.arange(64)
    c0 = np.arange(128)
    angle = 2 * np.pi / GRID * ((v0[None, :, None] * (128 * c1[None, None, :] + c0[:, None, None])) % GRID)
    first = np.concatenate([np.cos(angle), np.sin(angle)], axis=1)
    first = np.concatenate(hi_lo(first), axis=2)
    angle = 2 * np.pi / 128 * ((c0[:, None] * c0[None, :]) % 128)
    second = np.concatenate(hi_lo(np.concatenate([np.cos(angle), np.sin(angle)], axis=1)), axis=0)
    angle = 2 * np.pi / GRID * (v0[:, None] * c0[None, :])
    turn = np.concatenate([np.cos(angle), np.sin(angle)], axis=0).astype(np.float32)
    return first, second, turn


@functools.lru_cache(None)
def row_tables():
    scale = 1.0 / math.sqrt(BLOCKS * KVIS)
    u0, s = np.arange(256), np.arange(128)
    angle = 2 * np.pi / 256 * ((u0[:, None] * s[None, :]) % 256)
    first = np.concatenate([np.cos(angle), np.sin(angle)], axis=1).astype(jnp.bfloat16)
    comp, j = np.arange(128) // 64, np.arange(128) % 32
    plane = np.arange(128) // 32 % 2
    angle = 2 * np.pi / GRID * (u0[:, None] * j[None, :])
    turn_cos = (np.cos(angle) * scale).astype(np.float32)
    turn_sin = (np.sin(angle) * np.where(comp == 0, -1.0, 1.0) * scale).astype(np.float32)
    alternate = ((1.0 - 2.0 * (u0 % 2))[:, None] * ((comp == 0) & (j == 0))[None, :]).astype(np.float32)
    u1 = np.arange(32)
    angle = 2 * np.pi / 32 * ((u1[:, None] * j[None, :]) % 32)
    last = np.where(comp == 0, np.cos(angle), -np.sin(angle))
    last = np.concatenate([last * (plane == p) for p in range(2)], axis=0)
    last = np.concatenate(hi_lo(last), axis=1)
    return first, np.stack([turn_cos, turn_sin, alternate]), last


def iota(shape, dim):
    return lax.broadcasted_iota(I32, shape, dim)


def ones_where(mask):
    return jnp.where(mask, 1.0, 0.0).astype(BF16)


def dot(a, b):
    return jnp.dot(a, b, preferred_element_type=F32)


def dot_nt(a, b):
    return lax.dot_general(a, b, NT, preferred_element_type=F32)


def sort_kernel(vis_ref, keep_ref, plane_ref, row_ref, col_ref, cell_ref, tile_ref, out_ref, meta, wide):
    below = ones_where(iota((128, 128), 1) < iota((128, 128), 0))
    before = ones_where(iota((KVIS, KVIS), 0) < iota((KVIS, KVIS), 1))
    ones = jnp.ones((KVIS, KVIS), BF16)
    value = iota((128, KVIS), 0)
    place = iota((KVIS, KVIS), 0)
    slot = iota((8, KVIS), 0)
    lane = iota((1, 128), 1)

    meta[...] = jnp.zeros_like(meta)

    def one_block(i, carry):
        at = pl.ds(i, 1)
        row = row_ref[at, :]
        keep = keep_ref[at, :] == 1
        wplane = plane_ref[at, :]
        first = (128 + row) << (wplane >> 2)
        second = (128 + col_ref[at, :]) << (wplane & 3)
        x = jnp.where(slot == 4, first, jnp.where(slot == 5, second, jnp.where(slot == 6, row, 0)))
        x = x.astype(F32)
        for p in range(2):
            pair = vis_ref[i, p].astype(F32)
            for c in range(2):
                x = jnp.where((slot == 2 * p + c) & keep, pair[c : c + 1], x)
        x = x.astype(BF16)
        hit = value == row
        hot = ones_where(hit)
        rank = dot(hot, before) + dot(dot(below, hot).astype(BF16), ones)
        rank = jnp.sum(jnp.where(hit, rank, 0.0), axis=0, keepdims=True)
        moved = dot_nt(x, ones_where(place == rank.astype(I32)))
        left, right = moved[:, :128], moved[:, 128:]
        wide[pl.ds(pl.multiple_of(i * 8, 8), 8), :] = jnp.where(iota((8, 128), 0) < 4, left, pltpu.roll(right, 4, 0))
        for k, part in enumerate((left[4:5], left[5:6], right[4:5], right[5:6])):
            wide[pl.ds(CODES + i * 4 + k, 1), :] = part
        note = jnp.where(lane == 0, tile_ref[i], jnp.where(lane == 1, cell_ref[i], 0)).astype(F32)
        note = jnp.where(lane == 2, moved[6:7, 127:128], jnp.where(lane == 3, moved[6:7, 128:129], note))
        meta[at, :] = note
        return carry

    lax.fori_loop(0, NB_DEV, one_block, 0, unroll=8)
    turned = dot_nt(ones_where(iota((16, 128), 0) == iota((16, 128), 1)), meta[...].astype(BF16))
    out_ref[:NOTES, :] = wide[...].astype(BF16)
    out_ref[NOTES:, :] = turned.astype(BF16)


AGR = 208
CODES = 128
NOTES = 192
PARTS = ((0, 32, 32), (64, 32, 32), (128, 48, 32))
ORDERS = (("x", "y", "z"), ("y", "z", "x"), ("z", "x", "y"))


def gather_kernel(x_ref, all_ref, send, recv, local):
    au, vert = lax.axis_index("au"), lax.axis_index("vert")
    here = {"y": au // 4, "z": au % 4, "x": vert // 2}
    core = vert % 2

    def device(at, core):
        return (at["y"] * 4 + at["z"], at["x"] * 2 + core)

    def moved(dim, step):
        return {**here, dim: (here[dim] + step) % 4}

    sibling = device(here, 1 - core)
    barrier = pltpu.get_barrier_semaphore()
    for other in [device(moved(d, step), core) for d in "xyz" for step in (1, 2, 3)] + [sibling]:
        pl.semaphore_signal(barrier, inc=1, device_id=other, device_id_type=pl.DeviceIdType.MESH)
    own = pltpu.make_async_copy(x_ref, all_ref.at[here["y"], here["z"], here["x"], core], local)
    own.start()
    own.wait()
    pl.semaphore_wait(barrier, 10)

    def region(part, full, at, rows=None):
        first, one, two = PARTS[part]
        start, size = {None: (first, one + two), 0: (first, one), 1: (first + one, two)}[rows]
        index = [slice(None) if d in full else at[d] for d in "yzx"]
        return all_ref.at[(*index, core, pl.ds(start, size), slice(None))]

    used = [0]
    started = []

    def copy(ref, to):
        n = used[0]
        used[0] += 1
        made = pltpu.make_async_remote_copy(
            src_ref=ref, dst_ref=ref, send_sem=send.at[n], recv_sem=recv.at[n],
            device_id=to, device_id_type=pl.DeviceIdType.MESH,
        )
        made.start()
        started.append(made)
        return made

    shared = []
    for phase in range(2):
        direct = []
        for part, order in enumerate(ORDERS):
            ref = region(part, order[:phase], here)
            direct += [copy(ref, device(moved(order[phase], step), core)) for step in (2, 1, 3)]
        for made in direct:
            made.wait_recv()
    for phase in (2,):
        plain, relayed = [], []
        for part, order in enumerate(ORDERS):
            full, dim = order[:phase], order[phase]
            ref = region(part, full, here)
            right = copy(ref, device(moved(dim, 1), core))
            left = copy(ref, device(moved(dim, 3), core))
            plain.append((right, left))
        if phase == 2:
            for part, order in enumerate(ORDERS):
                shared.append(copy(region(part, order[:2], here), sibling))
        for part, order in enumerate(ORDERS):
            full, dim = order[:phase], order[phase]
            right, left = plain[part]
            right.wait_recv()
            one = copy(region(part, full, moved(dim, 3), 0), device(moved(dim, 1), core))
            if phase == 2:
                shared.append(copy(region(part, full, moved(dim, 3)), sibling))
            left.wait_recv()
            two = copy(region(part, full, moved(dim, 1), 1), device(moved(dim, 3), core))
            if phase == 2:
                shared.append(copy(region(part, full, moved(dim, 1)), sibling))
            relayed.append((one, two))
        for part, order in enumerate(ORDERS):
            full, dim = order[:phase], order[phase]
            for half, made in enumerate(relayed[part]):
                made.wait_recv()
                if phase == 2:
                    shared.append(copy(region(part, full, moved(dim, 2), half), sibling))
    for made in shared:
        made.wait_recv()
    for made in started:
        made.wait_send()


COPIES = 3 * (3 + 3 + 4 + 5)


def gathered(ordered):
    anywhere = pl.BlockSpec(memory_space=pl.ANY)
    return pl.pallas_call(
        gather_kernel,
        out_shape=jax.ShapeDtypeStruct((4, 4, 4, 2, AGR, 128), BF16),
        in_specs=[anywhere],
        out_specs=anywhere,
        scratch_shapes=[
            pltpu.SemaphoreType.DMA((COPIES,)), pltpu.SemaphoreType.DMA((COPIES,)), pltpu.SemaphoreType.DMA
        ],
        compiler_params=pltpu.CompilerParams(collective_id=0, has_side_effects=True),
        name="gather_blocks",
    )(ordered)


def pick(halves, index, low):
    first, second = [jnp.take_along_axis(half, index, axis=0, mode="promise_in_bounds") for half in halves]
    return jnp.where(low, first, second)


def placed(sources, tap, limit):
    halves = [(source[:8], source[8:]) for source in sources]
    parts = [[] for _ in sources]
    for i in range(tap.shape[0] // 8):
        t = tap[8 * i : 8 * i + 8]
        inside = (t >= 0) & (t < limit)
        low = t < 8
        index = t & 7
        for out, pair in zip(parts, halves):
            out.append(jnp.where(inside, pick(pair, index, low), 0.0))
    return [jnp.concatenate(part, axis=0) for part in parts]


def grid_kernel(
    words, meta, bits, strip, x_all, first_all, taps_ref, second_ref, turn_ref,
    out_ref, acc, mid, stage, acc4, extra, x_ref, first_ref, spread, items, sems,
):
    s = strip[0]
    fetch_x = pltpu.make_async_copy(x_all, x_ref, sems.at[0])
    fetch_x.start()
    fetch_first = pltpu.make_async_copy(first_all, first_ref, sems.at[1])
    fetch_first.start()
    acc[0] = jnp.zeros(acc.shape[1:], F32)

    @pl.when(s == 0)
    def _():
        acc[1] = jnp.zeros(acc.shape[1:], F32)

    table = taps_ref[...]
    table_hi = table.astype(BF16)
    table_lo = (table - table_hi.astype(F32)).astype(BF16)
    both_tables = jnp.concatenate([table_hi, table_lo], axis=0)

    def listed(kind, count, groups=128):
        def group(g, n):
            def step(state):
                word, n = state
                low = word & -word
                bit = bits[lax.shift_right_logical(low * BIT_MUL, 27)]
                items[n] = (kind << 12) | ((g * NB_DEV + (bit & 15)) << 1) | (bit >> 4)
                return word ^ low, n + 1

            return lax.while_loop(lambda state: state[0] != 0, step, (words[kind * 128 + g], n))[1]

        return lax.fori_loop(0, groups, group, count)

    def place_of(code):
        block = (code >> 1) & (BLOCKS - 1)
        where = meta[block]
        cell = (where >> 14) & 31
        anchor_row = (where >> 19) * TILE_R + (cell >> 3) * 128
        return anchor_row, ((block >> 4) & 7) * TILE_C + (cell & 7) * 128

    def values_of(code):
        half, block = code & 1, (code >> 1) & (BLOCKS - 1)
        owner, own = block >> 4, block & 15
        x = x_ref[owner, pl.ds(pl.multiple_of((own >> 1) * 16, 16), 16), :].astype(F32)
        x = jnp.where((own & 1) == 1, x[8:], x[:8])
        x = jnp.where(half == 1, pltpu.roll(x, 4, 0), x)
        packed = x_ref[owner, pl.ds(pl.multiple_of(CODES + (own >> 2) * 16, 16), 16), :].astype(F32)
        packed = jnp.where((own & 2) == 2, packed[8:], packed[:8])
        packed = jnp.where((own & 1) == 1, pltpu.roll(packed, 4, 0), packed)
        packed = jnp.where(half == 1, pltpu.roll(packed, 6, 0), packed).astype(I32)
        first, second = packed[:1], packed[1:2]
        power = sum([(first >= (128 << n)).astype(I32) for n in range(1, 8)])
        power2 = sum([(second >= (128 << n)).astype(I32) for n in range(1, 4)])
        return x, (first >> power) - 128, (second >> power2) - 128, power * 4 + power2

    def factors_of(x, wplane):
        chosen = ones_where(iota((32, 128), 0) == wplane)
        taps = dot(both_tables, chosen)
        tap_re, tap_im = taps[:16], taps[16:32]
        full_re, full_im = tap_re + taps[32:48], tap_im + taps[48:64]
        weights_re, weights_im = [], []
        for p in range(2):
            re, im = x[2 * p : 2 * p + 1], x[2 * p + 1 : 2 * p + 2]
            weights_re.append((re * full_re - im * full_im).astype(BF16).astype(F32))
            weights_im.append((re * full_im + im * full_re).astype(BF16).astype(F32))
        return weights_re + weights_im + [tap_re, tap_im]

    def limit_of(col, anchor_col):
        return jnp.minimum(jnp.where(anchor_col == GRID - 128, 128, 1000) - col, TAPS)

    def item(code, valid, slot):
        anchor_row, anchor_col = place_of(code)
        base_at = pl.multiple_of(slot * 104, 8)
        where = spread[pl.ds(base_at + 96, 8), :].astype(I32)
        row, col = where[:1], where[1:2]
        limit = limit_of(col, anchor_col)
        factors = [spread[pl.ds(base_at + 16 * i, 16), :] for i in range(6)]
        weights, taps = factors[:4], factors[4:]
        kind = code >> 12
        mirror, middle = kind == 1, kind == 2
        sign = jnp.where(mirror, -1, 1)
        base = jnp.where(middle, GRID // 2, jnp.where(mirror, GRID - s * ROWS, s * ROWS)) - anchor_row
        base = jnp.where(valid, base, -100000)
        least = jnp.where(mirror & (s == 0), 1, 0)
        j = iota((ROWS, 128), 0)
        most = jnp.where(middle, 0, ROWS)
        tap = jnp.where((j < least) | (j > most), -1, base + sign * j - row)
        re0, re1, im0, im1 = placed(weights, tap, TAPS)
        flip = jnp.where(mirror, -1.0, 1.0)
        left = jnp.concatenate([re0, re1, im0 * flip, im1 * flip], axis=0).astype(BF16)
        right = jnp.concatenate([-im0, -im1, re0 * flip, re1 * flip], axis=0).astype(BF16)
        tap = jnp.where(mirror, 144, 0) + sign * iota((WINDOW, 128), 0) - col
        col_re, col_im = placed(taps, tap, limit)
        cols = jnp.concatenate([col_re.astype(BF16), col_im.astype(BF16)], axis=1)
        patch = dot_nt(cols, jnp.concatenate([left, right], axis=1))
        start = jnp.where(mirror, GRID - 128 - anchor_col, anchor_col + HEAD)
        return middle.astype(I32), pl.multiple_of(start, 16), patch

    count = listed(2, listed(1, listed(0, 0)), jnp.where(s == 0, 128, 0))
    fetch_x.wait()

    def batch(i, carry):
        first_item = i * BATCH
        rounds = (jnp.minimum(count - first_item, BATCH) + UNROLL - 1) // UNROLL

        def code_at(n):
            valid = n < count
            return jnp.where(valid, items[n], 0), valid

        def prepare(r, carry):
            for k in range(UNROLL):
                slot = r * UNROLL + k
                x, row, col, wplane = values_of(code_at(first_item + slot)[0])
                base_at = pl.multiple_of(slot * 104, 8)
                for f, factor in enumerate(factors_of(x, wplane)):
                    spread[pl.ds(base_at + f * 16, 16), :] = factor
                spread[pl.ds(base_at + 96, 8), :] = jnp.where(iota((8, 128), 0) == 0, row, col).astype(F32)
            return carry

        lax.fori_loop(0, rounds, prepare, 0)

        def several(r, carry):
            found = []
            for k in range(UNROLL):
                slot = r * UNROLL + k
                found.append(item(*code_at(first_item + slot), slot))
            for target, start, patch in found:
                acc[target, pl.ds(start, WINDOW), :] += patch
            return carry

        lax.fori_loop(0, rounds, several, 0)
        return carry

    lax.fori_loop(0, (count + BATCH - 1) // BATCH, batch, 0)
    acc[0, HEAD : HEAD + 8, :] += jnp.where(iota((8, 128), 0) == 0, acc[0, HEAD + GRID : HEAD + GRID + 8, :], 0.0)

    lane = iota((1, 128), 1)
    flip = jnp.where(lane < 64, -1.0, 1.0)

    fetch_first.wait()

    @pl.when(s == 0)
    def _():
        picked = ones_where(iota((8, 128), 1) == 32 * iota((8, 128), 0))

        def turn_block(c1, carry):
            block = acc[1, pl.ds(pl.multiple_of(HEAD + c1 * 128, 16), 128), :].astype(BF16)
            acc4[pl.ds(pl.multiple_of(c1 * 8, 8), 8), :] = dot_nt(picked, block)
            return carry

        lax.fori_loop(0, 64, turn_block, 0, unroll=8)
        cosine = first_ref[0, :64, :64]
        sine = first_ref[0, 64:, :64]
        turn_cos, turn_sin = turn_ref[:64], turn_ref[64:]
        for p in range(2):
            re = acc4[pl.ds(p, 64, stride=8), :].astype(BF16)
            im = acc4[pl.ds(2 + p, 64, stride=8), :].astype(BF16)
            mid_re = dot(cosine, re) - dot(sine, im)
            mid_im = dot(cosine, im) + dot(sine, re)
            turned_re = (mid_re * turn_cos - mid_im * turn_sin).astype(BF16)
            turned_im = (mid_re * turn_sin + mid_im * turn_cos).astype(BF16)
            extra[p] = dot(turned_re, second_ref[:128, :128]) - dot(turned_im, second_ref[:128, 128:])

    def column_first(c0, carry):
        h = acc[0, pl.ds(HEAD + c0, 64, stride=128), :]
        high = h.astype(BF16)
        low = (h - high.astype(F32)).astype(BF16)
        factors = first_ref[c0]
        got = dot(
            jnp.concatenate([factors, factors], axis=1), jnp.concatenate([high, high, low, low], axis=0)
        )
        y = got[:64] + flip * pltpu.roll(got[64:], 64, 1)
        mid[pl.ds(pl.multiple_of(c0 * 64, 64), 64), :] = y
        return carry

    lax.fori_loop(0, 128, column_first, 0, unroll=16)

    second_hi = second_ref[:128]
    second_lo = second_ref[128:]

    for group in range(4):

        def column_second(v, carry):
            v0 = group * 16 + v
            y = mid[pl.ds(v0, 128, stride=64), :]
            turned = flip * pltpu.roll(y, 64, 1)
            pair = jnp.concatenate([y.astype(BF16), turned.astype(BF16)], axis=0)
            z = dot(second_hi, pair) + dot(second_lo, pair)
            stage[pl.ds(v, 128, stride=16), :] = z
            return carry

        lax.fori_loop(0, 16, column_second, 0, unroll=16)

        def pack(d, carry):
            out_ref[d, group * 16 : group * 16 + 16, :] = stage[
                pl.ds(pl.multiple_of(d * 16, 16), 16), :
            ].astype(BF16)
            return carry

        def pack_middle(d, carry):
            z = stage[pl.ds(pl.multiple_of(d * 16, 16), 16), :]
            at = jnp.full((16, 128), d, I32)
            for p in range(2):
                middle = jnp.take_along_axis(
                    extra[p, group * 16 : group * 16 + 16, :], at, axis=1, mode="promise_in_bounds"
                )
                z = jnp.where(lane == 64 + 32 * p, middle, z)
            out_ref[d, group * 16 : group * 16 + 16, :] = z.astype(BF16)
            return carry

        @pl.when(s != 0)
        def _():
            lax.fori_loop(0, 128, pack, 0, unroll=8)

        @pl.when(s == 0)
        def _():
            lax.fori_loop(0, 128, pack_middle, 0, unroll=8)


def image_kernel(in_ref, first_ref, turn_ref, last_ref, out_ref, wide, left, right):
    def widen(s, carry):
        wide[pl.ds(pl.multiple_of(s * 16, 16), 16), :] = in_ref[s].astype(F32)
        return carry

    lax.fori_loop(0, DEVICES, widen, 0, unroll=8)
    flip = jnp.where(iota((1, 128), 1) < 64, -1.0, 1.0)
    first = first_ref[...]
    last = last_ref[...]

    def one(v, carry):
        y = wide[pl.ds(v, DEVICES, stride=16), :]
        rolled = pltpu.roll(y, 64, 1)
        pair = jnp.concatenate([y.astype(BF16), (flip * rolled).astype(BF16)], axis=0)
        got = dot(first, pair) + turn_ref[2] * rolled[:1]
        turned = (got * turn_ref[0] + pltpu.roll(got, 64, 1) * turn_ref[1]).astype(BF16)
        result = dot_nt(last, jnp.concatenate([turned, turned], axis=1))
        left[pl.ds(pl.multiple_of(v * 64, 64), 64), :] = result[:, :128]
        right[pl.ds(pl.multiple_of(v * 64, 64), 64), :] = result[:, 128:]
        return carry

    lax.fori_loop(0, 16, one, 0, unroll=16)

    def place(u1, carry):
        for p in range(2):
            for half in range(2):
                for side, ref in ((0, left), (1, right)):
                    out_ref[p, half * 8 : half * 8 + 8, pl.ds(pl.multiple_of(u1 * 256 + side * 128, 128), 128)] = (
                        ref[pl.ds(half * 512 + p * 32 + u1, 8, stride=64), :]
                    )
        return carry

    lax.fori_loop(0, 32, place, 0, unroll=4)


def words_of(code, s):
    row = (code >> 19) * TILE_R + ((code >> 17) & 3) * 128
    top, bottom = (code >> 7) & 127, code & 127
    shift = jnp.arange(NB_DEV, dtype=I32)[None, :]

    def packed(first, final):
        hit = (final >= 0) & (first < 128 + TAPS - 1)
        one = (hit & (top >= first - (TAPS - 1))).astype(I32)
        two = (hit & (bottom <= final)).astype(I32)
        both = one.reshape(128, NB_DEV) << shift | two.reshape(128, NB_DEV) << (shift + 16)
        return jnp.sum(both, axis=1)

    direct = s * ROWS - row
    mirror = GRID - ROWS + 1 - s * ROWS - row
    middle = GRID // 2 - row
    middle = packed(middle, middle) * (s == 0).astype(I32)
    return jnp.concatenate([packed(direct, direct + ROWS - 1), packed(mirror, mirror + ROWS - 1), middle])


def gridded(words, codes_all, s, x_all, taps):
    vmem = pl.BlockSpec(memory_space=pltpu.VMEM)
    smem = pl.BlockSpec(memory_space=pltpu.SMEM)
    first, second, turn = column_tables()
    return pl.pallas_call(
        grid_kernel,
        out_shape=jax.ShapeDtypeStruct((DEVICES, 64, 128), BF16),
        in_specs=[smem] * 4 + [pl.BlockSpec(memory_space=pl.ANY)] * 2 + [vmem] * 3,
        out_specs=vmem,
        scratch_shapes=[
            pltpu.VMEM((2, HEAD + GRID + 32, 128), F32),
            pltpu.VMEM((128 * 64, 128), F32),
            pltpu.VMEM((DEVICES * 16, 128), F32),
            pltpu.VMEM((64 * 8, 128), F32),
            pltpu.VMEM((2, 64, 128), F32),
            pltpu.VMEM((DEVICES, AGR, 128), BF16),
            pltpu.VMEM((128, 128, 128), BF16),
            pltpu.VMEM((BATCH * 104, 128), F32),
            pltpu.SMEM((4096,), I32),
            pltpu.SemaphoreType.DMA((2,)),
        ],
        compiler_params=pltpu.CompilerParams(vmem_limit_bytes=60 * 1024 * 1024),
        name="grid_columns",
    )(
        words, codes_all, jnp.asarray(bit_table()), s.reshape(1).astype(I32),
        x_all, jnp.asarray(first), taps, jnp.asarray(second), jnp.asarray(turn),
    )


def imaged(got):
    first, turn, last = row_tables()
    return pl.pallas_call(
        image_kernel,
        out_shape=jax.ShapeDtypeStruct((2, 64, GRID), F32),
        grid=(4,),
        in_specs=[
            pl.BlockSpec((DEVICES, 16, 128), lambda i: (0, i, 0)),
            pl.BlockSpec((256, 256), lambda i: (0, 0)),
            pl.BlockSpec((3, 256, 128), lambda i: (0, 0, 0)),
            pl.BlockSpec((64, 256), lambda i: (0, 0)),
        ],
        out_specs=pl.BlockSpec((2, 16, GRID), lambda i: (0, i, 0)),
        scratch_shapes=[
            pltpu.VMEM((DEVICES * 16, 128), F32),
            pltpu.VMEM((16 * 64, 128), F32),
            pltpu.VMEM((16 * 64, 128), F32),
        ],
        compiler_params=pltpu.CompilerParams(vmem_limit_bytes=48 * 1024 * 1024),
        name="image_rows",
    )(got, jnp.asarray(first), jnp.asarray(turn), jnp.asarray(last))


def sorted_blocks(visibilities, keep_flags, kernel_index, row_offset, col_offset, cell_index, tile_row):
    vmem = pl.BlockSpec(memory_space=pltpu.VMEM)
    smem = pl.BlockSpec(memory_space=pltpu.SMEM)
    return pl.pallas_call(
        sort_kernel,
        out_shape=jax.ShapeDtypeStruct((AGR, 128), BF16),
        in_specs=[vmem] * 5 + [smem] * 2,
        out_specs=vmem,
        scratch_shapes=[pltpu.VMEM((128, 128), F32), pltpu.VMEM((NOTES, 128), F32)],
        name="sort_blocks",
    )(visibilities, keep_flags, kernel_index, row_offset, col_offset, cell_index, tile_row)


def shards(visibilities, keep_flags, kernel_index, row_offset, col_offset, cell_index, tile_row, kernel_taps):
    s = lax.axis_index("au") * 8 + lax.axis_index("vert")
    ordered = sorted_blocks(
        visibilities, keep_flags, kernel_index, row_offset, col_offset, cell_index, tile_row.reshape(NB_DEV)
    )
    x_all = gathered(ordered).reshape(DEVICES, AGR, 128)
    found = x_all[:, NOTES : NOTES + 4, :NB_DEV].astype(I32)
    codes_all = ((found[:, 0] * 32 + found[:, 1]) << 14) | (found[:, 2] << 7) | found[:, 3]
    codes_all = codes_all.reshape(BLOCKS)
    words = words_of(codes_all, s)
    taps = kernel_taps.transpose(1, 2, 0).reshape(2 * TAPS, 32)
    sent = gridded(words, codes_all, s, x_all, taps)
    got = lax.all_to_all(sent, BOTH, split_axis=0, concat_axis=0, tiled=True)
    return imaged(got)


def solution(mesh):
    in_specs = (
        P(BOTH, None, None, None),
        P(BOTH, None),
        P(BOTH, None),
        P(BOTH, None),
        P(BOTH, None),
        P(BOTH),
        P(BOTH, None),
        P(),
    )
    out_specs = P(None, BOTH, None)
    return jax.shard_map(shards, mesh=mesh, in_specs=in_specs, out_specs=out_specs, check_vma=False)
```

```python
import functools
import math

import jax
import jax.numpy as jnp
import numpy as np
from jax import lax
from jax.experimental import pallas as pl
from jax.experimental.pallas import tpu as pltpu
from jax.sharding import PartitionSpec as P

KVIS = 256
TAPS = 16
TILE_R = 512
TILE_C = 1024
NB_DEV = 16
BLOCKS = 2048
GRID = 8192
DEVICES = 128
ROWS = 32
HEAD = 16
WINDOW = 152
UNROLL = 16
BATCH = 64
BOTH = ("au", "vert")
F32 = jnp.float32
BF16 = jnp.bfloat16
I32 = jnp.int32
NT = (((1,), (1,)), ((), ()))
BIT_MUL = 0x077CB531


def bit_table():
    table = np.zeros(32, np.int32)
    for bit in range(32):
        table[((BIT_MUL << bit) & 0xFFFFFFFF) >> 27] = bit
    return table


def hi_lo(values):
    high = values.astype(jnp.bfloat16)
    low = (values - high.astype(np.float64)).astype(jnp.bfloat16)
    return high, low


@functools.lru_cache(None)
def column_tables():
    v0, c1 = np.arange(64), np.arange(64)
    c0 = np.arange(128)
    angle = 2 * np.pi / GRID * ((v0[None, :, None] * (128 * c1[None, None, :] + c0[:, None, None])) % GRID)
    first = np.concatenate([np.cos(angle), np.sin(angle)], axis=1)
    first = np.concatenate(hi_lo(first), axis=2)
    angle = 2 * np.pi / 128 * ((c0[:, None] * c0[None, :]) % 128)
    second = np.concatenate(hi_lo(np.concatenate([np.cos(angle), np.sin(angle)], axis=1)), axis=0)
    angle = 2 * np.pi / GRID * (v0[:, None] * c0[None, :])
    turn = np.concatenate([np.cos(angle), np.sin(angle)], axis=0).astype(np.float32)
    return first, second, turn


@functools.lru_cache(None)
def row_tables():
    scale = 1.0 / math.sqrt(BLOCKS * KVIS)
    u0, s = np.arange(256), np.arange(128)
    angle = 2 * np.pi / 256 * ((u0[:, None] * s[None, :]) % 256)
    first = np.concatenate([np.cos(angle), np.sin(angle)], axis=1).astype(jnp.bfloat16)
    comp, j = np.arange(128) // 64, np.arange(128) % 32
    plane = np.arange(128) // 32 % 2
    angle = 2 * np.pi / GRID * (u0[:, None] * j[None, :])
    turn_cos = (np.cos(angle) * scale).astype(np.float32)
    turn_sin = (np.sin(angle) * np.where(comp == 0, -1.0, 1.0) * scale).astype(np.float32)
    alternate = ((1.0 - 2.0 * (u0 % 2))[:, None] * ((comp == 0) & (j == 0))[None, :]).astype(np.float32)
    u1 = np.arange(32)
    angle = 2 * np.pi / 32 * ((u1[:, None] * j[None, :]) % 32)
    last = np.where(comp == 0, np.cos(angle), -np.sin(angle))
    last = np.concatenate([last * (plane == p) for p in range(2)], axis=0)
    last = np.concatenate(hi_lo(last), axis=1)
    return first, np.stack([turn_cos, turn_sin, alternate]), last


def iota(shape, dim):
    return lax.broadcasted_iota(I32, shape, dim)


def ones_where(mask):
    return jnp.where(mask, 1.0, 0.0).astype(BF16)


def dot(a, b):
    return jnp.dot(a, b, preferred_element_type=F32)


def dot_nt(a, b):
    return lax.dot_general(a, b, NT, preferred_element_type=F32)


def sort_kernel(vis_ref, keep_ref, plane_ref, row_ref, col_ref, cell_ref, tile_ref, out_ref, meta, wide):
    below = ones_where(iota((128, 128), 1) < iota((128, 128), 0))
    before = ones_where(iota((KVIS, KVIS), 0) < iota((KVIS, KVIS), 1))
    ones = jnp.ones((KVIS, KVIS), BF16)
    value = iota((128, KVIS), 0)
    place = iota((KVIS, KVIS), 0)
    slot = iota((8, KVIS), 0)
    lane = iota((1, 128), 1)

    meta[...] = jnp.zeros_like(meta)

    def one_block(i, carry):
        at = pl.ds(i, 1)
        row = row_ref[at, :]
        keep = keep_ref[at, :] == 1
        wplane = plane_ref[at, :]
        first = (128 + row) << (wplane >> 2)
        second = (128 + col_ref[at, :]) << (wplane & 3)
        x = jnp.where(slot == 4, first, jnp.where(slot == 5, second, jnp.where(slot == 6, row, 0)))
        x = x.astype(F32)
        for p in range(2):
            pair = vis_ref[i, p].astype(F32)
            for c in range(2):
                x = jnp.where((slot == 2 * p + c) & keep, pair[c : c + 1], x)
        x = x.astype(BF16)
        hit = value == row
        hot = ones_where(hit)
        rank = dot(hot, before) + dot(dot(below, hot).astype(BF16), ones)
        rank = jnp.sum(jnp.where(hit, rank, 0.0), axis=0, keepdims=True)
        moved = dot_nt(x, ones_where(place == rank.astype(I32)))
        left, right = moved[:, :128], moved[:, 128:]
        wide[pl.ds(pl.multiple_of(i * 8, 8), 8), :] = jnp.where(iota((8, 128), 0) < 4, left, pltpu.roll(right, 4, 0))
        for k, part in enumerate((left[4:5], left[5:6], right[4:5], right[5:6])):
            wide[pl.ds(CODES + i * 4 + k, 1), :] = part
        note = jnp.where(lane == 0, tile_ref[i], jnp.where(lane == 1, cell_ref[i], 0)).astype(F32)
        note = jnp.where(lane == 2, moved[6:7, 127:128], jnp.where(lane == 3, moved[6:7, 128:129], note))
        meta[at, :] = note
        return carry

    lax.fori_loop(0, NB_DEV, one_block, 0, unroll=8)
    turned = dot_nt(ones_where(iota((16, 128), 0) == iota((16, 128), 1)), meta[...].astype(BF16))
    out_ref[:NOTES, :] = wide[...].astype(BF16)
    out_ref[NOTES:, :] = turned.astype(BF16)


AGR = 208
CODES = 128
NOTES = 192
PARTS = ((0, 32, 32), (64, 32, 32), (128, 48, 32))
ORDERS = (("x", "y", "z"), ("y", "z", "x"), ("z", "x", "y"))


def gather_kernel(x_ref, all_ref, send, recv, local):
    au, vert = lax.axis_index("au"), lax.axis_index("vert")
    here = {"y": au // 4, "z": au % 4, "x": vert // 2}
    core = vert % 2

    def device(at, core):
        return (at["y"] * 4 + at["z"], at["x"] * 2 + core)

    def moved(dim, step):
        return {**here, dim: (here[dim] + step) % 4}

    sibling = device(here, 1 - core)
    barrier = pltpu.get_barrier_semaphore()
    for other in [device(moved(d, step), core) for d in "xyz" for step in (1, 2, 3)] + [sibling]:
        pl.semaphore_signal(barrier, inc=1, device_id=other, device_id_type=pl.DeviceIdType.MESH)
    own = pltpu.make_async_copy(x_ref, all_ref.at[here["y"], here["z"], here["x"], core], local)
    own.start()
    own.wait()
    pl.semaphore_wait(barrier, 10)

    def region(part, full, at, rows=None):
        first, one, two = PARTS[part]
        start, size = {None: (first, one + two), 0: (first, one), 1: (first + one, two)}[rows]
        index = [slice(None) if d in full else at[d] for d in "yzx"]
        return all_ref.at[(*index, core, pl.ds(start, size), slice(None))]

    used = [0]
    started = []

    def copy(ref, to):
        n = used[0]
        used[0] += 1
        made = pltpu.make_async_remote_copy(
            src_ref=ref, dst_ref=ref, send_sem=send.at[n], recv_sem=recv.at[n],
            device_id=to, device_id_type=pl.DeviceIdType.MESH,
        )
        made.start()
        started.append(made)
        return made

    shared = []
    for phase in range(2):
        direct = []
        for part, order in enumerate(ORDERS):
            ref = region(part, order[:phase], here)
            direct += [copy(ref, device(moved(order[phase], step), core)) for step in (2, 1, 3)]
        for made in direct:
            made.wait_recv()
    for phase in (2,):
        plain, relayed = [], []
        for part, order in enumerate(ORDERS):
            full, dim = order[:phase], order[phase]
            ref = region(part, full, here)
            right = copy(ref, device(moved(dim, 1), core))
            left = copy(ref, device(moved(dim, 3), core))
            plain.append((right, left))
        if phase == 2:
            for part, order in enumerate(ORDERS):
                shared.append(copy(region(part, order[:2], here), sibling))
        for part, order in enumerate(ORDERS):
            full, dim = order[:phase], order[phase]
            right, left = plain[part]
            right.wait_recv()
            one = copy(region(part, full, moved(dim, 3), 0), device(moved(dim, 1), core))
            if phase == 2:
                shared.append(copy(region(part, full, moved(dim, 3)), sibling))
            left.wait_recv()
            two = copy(region(part, full, moved(dim, 1), 1), device(moved(dim, 3), core))
            if phase == 2:
                shared.append(copy(region(part, full, moved(dim, 1)), sibling))
            relayed.append((one, two))
        for part, order in enumerate(ORDERS):
            full, dim = order[:phase], order[phase]
            for half, made in enumerate(relayed[part]):
                made.wait_recv()
                if phase == 2:
                    shared.append(copy(region(part, full, moved(dim, 2), half), sibling))
    for made in shared:
        made.wait_recv()
    for made in started:
        made.wait_send()


COPIES = 3 * (3 + 3 + 4 + 5)


def gathered(ordered):
    anywhere = pl.BlockSpec(memory_space=pl.ANY)
    return pl.pallas_call(
        gather_kernel,
        out_shape=jax.ShapeDtypeStruct((4, 4, 4, 2, AGR, 128), BF16),
        in_specs=[anywhere],
        out_specs=anywhere,
        scratch_shapes=[
            pltpu.SemaphoreType.DMA((COPIES,)), pltpu.SemaphoreType.DMA((COPIES,)), pltpu.SemaphoreType.DMA
        ],
        compiler_params=pltpu.CompilerParams(collective_id=0, has_side_effects=True),
        name="gather_blocks",
    )(ordered)


def pick(halves, index, low):
    first, second = [jnp.take_along_axis(half, index, axis=0, mode="promise_in_bounds") for half in halves]
    return jnp.where(low, first, second)


def placed(sources, tap, limit):
    halves = [(source[:8], source[8:]) for source in sources]
    parts = [[] for _ in sources]
    for i in range(tap.shape[0] // 8):
        t = tap[8 * i : 8 * i + 8]
        inside = (t >= 0) & (t < limit)
        low = t < 8
        index = t & 7
        for out, pair in zip(parts, halves):
            out.append(jnp.where(inside, pick(pair, index, low), 0.0))
    return [jnp.concatenate(part, axis=0) for part in parts]


def grid_kernel(
    words0, words1, words2, meta, bits, strip, x_all, first_all, taps_ref, second_ref, turn_ref,
    out_ref, acc, mid, stage, acc4, extra, x_ref, first_ref, spread, items, sems,
):
    words = (words0, words1, words2)
    s = strip[0]
    fetch_x = pltpu.make_async_copy(x_all, x_ref, sems.at[0])
    fetch_x.start()
    fetch_first = pltpu.make_async_copy(first_all, first_ref, sems.at[1])
    acc[0] = jnp.zeros(acc.shape[1:], F32)

    @pl.when(s == 0)
    def _():
        acc[1] = jnp.zeros(acc.shape[1:], F32)

    table = taps_ref[...]
    table_hi = table.astype(BF16)
    table_lo = (table - table_hi.astype(F32)).astype(BF16)
    both_tables = jnp.concatenate([table_hi, table_lo], axis=0)

    def listed(kind, count, groups=128):
        def group(g, n):
            def step(state):
                word, n = state
                low = word & -word
                bit = bits[lax.shift_right_logical(low * BIT_MUL, 27)]
                items[n] = (kind << 12) | ((g * NB_DEV + (bit & 15)) << 1) | (bit >> 4)
                return word ^ low, n + 1

            return lax.while_loop(lambda state: state[0] != 0, step, (words[kind][g], n))[1]

        return lax.fori_loop(0, groups, group, count)

    def place_of(code):
        block = (code >> 1) & (BLOCKS - 1)
        where = meta[block]
        cell = (where >> 14) & 31
        anchor_row = (where >> 19) * TILE_R + (cell >> 3) * 128
        return anchor_row, ((block >> 4) & 7) * TILE_C + (cell & 7) * 128

    def values_of(code):
        half, block = code & 1, (code >> 1) & (BLOCKS - 1)
        owner, own = block >> 4, block & 15
        x = x_ref[owner, pl.ds(pl.multiple_of((own >> 1) * 16, 16), 16), :].astype(F32)
        x = jnp.where((own & 1) == 1, x[8:], x[:8])
        x = jnp.where(half == 1, pltpu.roll(x, 4, 0), x)
        packed = x_ref[owner, pl.ds(pl.multiple_of(CODES + (own >> 2) * 16, 16), 16), :].astype(F32)
        packed = jnp.where((own & 2) == 2, packed[8:], packed[:8])
        packed = jnp.where((own & 1) == 1, pltpu.roll(packed, 4, 0), packed)
        packed = jnp.where(half == 1, pltpu.roll(packed, 6, 0), packed).astype(I32)
        first, second = packed[:1], packed[1:2]
        power = sum([(first >= (128 << n)).astype(I32) for n in range(1, 8)])
        power2 = sum([(second >= (128 << n)).astype(I32) for n in range(1, 4)])
        return x, (first >> power) - 128, (second >> power2) - 128, power * 4 + power2

    def factors_of(x, wplane, flip):
        chosen = ones_where(iota((32, 128), 0) == wplane)
        taps = dot(both_tables, chosen)
        tap_re, tap_im = taps[:16], taps[16:32]
        full_re, full_im = tap_re + taps[32:48], tap_im + taps[48:64]
        weights_re, weights_im = [], []
        for p in range(2):
            re, im = x[2 * p : 2 * p + 1], x[2 * p + 1 : 2 * p + 2]
            weights_re.append((re * full_re - im * full_im).astype(BF16).astype(F32))
            weights_im.append((re * full_im + im * full_re).astype(BF16).astype(F32))
        return weights_re + [im * flip for im in weights_im] + [tap_re, tap_im * flip]

    def limit_of(col, anchor_col):
        return jnp.minimum(jnp.where(anchor_col == GRID - 128, 128, 1000) - col, TAPS)

    def item(code, valid, slot):
        anchor_row, anchor_col = place_of(code)
        base_at = pl.multiple_of(slot * 104, 8)
        where = spread[pl.ds(base_at + 96, 8), :].astype(I32)
        row, col = where[:1], where[1:2]
        limit = limit_of(col, anchor_col)
        factors = [spread[pl.ds(base_at + 16 * i, 16), :] for i in range(6)]
        weights, taps = factors[:4], factors[4:]
        kind = code >> 12
        mirror, middle = kind == 1, kind == 2
        sign = jnp.where(mirror, -1, 1)
        base = jnp.where(middle, GRID // 2, jnp.where(mirror, GRID - s * ROWS, s * ROWS)) - anchor_row
        base = jnp.where(valid, base, -100000)
        least = jnp.where(mirror & (s == 0), 1, 0)
        j = iota((ROWS, 128), 0)
        most = jnp.where(middle, 0, ROWS)
        tap = jnp.where((j < least) | (j > most), -1, base + sign * j - row)
        re0, re1, im0, im1 = placed(weights, tap, TAPS)
        left = jnp.concatenate([re0, re1, im0, im1], axis=0).astype(BF16)
        right = jnp.concatenate([-im0, -im1, re0, re1], axis=0).astype(BF16)
        tap = jnp.where(mirror, 144, 0) + sign * iota((WINDOW, 128), 0) - col
        col_re, col_im = placed(taps, tap, limit)
        cols = jnp.concatenate([col_re.astype(BF16), col_im.astype(BF16)], axis=1)
        patch = dot_nt(cols, jnp.concatenate([left, right], axis=1))
        start = jnp.where(mirror, GRID - 128 - anchor_col, anchor_col + HEAD)
        return middle.astype(I32), pl.multiple_of(start, 16), patch

    count = listed(2, listed(1, listed(0, 0)), jnp.where(s == 0, 128, 0))
    fetch_x.wait()
    fetch_first.start()

    def batch(i, carry):
        first_item = i * BATCH
        rounds = (jnp.minimum(count - first_item, BATCH) + UNROLL - 1) // UNROLL

        def code_at(n):
            valid = n < count
            return jnp.where(valid, items[n], 0), valid

        def prepare(r, carry):
            for k in range(UNROLL):
                slot = r * UNROLL + k
                code = code_at(first_item + slot)[0]
                x, row, col, wplane = values_of(code)
                flip = jnp.where((code >> 12) == 1, -1.0, 1.0)
                base_at = pl.multiple_of(slot * 104, 8)
                for f, factor in enumerate(factors_of(x, wplane, flip)):
                    spread[pl.ds(base_at + f * 16, 16), :] = factor
                spread[pl.ds(base_at + 96, 8), :] = jnp.where(iota((8, 128), 0) == 0, row, col).astype(F32)
            return carry

        lax.fori_loop(0, rounds, prepare, 0)

        def several(r, carry):
            found = []
            for k in range(UNROLL):
                slot = r * UNROLL + k
                found.append(item(*code_at(first_item + slot), slot))
            for target, start, patch in found:
                acc[target, pl.ds(start, WINDOW), :] += patch
            return carry

        lax.fori_loop(0, rounds, several, 0)
        return carry

    lax.fori_loop(0, (count + BATCH - 1) // BATCH, batch, 0)
    acc[0, HEAD : HEAD + 8, :] += jnp.where(iota((8, 128), 0) == 0, acc[0, HEAD + GRID : HEAD + GRID + 8, :], 0.0)

    lane = iota((1, 128), 1)
    flip = jnp.where(lane < 64, -1.0, 1.0)

    fetch_first.wait()

    @pl.when(s == 0)
    def _():
        picked = ones_where(iota((8, 128), 1) == 32 * iota((8, 128), 0))

        def turn_block(c1, carry):
            block = acc[1, pl.ds(pl.multiple_of(HEAD + c1 * 128, 16), 128), :].astype(BF16)
            acc4[pl.ds(pl.multiple_of(c1 * 8, 8), 8), :] = dot_nt(picked, block)
            return carry

        lax.fori_loop(0, 64, turn_block, 0, unroll=8)
        cosine = first_ref[0, :64, :64]
        sine = first_ref[0, 64:, :64]
        turn_cos, turn_sin = turn_ref[:64], turn_ref[64:]
        for p in range(2):
            re = acc4[pl.ds(p, 64, stride=8), :].astype(BF16)
            im = acc4[pl.ds(2 + p, 64, stride=8), :].astype(BF16)
            mid_re = dot(cosine, re) - dot(sine, im)
            mid_im = dot(cosine, im) + dot(sine, re)
            turned_re = (mid_re * turn_cos - mid_im * turn_sin).astype(BF16)
            turned_im = (mid_re * turn_sin + mid_im * turn_cos).astype(BF16)
            extra[p] = dot(turned_re, second_ref[:128, :128]) - dot(turned_im, second_ref[:128, 128:])

    def column_first(c0, carry):
        h = acc[0, pl.ds(HEAD + c0, 64, stride=128), :]
        high = h.astype(BF16)
        low = (h - high.astype(F32)).astype(BF16)
        factors = first_ref[c0]
        got = dot(
            jnp.concatenate([factors, factors], axis=1), jnp.concatenate([high, high, low, low], axis=0)
        )
        y = got[:64] + flip * pltpu.roll(got[64:], 64, 1)
        mid[pl.ds(pl.multiple_of(c0 * 64, 64), 64), :] = y
        return carry

    lax.fori_loop(0, 128, column_first, 0, unroll=16)

    spots = ones_where(iota((256, 128), 1) == 64 + 32 * (iota((256, 128), 0) // 128))
    second_hi = second_ref[:128]
    second_lo = second_ref[128:]

    for group in range(4):

        def column_second(v, carry):
            v0 = group * 16 + v
            y = mid[pl.ds(v0, 128, stride=64), :]
            turned = flip * pltpu.roll(y, 64, 1)
            pair = jnp.concatenate([y.astype(BF16), turned.astype(BF16)], axis=0)
            z = dot(second_hi, pair) + dot(second_lo, pair)
            stage[pl.ds(v, 128, stride=16), :] = z
            return carry

        lax.fori_loop(0, 16, column_second, 0, unroll=16)

        def pack(d, carry):
            out_ref[d, group * 16 : group * 16 + 16, :] = stage[
                pl.ds(pl.multiple_of(d * 16, 16), 16), :
            ].astype(BF16)
            return carry

        def pack_middle(d8, carry):
            ahead = [extra[p, group * 16 : group * 16 + 16, :] for p in range(2)]
            parts = []
            for k in range(8):
                mine = iota((16, 128), 1) == d8 * 8 + k
                parts.append(jnp.concatenate([jnp.where(mine, z, 0.0) for z in ahead], axis=1))
            more = dot(jnp.concatenate(parts, axis=0).astype(BF16), spots)
            z = stage[pl.ds(pl.multiple_of(d8 * 128, 128), 128), :]
            z = jnp.where((lane == 64) | (lane == 96), more, z).astype(BF16)
            for k in range(8):
                out_ref[d8 * 8 + k, group * 16 : group * 16 + 16, :] = z[16 * k : 16 * k + 16]
            return carry

        @pl.when(s != 0)
        def _():
            lax.fori_loop(0, 128, pack, 0, unroll=8)

        @pl.when(s == 0)
        def _():
            lax.fori_loop(0, 16, pack_middle, 0, unroll=8)


def image_kernel(in_ref, first_ref, turn_ref, last_ref, out_ref, wide, left, right):
    def widen(s, carry):
        wide[pl.ds(pl.multiple_of(s * 16, 16), 16), :] = in_ref[s].astype(F32)
        return carry

    lax.fori_loop(0, DEVICES, widen, 0, unroll=8)
    flip = jnp.where(iota((1, 128), 1) < 64, -1.0, 1.0)
    first = first_ref[...]
    last = last_ref[...]

    def one(v, carry):
        y = wide[pl.ds(v, DEVICES, stride=16), :]
        rolled = pltpu.roll(y, 64, 1)
        pair = jnp.concatenate([y.astype(BF16), (flip * rolled).astype(BF16)], axis=0)
        got = dot(first, pair) + turn_ref[2] * rolled[:1]
        turned = (got * turn_ref[0] + pltpu.roll(got, 64, 1) * turn_ref[1]).astype(BF16)
        result = dot_nt(last, jnp.concatenate([turned, turned], axis=1))
        left[pl.ds(pl.multiple_of(v * 64, 64), 64), :] = result[:, :128]
        right[pl.ds(pl.multiple_of(v * 64, 64), 64), :] = result[:, 128:]
        return carry

    lax.fori_loop(0, 16, one, 0, unroll=16)

    def place(u1, carry):
        for p in range(2):
            for half in range(2):
                for side, ref in ((0, left), (1, right)):
                    out_ref[p, half * 8 : half * 8 + 8, pl.ds(pl.multiple_of(u1 * 256 + side * 128, 128), 128)] = (
                        ref[pl.ds(half * 512 + p * 32 + u1, 8, stride=64), :]
                    )
        return carry

    lax.fori_loop(0, 32, place, 0, unroll=4)


def words_of(code, s):
    row = (code >> 19) * TILE_R + ((code >> 17) & 3) * 128
    top, bottom = (code >> 7) & 127, code & 127
    shift = jnp.arange(NB_DEV, dtype=I32)[None, :]

    def packed(first, final):
        hit = (final >= 0) & (first < 128 + TAPS - 1)
        one = (hit & (top >= first - (TAPS - 1))).astype(I32)
        two = (hit & (bottom <= final)).astype(I32)
        both = one << shift | two << (shift + 16)
        return jnp.sum(both, axis=1)

    direct = s * ROWS - row
    mirror = GRID - ROWS + 1 - s * ROWS - row
    middle = GRID // 2 - row
    middle = packed(middle, middle) * (s == 0).astype(I32)
    return packed(direct, direct + ROWS - 1), packed(mirror, mirror + ROWS - 1), middle


def gridded(words, codes_all, s, x_all, taps):
    vmem = pl.BlockSpec(memory_space=pltpu.VMEM)
    smem = pl.BlockSpec(memory_space=pltpu.SMEM)
    first, second, turn = column_tables()
    return pl.pallas_call(
        grid_kernel,
        out_shape=jax.ShapeDtypeStruct((DEVICES, 64, 128), BF16),
        in_specs=[smem] * 6 + [pl.BlockSpec(memory_space=pl.ANY)] * 2 + [vmem] * 3,
        out_specs=vmem,
        scratch_shapes=[
            pltpu.VMEM((2, HEAD + GRID + 32, 128), F32),
            pltpu.VMEM((128 * 64, 128), F32),
            pltpu.VMEM((DEVICES * 16, 128), F32),
            pltpu.VMEM((64 * 8, 128), F32),
            pltpu.VMEM((2, 64, 128), F32),
            pltpu.VMEM((DEVICES, AGR, 128), BF16),
            pltpu.VMEM((128, 128, 128), BF16),
            pltpu.VMEM((BATCH * 104, 128), F32),
            pltpu.SMEM((4096,), I32),
            pltpu.SemaphoreType.DMA((2,)),
        ],
        compiler_params=pltpu.CompilerParams(vmem_limit_bytes=60 * 1024 * 1024),
        name="grid_columns",
    )(
        *words, codes_all.reshape(BLOCKS), jnp.asarray(bit_table()), s.reshape(1).astype(I32),
        x_all, jnp.asarray(first), taps, jnp.asarray(second), jnp.asarray(turn),
    )


def imaged(got):
    first, turn, last = row_tables()
    return pl.pallas_call(
        image_kernel,
        out_shape=jax.ShapeDtypeStruct((2, 64, GRID), F32),
        grid=(4,),
        in_specs=[
            pl.BlockSpec((DEVICES, 16, 128), lambda i: (0, i, 0)),
            pl.BlockSpec((256, 256), lambda i: (0, 0)),
            pl.BlockSpec((3, 256, 128), lambda i: (0, 0, 0)),
            pl.BlockSpec((64, 256), lambda i: (0, 0)),
        ],
        out_specs=pl.BlockSpec((2, 16, GRID), lambda i: (0, i, 0)),
        scratch_shapes=[
            pltpu.VMEM((DEVICES * 16, 128), F32),
            pltpu.VMEM((16 * 64, 128), F32),
            pltpu.VMEM((16 * 64, 128), F32),
        ],
        compiler_params=pltpu.CompilerParams(vmem_limit_bytes=48 * 1024 * 1024),
        name="image_rows",
    )(got, jnp.asarray(first), jnp.asarray(turn), jnp.asarray(last))


def sorted_blocks(visibilities, keep_flags, kernel_index, row_offset, col_offset, cell_index, tile_row):
    vmem = pl.BlockSpec(memory_space=pltpu.VMEM)
    smem = pl.BlockSpec(memory_space=pltpu.SMEM)
    return pl.pallas_call(
        sort_kernel,
        out_shape=jax.ShapeDtypeStruct((AGR, 128), BF16),
        in_specs=[vmem] * 5 + [smem] * 2,
        out_specs=vmem,
        scratch_shapes=[pltpu.VMEM((128, 128), F32), pltpu.VMEM((NOTES, 128), F32)],
        name="sort_blocks",
    )(visibilities, keep_flags, kernel_index, row_offset, col_offset, cell_index, tile_row)


def shards(visibilities, keep_flags, kernel_index, row_offset, col_offset, cell_index, tile_row, kernel_taps):
    s = lax.axis_index("au") * 8 + lax.axis_index("vert")
    ordered = sorted_blocks(
        visibilities, keep_flags, kernel_index, row_offset, col_offset, cell_index, tile_row.reshape(NB_DEV)
    )
    x_all = gathered(ordered).reshape(DEVICES, AGR, 128)
    found = x_all[:, NOTES : NOTES + 4, :NB_DEV].astype(I32)
    codes_all = ((found[:, 0] * 32 + found[:, 1]) << 14) | (found[:, 2] << 7) | found[:, 3]
    words = words_of(codes_all, s)
    taps = kernel_taps.transpose(1, 2, 0).reshape(2 * TAPS, 32)
    sent = gridded(words, codes_all, s, x_all, taps)
    got = lax.all_to_all(sent, BOTH, split_axis=0, concat_axis=0, tiled=True)
    return imaged(got)


def solution(mesh):
    in_specs = (
        P(BOTH, None, None, None),
        P(BOTH, None),
        P(BOTH, None),
        P(BOTH, None),
        P(BOTH, None),
        P(BOTH),
        P(BOTH, None),
        P(),
    )
    out_specs = P(None, BOTH, None)
    return jax.shard_map(shards, mesh=mesh, in_specs=in_specs, out_specs=out_specs, check_vma=False)
```

```python
import functools
import math

import jax
import jax.numpy as jnp
import numpy as np
from jax import lax
from jax.experimental import pallas as pl
from jax.experimental.pallas import tpu as pltpu
from jax.sharding import PartitionSpec as P

KVIS = 256
TAPS = 16
TILE_R = 512
TILE_C = 1024
NB_DEV = 16
BLOCKS = 2048
GRID = 8192
DEVICES = 128
ROWS = 32
HEAD = 16
WINDOW = 152
UNROLL = 16
BATCH = 64
BOTH = ("au", "vert")
F32 = jnp.float32
BF16 = jnp.bfloat16
I32 = jnp.int32
NT = (((1,), (1,)), ((), ()))
BIT_MUL = 0x077CB531


def bit_table():
    table = np.zeros(32, np.int32)
    for bit in range(32):
        table[((BIT_MUL << bit) & 0xFFFFFFFF) >> 27] = bit
    return table


def hi_lo(values):
    high = values.astype(jnp.bfloat16)
    low = (values - high.astype(np.float64)).astype(jnp.bfloat16)
    return high, low


@functools.lru_cache(None)
def column_tables():
    v0, c1 = np.arange(64), np.arange(64)
    c0 = np.arange(128)
    angle = 2 * np.pi / GRID * ((v0[None, :, None] * (128 * c1[None, None, :] + c0[:, None, None])) % GRID)
    first = np.concatenate([np.cos(angle), np.sin(angle)], axis=1)
    first = np.concatenate(hi_lo(first), axis=2)
    angle = 2 * np.pi / 128 * ((c0[:, None] * c0[None, :]) % 128)
    second = np.concatenate(hi_lo(np.concatenate([np.cos(angle), np.sin(angle)], axis=1)), axis=0)
    angle = 2 * np.pi / GRID * (v0[:, None] * c0[None, :])
    turn = np.concatenate([np.cos(angle), np.sin(angle)], axis=0).astype(np.float32)
    return first, second, turn


@functools.lru_cache(None)
def row_tables():
    scale = 1.0 / math.sqrt(BLOCKS * KVIS)
    u0, s = np.arange(256), np.arange(128)
    angle = 2 * np.pi / 256 * ((u0[:, None] * s[None, :]) % 256)
    first = np.concatenate([np.cos(angle), np.sin(angle)], axis=1).astype(jnp.bfloat16)
    comp, j = np.arange(128) // 64, np.arange(128) % 32
    plane = np.arange(128) // 32 % 2
    angle = 2 * np.pi / GRID * (u0[:, None] * j[None, :])
    turn_cos = (np.cos(angle) * scale).astype(np.float32)
    turn_sin = (np.sin(angle) * np.where(comp == 0, -1.0, 1.0) * scale).astype(np.float32)
    alternate = ((1.0 - 2.0 * (u0 % 2))[:, None] * ((comp == 0) & (j == 0))[None, :]).astype(np.float32)
    u1 = np.arange(32)
    angle = 2 * np.pi / 32 * ((u1[:, None] * j[None, :]) % 32)
    last = np.where(comp == 0, np.cos(angle), -np.sin(angle))
    last = np.concatenate([last * (plane == p) for p in range(2)], axis=0)
    last = np.concatenate(hi_lo(last), axis=1)
    return first, np.stack([turn_cos, turn_sin, alternate]), last


def iota(shape, dim):
    return lax.broadcasted_iota(I32, shape, dim)


def ones_where(mask):
    return jnp.where(mask, 1.0, 0.0).astype(BF16)


def dot(a, b):
    return jnp.dot(a, b, preferred_element_type=F32)


def dot_nt(a, b):
    return lax.dot_general(a, b, NT, preferred_element_type=F32)


def sort_kernel(vis_ref, keep_ref, plane_ref, row_ref, col_ref, cell_ref, tile_ref, out_ref, meta, wide):
    below = ones_where(iota((128, 128), 1) < iota((128, 128), 0))
    before = ones_where(iota((KVIS, KVIS), 0) < iota((KVIS, KVIS), 1))
    ones = jnp.ones((KVIS, KVIS), BF16)
    value = iota((128, KVIS), 0)
    place = iota((KVIS, KVIS), 0)
    slot = iota((8, KVIS), 0)
    lane = iota((1, 128), 1)

    meta[...] = jnp.zeros_like(meta)

    def one_block(i, carry):
        at = pl.ds(i, 1)
        row = row_ref[at, :]
        keep = keep_ref[at, :] == 1
        wplane = plane_ref[at, :]
        first = (128 + row) << (wplane >> 2)
        second = (128 + col_ref[at, :]) << (wplane & 3)
        x = jnp.where(slot == 4, first, jnp.where(slot == 5, second, jnp.where(slot == 6, row, 0)))
        x = x.astype(F32)
        for p in range(2):
            pair = vis_ref[i, p].astype(F32)
            for c in range(2):
                x = jnp.where((slot == 2 * p + c) & keep, pair[c : c + 1], x)
        x = x.astype(BF16)
        hit = value == row
        hot = ones_where(hit)
        rank = dot(hot, before) + dot(dot(below, hot).astype(BF16), ones)
        rank = jnp.sum(jnp.where(hit, rank, 0.0), axis=0, keepdims=True)
        moved = dot_nt(x, ones_where(place == rank.astype(I32)))
        left, right = moved[:, :128], moved[:, 128:]
        wide[pl.ds(pl.multiple_of(i * 8, 8), 8), :] = jnp.where(iota((8, 128), 0) < 4, left, pltpu.roll(right, 4, 0))
        for k, part in enumerate((left[4:5], left[5:6], right[4:5], right[5:6])):
            wide[pl.ds(CODES + i * 4 + k, 1), :] = part
        note = jnp.where(lane == 0, tile_ref[i], jnp.where(lane == 1, cell_ref[i], 0)).astype(F32)
        note = jnp.where(lane == 2, moved[6:7, 127:128], jnp.where(lane == 3, moved[6:7, 128:129], note))
        meta[at, :] = note
        return carry

    lax.fori_loop(0, NB_DEV, one_block, 0, unroll=8)
    turned = dot_nt(ones_where(iota((16, 128), 0) == iota((16, 128), 1)), meta[...].astype(BF16))
    out_ref[:NOTES, :] = wide[...].astype(BF16)
    out_ref[NOTES:, :] = turned.astype(BF16)


AGR = 208
CODES = 128
NOTES = 192
PARTS = ((0, 32, 32), (64, 32, 32), (128, 48, 32))
ORDERS = (("x", "y", "z"), ("y", "z", "x"), ("z", "x", "y"))


def gather_kernel(x_ref, all_ref, send, recv, local):
    au, vert = lax.axis_index("au"), lax.axis_index("vert")
    here = {"y": au // 4, "z": au % 4, "x": vert // 2}
    core = vert % 2

    def device(at, core):
        return (at["y"] * 4 + at["z"], at["x"] * 2 + core)

    def moved(dim, step):
        return {**here, dim: (here[dim] + step) % 4}

    sibling = device(here, 1 - core)
    barrier = pltpu.get_barrier_semaphore()
    for other in [device(moved(d, step), core) for d in "xyz" for step in (1, 2, 3)] + [sibling]:
        pl.semaphore_signal(barrier, inc=1, device_id=other, device_id_type=pl.DeviceIdType.MESH)
    own = pltpu.make_async_copy(x_ref, all_ref.at[here["y"], here["z"], here["x"], core], local)
    own.start()
    own.wait()
    pl.semaphore_wait(barrier, 10)

    def region(part, full, at, rows=None):
        first, one, two = PARTS[part]
        start, size = {None: (first, one + two), 0: (first, one), 1: (first + one, two)}[rows]
        index = [slice(None) if d in full else at[d] for d in "yzx"]
        return all_ref.at[(*index, core, pl.ds(start, size), slice(None))]

    used = [0]
    started = []

    def copy(ref, to):
        n = used[0]
        used[0] += 1
        made = pltpu.make_async_remote_copy(
            src_ref=ref, dst_ref=ref, send_sem=send.at[n], recv_sem=recv.at[n],
            device_id=to, device_id_type=pl.DeviceIdType.MESH,
        )
        made.start()
        started.append(made)
        return made

    shared = []
    for phase in range(2):
        direct = []
        for part, order in enumerate(ORDERS):
            ref = region(part, order[:phase], here)
            direct += [copy(ref, device(moved(order[phase], step), core)) for step in (2, 1, 3)]
        for made in direct:
            made.wait_recv()
    for phase in (2,):
        plain, relayed = [], []
        for part, order in enumerate(ORDERS):
            full, dim = order[:phase], order[phase]
            ref = region(part, full, here)
            right = copy(ref, device(moved(dim, 1), core))
            left = copy(ref, device(moved(dim, 3), core))
            plain.append((right, left))
        if phase == 2:
            for part, order in enumerate(ORDERS):
                shared.append(copy(region(part, order[:2], here), sibling))
        for part, order in enumerate(ORDERS):
            full, dim = order[:phase], order[phase]
            right, left = plain[part]
            right.wait_recv()
            one = copy(region(part, full, moved(dim, 3), 0), device(moved(dim, 1), core))
            if phase == 2:
                shared.append(copy(region(part, full, moved(dim, 3)), sibling))
            left.wait_recv()
            two = copy(region(part, full, moved(dim, 1), 1), device(moved(dim, 3), core))
            if phase == 2:
                shared.append(copy(region(part, full, moved(dim, 1)), sibling))
            relayed.append((one, two))
        for part, order in enumerate(ORDERS):
            full, dim = order[:phase], order[phase]
            for half, made in enumerate(relayed[part]):
                made.wait_recv()
                if phase == 2:
                    shared.append(copy(region(part, full, moved(dim, 2), half), sibling))
    for made in shared:
        made.wait_recv()
    for made in started:
        made.wait_send()


COPIES = 3 * (3 + 3 + 4 + 5)


def gathered(ordered):
    anywhere = pl.BlockSpec(memory_space=pl.ANY)
    return pl.pallas_call(
        gather_kernel,
        out_shape=jax.ShapeDtypeStruct((4, 4, 4, 2, AGR, 128), BF16),
        in_specs=[anywhere],
        out_specs=anywhere,
        scratch_shapes=[
            pltpu.SemaphoreType.DMA((COPIES,)), pltpu.SemaphoreType.DMA((COPIES,)), pltpu.SemaphoreType.DMA
        ],
        compiler_params=pltpu.CompilerParams(collective_id=0, has_side_effects=True),
        name="gather_blocks",
    )(ordered)


def pick(halves, index, low):
    first, second = [jnp.take_along_axis(half, index, axis=0, mode="promise_in_bounds") for half in halves]
    return jnp.where(low, first, second)


def placed(sources, taps, limit):
    halves = [(source[:8], source[8:]) for source in sources]
    parts = [[] for _ in sources]
    for t in taps:
        inside = (t & -16) == 0 if limit is None else (t >= 0) & (t < limit)
        low = t < 8
        index = t & 7
        for out, pair in zip(parts, halves):
            out.append(jnp.where(inside, pick(pair, index, low), 0.0))
    return [jnp.concatenate(part, axis=0) for part in parts]


def grid_kernel(
    words0, words1, words2, meta, bits, strip, x_all, first_all, taps_ref, second_ref, turn_ref,
    out_ref, acc, mid, stage, acc4, extra, x_ref, first_ref, spread, items, sems,
):
    words = (words0, words1, words2)
    s = strip[0]
    fetch_x = pltpu.make_async_copy(x_all, x_ref, sems.at[0])
    fetch_x.start()
    fetch_first = pltpu.make_async_copy(first_all, first_ref, sems.at[1])
    acc[0] = jnp.zeros(acc.shape[1:], F32)

    @pl.when(s == 0)
    def _():
        acc[1] = jnp.zeros(acc.shape[1:], F32)

    table = taps_ref[...]
    table_hi = table.astype(BF16)
    table_lo = (table - table_hi.astype(F32)).astype(BF16)
    both_tables = jnp.concatenate([table_hi, table_lo], axis=0)

    def listed(kind, count, groups=128):
        def group(g, n):
            def step(state):
                word, n = state
                low = word & -word
                bit = bits[lax.shift_right_logical(low * BIT_MUL, 27)]
                items[n] = (kind << 12) | ((g * NB_DEV + (bit & 15)) << 1) | (bit >> 4)
                return word ^ low, n + 1

            return lax.while_loop(lambda state: state[0] != 0, step, (words[kind][g], n))[1]

        return lax.fori_loop(0, groups, group, count)

    def place_of(code):
        block = (code >> 1) & (BLOCKS - 1)
        where = meta[block]
        cell = (where >> 14) & 31
        anchor_row = (where >> 19) * TILE_R + (cell >> 3) * 128
        return anchor_row, ((block >> 4) & 7) * TILE_C + (cell & 7) * 128

    def values_of(code):
        half, block = code & 1, (code >> 1) & (BLOCKS - 1)
        owner, own = block >> 4, block & 15
        x = x_ref[owner, pl.ds(pl.multiple_of((own >> 1) * 16, 16), 16), :].astype(F32)
        x = jnp.where((own & 1) == 1, x[8:], x[:8])
        x = jnp.where(half == 1, pltpu.roll(x, 4, 0), x)
        packed = x_ref[owner, pl.ds(pl.multiple_of(CODES + (own >> 2) * 16, 16), 16), :].astype(F32)
        packed = jnp.where((own & 2) == 2, packed[8:], packed[:8])
        packed = jnp.where((own & 1) == 1, pltpu.roll(packed, 4, 0), packed)
        packed = jnp.where(half == 1, pltpu.roll(packed, 6, 0), packed).astype(I32)
        first, second = packed[:1], packed[1:2]
        power = sum([(first >= (128 << n)).astype(I32) for n in range(1, 8)])
        power2 = sum([(second >= (128 << n)).astype(I32) for n in range(1, 4)])
        return x, (first >> power) - 128, (second >> power2) - 128, power * 4 + power2

    def factors_of(x, wplane, flip):
        chosen = ones_where(iota((32, 128), 0) == wplane)
        taps = dot(both_tables, chosen)
        tap_re, tap_im = taps[:16], taps[16:32]
        full_re, full_im = tap_re + taps[32:48], tap_im + taps[48:64]
        weights_re, weights_im = [], []
        for p in range(2):
            re, im = x[2 * p : 2 * p + 1], x[2 * p + 1 : 2 * p + 2]
            weights_re.append((re * full_re - im * full_im).astype(BF16).astype(F32))
            weights_im.append((re * full_im + im * full_re).astype(BF16).astype(F32))
        return weights_re + [im * flip for im in weights_im] + [tap_re, tap_im * flip]

    def limit_of(col, anchor_col):
        return jnp.minimum(jnp.where(anchor_col == GRID - 128, 128, 1000) - col, TAPS)

    def item(code, valid, slot):
        anchor_row, anchor_col = place_of(code)
        base_at = pl.multiple_of(slot * 104, 8)
        where = spread[pl.ds(base_at + 96, 8), :].astype(I32)
        row, col = where[:1], where[1:2]
        limit = limit_of(col, anchor_col)
        factors = [spread[pl.ds(base_at + 16 * i, 16), :] for i in range(6)]
        weights, taps = factors[:4], factors[4:]
        kind = code >> 12
        mirror, middle = kind == 1, kind == 2
        sign = jnp.where(mirror, -1, 1)
        base = jnp.where(middle, GRID // 2, jnp.where(mirror, GRID - s * ROWS, s * ROWS)) - anchor_row
        base = jnp.where(valid, base, -100000)
        least = jnp.where(mirror & (s == 0), 1, 0)
        most = jnp.where(middle, 0, ROWS)
        step = 8 * sign
        j = iota((8, 128), 0)
        ahead = jnp.where(mirror, -j, j)
        tap = ahead + base - row
        beyond = jnp.where(middle, -100000, 0)
        tiles = [jnp.where((j < least) | (j > most), -1, tap)]
        tiles += [tap + (step * i + beyond) for i in range(1, ROWS // 8)]
        re0, re1, im0, im1 = placed(weights, tiles, None)
        left = jnp.concatenate([re0, re1, im0, im1], axis=0).astype(BF16)
        right = jnp.concatenate([-im0, -im1, re0, re1], axis=0).astype(BF16)
        tap = ahead + jnp.where(mirror, 144, 0) - col
        col_re, col_im = placed(taps, [tap + step * i for i in range(WINDOW // 8)], limit)
        cols = jnp.concatenate([col_re.astype(BF16), col_im.astype(BF16)], axis=1)
        patch = dot_nt(cols, jnp.concatenate([left, right], axis=1))
        start = jnp.where(mirror, GRID - 128 - anchor_col, anchor_col + HEAD)
        return middle.astype(I32), pl.multiple_of(start, 16), patch

    count = listed(2, listed(1, listed(0, 0)), jnp.where(s == 0, 128, 0))
    fetch_x.wait()
    fetch_first.start()

    def batch(i, carry):
        first_item = i * BATCH
        rounds = (jnp.minimum(count - first_item, BATCH) + UNROLL - 1) // UNROLL

        def code_at(n):
            valid = n < count
            return jnp.where(valid, items[n], 0), valid

        def prepare(r, carry):
            for k in range(UNROLL):
                slot = r * UNROLL + k
                code = code_at(first_item + slot)[0]
                x, row, col, wplane = values_of(code)
                flip = jnp.where((code >> 12) == 1, -1.0, 1.0)
                base_at = pl.multiple_of(slot * 104, 8)
                for f, factor in enumerate(factors_of(x, wplane, flip)):
                    spread[pl.ds(base_at + f * 16, 16), :] = factor
                spread[pl.ds(base_at + 96, 8), :] = jnp.where(iota((8, 128), 0) == 0, row, col).astype(F32)
            return carry

        lax.fori_loop(0, rounds, prepare, 0)

        def several(r, carry):
            found = []
            for k in range(UNROLL):
                slot = r * UNROLL + k
                found.append(item(*code_at(first_item + slot), slot))
            for target, start, patch in found:
                acc[target, pl.ds(start, WINDOW), :] += patch
            return carry

        lax.fori_loop(0, rounds, several, 0)
        return carry

    lax.fori_loop(0, (count + BATCH - 1) // BATCH, batch, 0)
    acc[0, HEAD : HEAD + 8, :] += jnp.where(iota((8, 128), 0) == 0, acc[0, HEAD + GRID : HEAD + GRID + 8, :], 0.0)

    lane = iota((1, 128), 1)
    flip = jnp.where(lane < 64, -1.0, 1.0)

    fetch_first.wait()

    @pl.when(s == 0)
    def _():
        picked = ones_where(iota((8, 128), 1) == 32 * iota((8, 128), 0))

        def turn_block(c1, carry):
            block = acc[1, pl.ds(pl.multiple_of(HEAD + c1 * 128, 16), 128), :].astype(BF16)
            acc4[pl.ds(pl.multiple_of(c1 * 8, 8), 8), :] = dot_nt(picked, block)
            return carry

        lax.fori_loop(0, 64, turn_block, 0, unroll=8)
        cosine = first_ref[0, :64, :64]
        sine = first_ref[0, 64:, :64]
        turn_cos, turn_sin = turn_ref[:64], turn_ref[64:]
        for p in range(2):
            re = acc4[pl.ds(p, 64, stride=8), :].astype(BF16)
            im = acc4[pl.ds(2 + p, 64, stride=8), :].astype(BF16)
            mid_re = dot(cosine, re) - dot(sine, im)
            mid_im = dot(cosine, im) + dot(sine, re)
            turned_re = (mid_re * turn_cos - mid_im * turn_sin).astype(BF16)
            turned_im = (mid_re * turn_sin + mid_im * turn_cos).astype(BF16)
            extra[p] = dot(turned_re, second_ref[:128, :128]) - dot(turned_im, second_ref[:128, 128:])

    def column_first(c0, carry):
        h = acc[0, pl.ds(HEAD + c0, 64, stride=128), :]
        high = h.astype(BF16)
        low = (h - high.astype(F32)).astype(BF16)
        factors = first_ref[c0]
        got = dot(
            jnp.concatenate([factors, factors], axis=1), jnp.concatenate([high, high, low, low], axis=0)
        )
        y = got[:64] + flip * pltpu.roll(got[64:], 64, 1)
        mid[pl.ds(pl.multiple_of(c0 * 64, 64), 64), :] = y
        return carry

    lax.fori_loop(0, 128, column_first, 0, unroll=16)

    spots = ones_where(iota((256, 128), 1) == 64 + 32 * (iota((256, 128), 0) // 128))
    second_hi = second_ref[:128]
    second_lo = second_ref[128:]

    for group in range(4):

        def column_second(v, carry):
            v0 = group * 16 + v
            y = mid[pl.ds(v0, 128, stride=64), :]
            turned = flip * pltpu.roll(y, 64, 1)
            pair = jnp.concatenate([y.astype(BF16), turned.astype(BF16)], axis=0)
            z = dot(second_hi, pair) + dot(second_lo, pair)
            stage[pl.ds(v, 128, stride=16), :] = z
            return carry

        lax.fori_loop(0, 16, column_second, 0, unroll=16)

        def pack(d, carry):
            out_ref[d, group * 16 : group * 16 + 16, :] = stage[
                pl.ds(pl.multiple_of(d * 16, 16), 16), :
            ].astype(BF16)
            return carry

        def pack_middle(d8, carry):
            ahead = [extra[p, group * 16 : group * 16 + 16, :] for p in range(2)]
            parts = []
            for k in range(8):
                mine = iota((16, 128), 1) == d8 * 8 + k
                parts.append(jnp.concatenate([jnp.where(mine, z, 0.0) for z in ahead], axis=1))
            more = dot(jnp.concatenate(parts, axis=0).astype(BF16), spots)
            z = stage[pl.ds(pl.multiple_of(d8 * 128, 128), 128), :]
            z = jnp.where((lane == 64) | (lane == 96), more, z).astype(BF16)
            for k in range(8):
                out_ref[d8 * 8 + k, group * 16 : group * 16 + 16, :] = z[16 * k : 16 * k + 16]
            return carry

        @pl.when(s != 0)
        def _():
            lax.fori_loop(0, 128, pack, 0, unroll=8)

        @pl.when(s == 0)
        def _():
            lax.fori_loop(0, 16, pack_middle, 0, unroll=8)


def image_kernel(in_ref, first_ref, turn_ref, last_ref, out_ref, wide, left, right):
    def widen(s, carry):
        wide[pl.ds(pl.multiple_of(s * 16, 16), 16), :] = in_ref[s].astype(F32)
        return carry

    lax.fori_loop(0, DEVICES, widen, 0, unroll=8)
    flip = jnp.where(iota((1, 128), 1) < 64, -1.0, 1.0)
    first = first_ref[...]
    last = last_ref[...]

    def one(v, carry):
        y = wide[pl.ds(v, DEVICES, stride=16), :]
        rolled = pltpu.roll(y, 64, 1)
        pair = jnp.concatenate([y.astype(BF16), (flip * rolled).astype(BF16)], axis=0)
        got = dot(first, pair) + turn_ref[2] * rolled[:1]
        turned = (got * turn_ref[0] + pltpu.roll(got, 64, 1) * turn_ref[1]).astype(BF16)
        result = dot_nt(last, jnp.concatenate([turned, turned], axis=1))
        left[pl.ds(pl.multiple_of(v * 64, 64), 64), :] = result[:, :128]
        right[pl.ds(pl.multiple_of(v * 64, 64), 64), :] = result[:, 128:]
        return carry

    lax.fori_loop(0, 16, one, 0, unroll=16)

    def place(u1, carry):
        for p in range(2):
            for half in range(2):
                for side, ref in ((0, left), (1, right)):
                    out_ref[p, half * 8 : half * 8 + 8, pl.ds(pl.multiple_of(u1 * 256 + side * 128, 128), 128)] = (
                        ref[pl.ds(half * 512 + p * 32 + u1, 8, stride=64), :]
                    )
        return carry

    lax.fori_loop(0, 32, place, 0, unroll=4)


def words_of(code, s):
    row = (code >> 19) * TILE_R + ((code >> 17) & 3) * 128
    top, bottom = (code >> 7) & 127, code & 127
    shift = jnp.arange(NB_DEV, dtype=I32)[None, :]

    def packed(first, final):
        hit = (final >= 0) & (first < 128 + TAPS - 1)
        one = (hit & (top >= first - (TAPS - 1))).astype(I32)
        two = (hit & (bottom <= final)).astype(I32)
        both = one << shift | two << (shift + 16)
        return jnp.sum(both, axis=1)

    direct = s * ROWS - row
    mirror = GRID - ROWS + 1 - s * ROWS - row
    middle = GRID // 2 - row
    middle = packed(middle, middle) * (s == 0).astype(I32)
    return packed(direct, direct + ROWS - 1), packed(mirror, mirror + ROWS - 1), middle


def gridded(words, codes_all, s, x_all, taps):
    vmem = pl.BlockSpec(memory_space=pltpu.VMEM)
    smem = pl.BlockSpec(memory_space=pltpu.SMEM)
    first, second, turn = column_tables()
    return pl.pallas_call(
        grid_kernel,
        out_shape=jax.ShapeDtypeStruct((DEVICES, 64, 128), BF16),
        in_specs=[smem] * 6 + [pl.BlockSpec(memory_space=pl.ANY)] * 2 + [vmem] * 3,
        out_specs=vmem,
        scratch_shapes=[
            pltpu.VMEM((2, HEAD + GRID + 32, 128), F32),
            pltpu.VMEM((128 * 64, 128), F32),
            pltpu.VMEM((DEVICES * 16, 128), F32),
            pltpu.VMEM((64 * 8, 128), F32),
            pltpu.VMEM((2, 64, 128), F32),
            pltpu.VMEM((DEVICES, AGR, 128), BF16),
            pltpu.VMEM((128, 128, 128), BF16),
            pltpu.VMEM((BATCH * 104, 128), F32),
            pltpu.SMEM((4096,), I32),
            pltpu.SemaphoreType.DMA((2,)),
        ],
        compiler_params=pltpu.CompilerParams(vmem_limit_bytes=60 * 1024 * 1024),
        name="grid_columns",
    )(
        *words, codes_all.reshape(BLOCKS), jnp.asarray(bit_table()), s.reshape(1).astype(I32),
        x_all, jnp.asarray(first), taps, jnp.asarray(second), jnp.asarray(turn),
    )


def imaged(got):
    first, turn, last = row_tables()
    return pl.pallas_call(
        image_kernel,
        out_shape=jax.ShapeDtypeStruct((2, 64, GRID), F32),
        grid=(4,),
        in_specs=[
            pl.BlockSpec((DEVICES, 16, 128), lambda i: (0, i, 0)),
            pl.BlockSpec((256, 256), lambda i: (0, 0)),
            pl.BlockSpec((3, 256, 128), lambda i: (0, 0, 0)),
            pl.BlockSpec((64, 256), lambda i: (0, 0)),
        ],
        out_specs=pl.BlockSpec((2, 16, GRID), lambda i: (0, i, 0)),
        scratch_shapes=[
            pltpu.VMEM((DEVICES * 16, 128), F32),
            pltpu.VMEM((16 * 64, 128), F32),
            pltpu.VMEM((16 * 64, 128), F32),
        ],
        compiler_params=pltpu.CompilerParams(vmem_limit_bytes=48 * 1024 * 1024),
        name="image_rows",
    )(got, jnp.asarray(first), jnp.asarray(turn), jnp.asarray(last))


def sorted_blocks(visibilities, keep_flags, kernel_index, row_offset, col_offset, cell_index, tile_row):
    vmem = pl.BlockSpec(memory_space=pltpu.VMEM)
    smem = pl.BlockSpec(memory_space=pltpu.SMEM)
    return pl.pallas_call(
        sort_kernel,
        out_shape=jax.ShapeDtypeStruct((AGR, 128), BF16),
        in_specs=[vmem] * 5 + [smem] * 2,
        out_specs=vmem,
        scratch_shapes=[pltpu.VMEM((128, 128), F32), pltpu.VMEM((NOTES, 128), F32)],
        name="sort_blocks",
    )(visibilities, keep_flags, kernel_index, row_offset, col_offset, cell_index, tile_row)


def shards(visibilities, keep_flags, kernel_index, row_offset, col_offset, cell_index, tile_row, kernel_taps):
    s = lax.axis_index("au") * 8 + lax.axis_index("vert")
    ordered = sorted_blocks(
        visibilities, keep_flags, kernel_index, row_offset, col_offset, cell_index, tile_row.reshape(NB_DEV)
    )
    x_all = gathered(ordered).reshape(DEVICES, AGR, 128)
    found = x_all[:, NOTES : NOTES + 4, :NB_DEV].astype(I32)
    codes_all = ((found[:, 0] * 32 + found[:, 1]) << 14) | (found[:, 2] << 7) | found[:, 3]
    words = words_of(codes_all, s)
    taps = kernel_taps.transpose(1, 2, 0).reshape(2 * TAPS, 32)
    sent = gridded(words, codes_all, s, x_all, taps)
    got = lax.all_to_all(sent, BOTH, split_axis=0, concat_axis=0, tiled=True)
    return imaged(got)


def solution(mesh):
    in_specs = (
        P(BOTH, None, None, None),
        P(BOTH, None),
        P(BOTH, None),
        P(BOTH, None),
        P(BOTH, None),
        P(BOTH),
        P(BOTH, None),
        P(),
    )
    out_specs = P(None, BOTH, None)
    return jax.shard_map(shards, mesh=mesh, in_specs=in_specs, out_specs=out_specs, check_vma=False)
```

```python
import functools
import math

import jax
import jax.numpy as jnp
import numpy as np
from jax import lax
from jax.experimental import pallas as pl
from jax.experimental.pallas import tpu as pltpu
from jax.sharding import PartitionSpec as P

KVIS = 256
TAPS = 16
TILE_R = 512
TILE_C = 1024
NB_DEV = 16
BLOCKS = 2048
GRID = 8192
DEVICES = 128
ROWS = 32
HEAD = 16
WINDOW = 152
UNROLL = 16
BATCH = 64
BOTH = ("au", "vert")
F32 = jnp.float32
BF16 = jnp.bfloat16
I32 = jnp.int32
NT = (((1,), (1,)), ((), ()))
BIT_MUL = 0x077CB531


def bit_table():
    table = np.zeros(32, np.int32)
    for bit in range(32):
        table[((BIT_MUL << bit) & 0xFFFFFFFF) >> 27] = bit
    return table


def hi_lo(values):
    high = values.astype(jnp.bfloat16)
    low = (values - high.astype(np.float64)).astype(jnp.bfloat16)
    return high, low


@functools.lru_cache(None)
def column_tables():
    v0, c1 = np.arange(64), np.arange(64)
    c0 = np.arange(128)
    angle = 2 * np.pi / GRID * ((v0[None, :, None] * (128 * c1[None, None, :] + c0[:, None, None])) % GRID)
    first = np.concatenate([np.cos(angle), np.sin(angle)], axis=1)
    first = np.concatenate(hi_lo(first), axis=2)
    angle = 2 * np.pi / 128 * ((c0[:, None] * c0[None, :]) % 128)
    second = np.concatenate(hi_lo(np.concatenate([np.cos(angle), np.sin(angle)], axis=1)), axis=0)
    angle = 2 * np.pi / GRID * (v0[:, None] * c0[None, :])
    turn = np.concatenate([np.cos(angle), np.sin(angle)], axis=0).astype(np.float32)
    return first, second, turn


@functools.lru_cache(None)
def row_tables():
    scale = 1.0 / math.sqrt(BLOCKS * KVIS)
    u0, s = np.arange(256), np.arange(128)
    angle = 2 * np.pi / 256 * ((u0[:, None] * s[None, :]) % 256)
    first = np.concatenate([np.cos(angle), np.sin(angle)], axis=1).astype(jnp.bfloat16)
    comp, j = np.arange(128) // 64, np.arange(128) % 32
    plane = np.arange(128) // 32 % 2
    angle = 2 * np.pi / GRID * (u0[:, None] * j[None, :])
    turn_cos = (np.cos(angle) * scale).astype(np.float32)
    turn_sin = (np.sin(angle) * np.where(comp == 0, -1.0, 1.0) * scale).astype(np.float32)
    alternate = ((1.0 - 2.0 * (u0 % 2))[:, None] * ((comp == 0) & (j == 0))[None, :]).astype(np.float32)
    u1 = np.arange(32)
    angle = 2 * np.pi / 32 * ((u1[:, None] * j[None, :]) % 32)
    last = np.where(comp == 0, np.cos(angle), -np.sin(angle))
    last = np.concatenate([last * (plane == p) for p in range(2)], axis=0)
    last = np.concatenate(hi_lo(last), axis=1)
    return first, np.stack([turn_cos, turn_sin, alternate]), last


def iota(shape, dim):
    return lax.broadcasted_iota(I32, shape, dim)


def ones_where(mask):
    return jnp.where(mask, 1.0, 0.0).astype(BF16)


def dot(a, b):
    return jnp.dot(a, b, preferred_element_type=F32)


def dot_nt(a, b):
    return lax.dot_general(a, b, NT, preferred_element_type=F32)


def sort_kernel(vis_ref, keep_ref, plane_ref, row_ref, col_ref, cell_ref, tile_ref, out_ref, meta, wide):
    below = ones_where(iota((128, 128), 1) < iota((128, 128), 0))
    before = ones_where(iota((KVIS, KVIS), 0) < iota((KVIS, KVIS), 1))
    ones = jnp.ones((KVIS, KVIS), BF16)
    value = iota((128, KVIS), 0)
    place = iota((KVIS, KVIS), 0)
    slot = iota((8, KVIS), 0)
    lane = iota((1, 128), 1)

    meta[...] = jnp.zeros_like(meta)

    def one_block(i, carry):
        at = pl.ds(i, 1)
        row = row_ref[at, :]
        keep = keep_ref[at, :] == 1
        wplane = plane_ref[at, :]
        first = (128 + row) << (wplane >> 2)
        second = (128 + col_ref[at, :]) << (wplane & 3)
        x = jnp.where(slot == 4, first, jnp.where(slot == 5, second, jnp.where(slot == 6, row, 0)))
        x = x.astype(F32)
        for p in range(2):
            pair = vis_ref[i, p].astype(F32)
            for c in range(2):
                x = jnp.where((slot == 2 * p + c) & keep, pair[c : c + 1], x)
        x = x.astype(BF16)
        hit = value == row
        hot = ones_where(hit)
        rank = dot(hot, before) + dot(dot(below, hot).astype(BF16), ones)
        rank = jnp.sum(jnp.where(hit, rank, 0.0), axis=0, keepdims=True)
        moved = dot_nt(x, ones_where(place == rank.astype(I32)))
        left, right = moved[:, :128], moved[:, 128:]
        wide[pl.ds(pl.multiple_of(i * 8, 8), 8), :] = jnp.where(iota((8, 128), 0) < 4, left, pltpu.roll(right, 4, 0))
        for k, part in enumerate((left[4:5], left[5:6], right[4:5], right[5:6])):
            wide[pl.ds(CODES + i * 4 + k, 1), :] = part
        note = jnp.where(lane == 0, tile_ref[i], jnp.where(lane == 1, cell_ref[i], 0)).astype(F32)
        note = jnp.where(lane == 2, moved[6:7, 127:128], jnp.where(lane == 3, moved[6:7, 128:129], note))
        meta[at, :] = note
        return carry

    lax.fori_loop(0, NB_DEV, one_block, 0, unroll=8)
    turned = dot_nt(ones_where(iota((16, 128), 0) == iota((16, 128), 1)), meta[...].astype(BF16))
    out_ref[:NOTES, :] = wide[...].astype(BF16)
    out_ref[NOTES:, :] = turned.astype(BF16)


AGR = 208
CODES = 128
NOTES = 192
PARTS = ((0, 32, 32), (64, 32, 32), (128, 48, 32))
ORDERS = (("x", "y", "z"), ("y", "z", "x"), ("z", "x", "y"))


def gather_kernel(x_ref, all_ref, send, recv, local):
    au, vert = lax.axis_index("au"), lax.axis_index("vert")
    here = {"y": au // 4, "z": au % 4, "x": vert // 2}
    core = vert % 2

    def device(at, core):
        return (at["y"] * 4 + at["z"], at["x"] * 2 + core)

    def moved(dim, step):
        return {**here, dim: (here[dim] + step) % 4}

    sibling = device(here, 1 - core)
    barrier = pltpu.get_barrier_semaphore()
    for other in [device(moved(d, step), core) for d in "xyz" for step in (1, 2, 3)] + [sibling]:
        pl.semaphore_signal(barrier, inc=1, device_id=other, device_id_type=pl.DeviceIdType.MESH)
    own = pltpu.make_async_copy(x_ref, all_ref.at[here["y"], here["z"], here["x"], core], local)
    own.start()
    own.wait()
    pl.semaphore_wait(barrier, 10)

    def region(part, full, at, rows=None):
        first, one, two = PARTS[part]
        start, size = {None: (first, one + two), 0: (first, one), 1: (first + one, two)}[rows]
        index = [slice(None) if d in full else at[d] for d in "yzx"]
        return all_ref.at[(*index, core, pl.ds(start, size), slice(None))]

    used = [0]
    started = []

    def copy(ref, to):
        n = used[0]
        used[0] += 1
        made = pltpu.make_async_remote_copy(
            src_ref=ref, dst_ref=ref, send_sem=send.at[n], recv_sem=recv.at[n],
            device_id=to, device_id_type=pl.DeviceIdType.MESH,
        )
        made.start()
        started.append(made)
        return made

    shared = []

    def sends(part, phase):
        order = ORDERS[part]
        ref = region(part, order[:phase], here)
        return [copy(ref, device(moved(order[phase], step), core)) for step in (2, 1, 3)]

    before = [sends(part, 0) for part in range(3)]
    after = []
    for part in range(3):
        for made in before[part]:
            made.wait_recv()
        after.append(sends(part, 1))
    for phase in (2,):
        plain, relayed = [], []
        for part, order in enumerate(ORDERS):
            full, dim = order[:phase], order[phase]
            for made in after[part]:
                made.wait_recv()
            ref = region(part, full, here)
            right = copy(ref, device(moved(dim, 1), core))
            left = copy(ref, device(moved(dim, 3), core))
            plain.append((right, left))
            shared.append(copy(ref, sibling))
        for part, order in enumerate(ORDERS):
            full, dim = order[:phase], order[phase]
            right, left = plain[part]
            right.wait_recv()
            one = copy(region(part, full, moved(dim, 3), 0), device(moved(dim, 1), core))
            if phase == 2:
                shared.append(copy(region(part, full, moved(dim, 3)), sibling))
            left.wait_recv()
            two = copy(region(part, full, moved(dim, 1), 1), device(moved(dim, 3), core))
            if phase == 2:
                shared.append(copy(region(part, full, moved(dim, 1)), sibling))
            relayed.append((one, two))
        for part, order in enumerate(ORDERS):
            full, dim = order[:phase], order[phase]
            for half, made in enumerate(relayed[part]):
                made.wait_recv()
                if phase == 2:
                    shared.append(copy(region(part, full, moved(dim, 2), half), sibling))
    for made in shared:
        made.wait_recv()
    for made in started:
        made.wait_send()


COPIES = 3 * (3 + 3 + 4 + 5)


def gathered(ordered):
    anywhere = pl.BlockSpec(memory_space=pl.ANY)
    return pl.pallas_call(
        gather_kernel,
        out_shape=jax.ShapeDtypeStruct((4, 4, 4, 2, AGR, 128), BF16),
        in_specs=[anywhere],
        out_specs=anywhere,
        scratch_shapes=[
            pltpu.SemaphoreType.DMA((COPIES,)), pltpu.SemaphoreType.DMA((COPIES,)), pltpu.SemaphoreType.DMA
        ],
        compiler_params=pltpu.CompilerParams(collective_id=0, has_side_effects=True),
        name="gather_blocks",
    )(ordered)


def pick(halves, index, low):
    first, second = [jnp.take_along_axis(half, index, axis=0, mode="promise_in_bounds") for half in halves]
    return jnp.where(low, first, second)


def placed(sources, taps, limit):
    halves = [(source[:8], source[8:]) for source in sources]
    parts = [[] for _ in sources]
    for t in taps:
        inside = (t & -16) == 0 if limit is None else (t >= 0) & (t < limit)
        low = t < 8
        index = t & 7
        for out, pair in zip(parts, halves):
            out.append(jnp.where(inside, pick(pair, index, low), 0.0))
    return [jnp.concatenate(part, axis=0) for part in parts]


def grid_kernel(
    words0, words1, words2, meta, bits, strip, x_all, first_all, taps_ref, second_ref, turn_ref,
    out_ref, acc, mid, stage, acc4, extra, x_ref, first_ref, spread, items, sems,
):
    words = (words0, words1, words2)
    s = strip[0]
    fetch_x = pltpu.make_async_copy(x_all, x_ref, sems.at[0])
    fetch_x.start()
    fetch_first = pltpu.make_async_copy(first_all, first_ref, sems.at[1])
    acc[0] = jnp.zeros(acc.shape[1:], F32)

    @pl.when(s == 0)
    def _():
        acc[1] = jnp.zeros(acc.shape[1:], F32)

    table = taps_ref[...]
    table_hi = table.astype(BF16)
    table_lo = (table - table_hi.astype(F32)).astype(BF16)
    both_tables = jnp.concatenate([table_hi, table_lo], axis=0)

    def listed(kind, count, groups=128):
        def group(g, n):
            def step(state):
                word, n = state
                low = word & -word
                bit = bits[lax.shift_right_logical(low * BIT_MUL, 27)]
                items[n] = (kind << 12) | ((g * NB_DEV + (bit & 15)) << 1) | (bit >> 4)
                return word ^ low, n + 1

            return lax.while_loop(lambda state: state[0] != 0, step, (words[kind][g], n))[1]

        return lax.fori_loop(0, groups, group, count)

    def place_of(code):
        block = (code >> 1) & (BLOCKS - 1)
        where = meta[block]
        cell = (where >> 14) & 31
        anchor_row = (where >> 19) * TILE_R + (cell >> 3) * 128
        return anchor_row, ((block >> 4) & 7) * TILE_C + (cell & 7) * 128

    def values_of(code):
        half, block = code & 1, (code >> 1) & (BLOCKS - 1)
        owner, own = block >> 4, block & 15
        x = x_ref[owner, pl.ds(pl.multiple_of((own >> 1) * 16, 16), 16), :].astype(F32)
        x = jnp.where((own & 1) == 1, x[8:], x[:8])
        x = jnp.where(half == 1, pltpu.roll(x, 4, 0), x)
        packed = x_ref[owner, pl.ds(pl.multiple_of(CODES + (own >> 2) * 16, 16), 16), :].astype(F32)
        packed = jnp.where((own & 2) == 2, packed[8:], packed[:8])
        packed = jnp.where((own & 1) == 1, pltpu.roll(packed, 4, 0), packed)
        packed = jnp.where(half == 1, pltpu.roll(packed, 6, 0), packed).astype(I32)
        first, second = packed[:1], packed[1:2]
        power = sum([(first >= (128 << n)).astype(I32) for n in range(1, 8)])
        power2 = sum([(second >= (128 << n)).astype(I32) for n in range(1, 4)])
        return x, (first >> power) - 128, (second >> power2) - 128, power * 4 + power2

    def factors_of(x, wplane, flip):
        chosen = ones_where(iota((32, 128), 0) == wplane)
        taps = dot(both_tables, chosen)
        tap_re, tap_im = taps[:16], taps[16:32]
        full_re, full_im = tap_re + taps[32:48], tap_im + taps[48:64]
        weights_re, weights_im = [], []
        for p in range(2):
            re, im = x[2 * p : 2 * p + 1], x[2 * p + 1 : 2 * p + 2]
            weights_re.append((re * full_re - im * full_im).astype(BF16).astype(F32))
            weights_im.append((re * full_im + im * full_re).astype(BF16).astype(F32))
        return weights_re + [im * flip for im in weights_im] + [tap_re, tap_im * flip]

    def limit_of(col, anchor_col):
        return jnp.minimum(jnp.where(anchor_col == GRID - 128, 128, 1000) - col, TAPS)

    def item(code, valid, slot):
        anchor_row, anchor_col = place_of(code)
        base_at = pl.multiple_of(slot * 104, 8)
        where = spread[pl.ds(base_at + 96, 8), :].astype(I32)
        row, col = where[:1], where[1:2]
        limit = limit_of(col, anchor_col)
        factors = [spread[pl.ds(base_at + 16 * i, 16), :] for i in range(6)]
        weights, taps = factors[:4], factors[4:]
        kind = code >> 12
        mirror, middle = kind == 1, kind == 2
        sign = jnp.where(mirror, -1, 1)
        base = jnp.where(middle, GRID // 2, jnp.where(mirror, GRID - s * ROWS, s * ROWS)) - anchor_row
        base = jnp.where(valid, base, -100000)
        least = jnp.where(mirror & (s == 0), 1, 0)
        most = jnp.where(middle, 0, ROWS)
        step = 8 * sign
        j = iota((8, 128), 0)
        ahead = jnp.where(mirror, -j, j)
        tap = ahead + base - row
        beyond = jnp.where(middle, -100000, 0)
        tiles = [jnp.where((j < least) | (j > most), -1, tap)]
        tiles += [tap + (step * i + beyond) for i in range(1, ROWS // 8)]
        re0, re1, im0, im1 = placed(weights, tiles, None)
        left = jnp.concatenate([re0, re1, im0, im1], axis=0).astype(BF16)
        right = jnp.concatenate([-im0, -im1, re0, re1], axis=0).astype(BF16)
        tap = ahead + jnp.where(mirror, 144, 0) - col
        col_re, col_im = placed(taps, [tap + step * i for i in range(WINDOW // 8)], limit)
        cols = jnp.concatenate([col_re.astype(BF16), col_im.astype(BF16)], axis=1)
        patch = dot_nt(cols, jnp.concatenate([left, right], axis=1))
        start = jnp.where(mirror, GRID - 128 - anchor_col, anchor_col + HEAD)
        return middle.astype(I32), pl.multiple_of(start, 16), patch

    count = listed(2, listed(1, listed(0, 0)), jnp.where(s == 0, 128, 0))
    fetch_x.wait()
    fetch_first.start()

    def batch(i, carry):
        first_item = i * BATCH
        rounds = (jnp.minimum(count - first_item, BATCH) + UNROLL - 1) // UNROLL

        def code_at(n):
            valid = n < count
            return jnp.where(valid, items[n], 0), valid

        def prepare(r, carry):
            for k in range(UNROLL):
                slot = r * UNROLL + k
                code = code_at(first_item + slot)[0]
                x, row, col, wplane = values_of(code)
                flip = jnp.where((code >> 12) == 1, -1.0, 1.0)
                base_at = pl.multiple_of(slot * 104, 8)
                for f, factor in enumerate(factors_of(x, wplane, flip)):
                    spread[pl.ds(base_at + f * 16, 16), :] = factor
                spread[pl.ds(base_at + 96, 8), :] = jnp.where(iota((8, 128), 0) == 0, row, col).astype(F32)
            return carry

        lax.fori_loop(0, rounds, prepare, 0)

        def several(r, carry):
            found = []
            for k in range(UNROLL):
                slot = r * UNROLL + k
                found.append(item(*code_at(first_item + slot), slot))
            for target, start, patch in found:
                acc[target, pl.ds(start, WINDOW), :] += patch
            return carry

        lax.fori_loop(0, rounds, several, 0)
        return carry

    lax.fori_loop(0, (count + BATCH - 1) // BATCH, batch, 0)
    acc[0, HEAD : HEAD + 8, :] += jnp.where(iota((8, 128), 0) == 0, acc[0, HEAD + GRID : HEAD + GRID + 8, :], 0.0)

    lane = iota((1, 128), 1)
    flip = jnp.where(lane < 64, -1.0, 1.0)

    fetch_first.wait()

    @pl.when(s == 0)
    def _():
        picked = ones_where(iota((8, 128), 1) == 32 * iota((8, 128), 0))

        def turn_block(c1, carry):
            block = acc[1, pl.ds(pl.multiple_of(HEAD + c1 * 128, 16), 128), :].astype(BF16)
            acc4[pl.ds(pl.multiple_of(c1 * 8, 8), 8), :] = dot_nt(picked, block)
            return carry

        lax.fori_loop(0, 64, turn_block, 0, unroll=8)
        cosine = first_ref[0, :64, :64]
        sine = first_ref[0, 64:, :64]
        turn_cos, turn_sin = turn_ref[:64], turn_ref[64:]
        for p in range(2):
            re = acc4[pl.ds(p, 64, stride=8), :].astype(BF16)
            im = acc4[pl.ds(2 + p, 64, stride=8), :].astype(BF16)
            mid_re = dot(cosine, re) - dot(sine, im)
            mid_im = dot(cosine, im) + dot(sine, re)
            turned_re = (mid_re * turn_cos - mid_im * turn_sin).astype(BF16)
            turned_im = (mid_re * turn_sin + mid_im * turn_cos).astype(BF16)
            extra[p] = dot(turned_re, second_ref[:128, :128]) - dot(turned_im, second_ref[:128, 128:])

    def column_first(c0, carry):
        h = acc[0, pl.ds(HEAD + c0, 64, stride=128), :]
        high = h.astype(BF16)
        low = (h - high.astype(F32)).astype(BF16)
        factors = first_ref[c0]
        got = dot(
            jnp.concatenate([factors, factors], axis=1), jnp.concatenate([high, high, low, low], axis=0)
        )
        y = got[:64] + flip * pltpu.roll(got[64:], 64, 1)
        mid[pl.ds(pl.multiple_of(c0 * 64, 64), 64), :] = y
        return carry

    lax.fori_loop(0, 128, column_first, 0, unroll=16)

    spots = ones_where(iota((256, 128), 1) == 64 + 32 * (iota((256, 128), 0) // 128))
    second_hi = second_ref[:128]
    second_lo = second_ref[128:]

    for group in range(4):

        def column_second(v, carry):
            v0 = group * 16 + v
            y = mid[pl.ds(v0, 128, stride=64), :]
            turned = flip * pltpu.roll(y, 64, 1)
            pair = jnp.concatenate([y.astype(BF16), turned.astype(BF16)], axis=0)
            z = dot(second_hi, pair) + dot(second_lo, pair)
            stage[pl.ds(v, 128, stride=16), :] = z
            return carry

        lax.fori_loop(0, 16, column_second, 0, unroll=16)

        def pack(d, carry):
            out_ref[d, group * 16 : group * 16 + 16, :] = stage[
                pl.ds(pl.multiple_of(d * 16, 16), 16), :
            ].astype(BF16)
            return carry

        def pack_middle(d8, carry):
            ahead = [extra[p, group * 16 : group * 16 + 16, :] for p in range(2)]
            parts = []
            for k in range(8):
                mine = iota((16, 128), 1) == d8 * 8 + k
                parts.append(jnp.concatenate([jnp.where(mine, z, 0.0) for z in ahead], axis=1))
            more = dot(jnp.concatenate(parts, axis=0).astype(BF16), spots)
            z = stage[pl.ds(pl.multiple_of(d8 * 128, 128), 128), :]
            z = jnp.where((lane == 64) | (lane == 96), more, z).astype(BF16)
            for k in range(8):
                out_ref[d8 * 8 + k, group * 16 : group * 16 + 16, :] = z[16 * k : 16 * k + 16]
            return carry

        @pl.when(s != 0)
        def _():
            lax.fori_loop(0, 128, pack, 0, unroll=8)

        @pl.when(s == 0)
        def _():
            lax.fori_loop(0, 16, pack_middle, 0, unroll=8)


def image_kernel(in_ref, first_ref, turn_ref, last_ref, out_ref, wide, left, right):
    def widen(s, carry):
        wide[pl.ds(pl.multiple_of(s * 16, 16), 16), :] = in_ref[s].astype(F32)
        return carry

    lax.fori_loop(0, DEVICES, widen, 0, unroll=8)
    flip = jnp.where(iota((1, 128), 1) < 64, -1.0, 1.0)
    first = first_ref[...]
    last = last_ref[...]

    def one(v, carry):
        y = wide[pl.ds(v, DEVICES, stride=16), :]
        rolled = pltpu.roll(y, 64, 1)
        pair = jnp.concatenate([y.astype(BF16), (flip * rolled).astype(BF16)], axis=0)
        got = dot(first, pair) + turn_ref[2] * rolled[:1]
        turned = (got * turn_ref[0] + pltpu.roll(got, 64, 1) * turn_ref[1]).astype(BF16)
        result = dot_nt(last, jnp.concatenate([turned, turned], axis=1))
        left[pl.ds(pl.multiple_of(v * 64, 64), 64), :] = result[:, :128]
        right[pl.ds(pl.multiple_of(v * 64, 64), 64), :] = result[:, 128:]
        return carry

    lax.fori_loop(0, 16, one, 0, unroll=16)

    def place(u1, carry):
        for p in range(2):
            for half in range(2):
                for side, ref in ((0, left), (1, right)):
                    out_ref[p, half * 8 : half * 8 + 8, pl.ds(pl.multiple_of(u1 * 256 + side * 128, 128), 128)] = (
                        ref[pl.ds(half * 512 + p * 32 + u1, 8, stride=64), :]
                    )
        return carry

    lax.fori_loop(0, 32, place, 0, unroll=4)


def words_of(code, s):
    row = (code >> 19) * TILE_R + ((code >> 17) & 3) * 128
    top, bottom = (code >> 7) & 127, code & 127
    shift = jnp.arange(NB_DEV, dtype=I32)[None, :]

    def packed(first, final):
        hit = (final >= 0) & (first < 128 + TAPS - 1)
        one = (hit & (top >= first - (TAPS - 1))).astype(I32)
        two = (hit & (bottom <= final)).astype(I32)
        both = one << shift | two << (shift + 16)
        return jnp.sum(both, axis=1)

    direct = s * ROWS - row
    mirror = GRID - ROWS + 1 - s * ROWS - row
    middle = GRID // 2 - row
    middle = packed(middle, middle) * (s == 0).astype(I32)
    return packed(direct, direct + ROWS - 1), packed(mirror, mirror + ROWS - 1), middle


def gridded(words, codes_all, s, x_all, taps):
    vmem = pl.BlockSpec(memory_space=pltpu.VMEM)
    smem = pl.BlockSpec(memory_space=pltpu.SMEM)
    first, second, turn = column_tables()
    return pl.pallas_call(
        grid_kernel,
        out_shape=jax.ShapeDtypeStruct((DEVICES, 64, 128), BF16),
        in_specs=[smem] * 6 + [pl.BlockSpec(memory_space=pl.ANY)] * 2 + [vmem] * 3,
        out_specs=vmem,
        scratch_shapes=[
            pltpu.VMEM((2, HEAD + GRID + 32, 128), F32),
            pltpu.VMEM((128 * 64, 128), F32),
            pltpu.VMEM((DEVICES * 16, 128), F32),
            pltpu.VMEM((64 * 8, 128), F32),
            pltpu.VMEM((2, 64, 128), F32),
            pltpu.VMEM((DEVICES, AGR, 128), BF16),
            pltpu.VMEM((128, 128, 128), BF16),
            pltpu.VMEM((BATCH * 104, 128), F32),
            pltpu.SMEM((4096,), I32),
            pltpu.SemaphoreType.DMA((2,)),
        ],
        compiler_params=pltpu.CompilerParams(vmem_limit_bytes=60 * 1024 * 1024),
        name="grid_columns",
    )(
        *words, codes_all.reshape(BLOCKS), jnp.asarray(bit_table()), s.reshape(1).astype(I32),
        x_all, jnp.asarray(first), taps, jnp.asarray(second), jnp.asarray(turn),
    )


def imaged(got):
    first, turn, last = row_tables()
    return pl.pallas_call(
        image_kernel,
        out_shape=jax.ShapeDtypeStruct((2, 64, GRID), F32),
        grid=(4,),
        in_specs=[
            pl.BlockSpec((DEVICES, 16, 128), lambda i: (0, i, 0)),
            pl.BlockSpec((256, 256), lambda i: (0, 0)),
            pl.BlockSpec((3, 256, 128), lambda i: (0, 0, 0)),
            pl.BlockSpec((64, 256), lambda i: (0, 0)),
        ],
        out_specs=pl.BlockSpec((2, 16, GRID), lambda i: (0, i, 0)),
        scratch_shapes=[
            pltpu.VMEM((DEVICES * 16, 128), F32),
            pltpu.VMEM((16 * 64, 128), F32),
            pltpu.VMEM((16 * 64, 128), F32),
        ],
        compiler_params=pltpu.CompilerParams(vmem_limit_bytes=48 * 1024 * 1024),
        name="image_rows",
    )(got, jnp.asarray(first), jnp.asarray(turn), jnp.asarray(last))


def sorted_blocks(visibilities, keep_flags, kernel_index, row_offset, col_offset, cell_index, tile_row):
    vmem = pl.BlockSpec(memory_space=pltpu.VMEM)
    smem = pl.BlockSpec(memory_space=pltpu.SMEM)
    return pl.pallas_call(
        sort_kernel,
        out_shape=jax.ShapeDtypeStruct((AGR, 128), BF16),
        in_specs=[vmem] * 5 + [smem] * 2,
        out_specs=vmem,
        scratch_shapes=[pltpu.VMEM((128, 128), F32), pltpu.VMEM((NOTES, 128), F32)],
        name="sort_blocks",
    )(visibilities, keep_flags, kernel_index, row_offset, col_offset, cell_index, tile_row)


def shards(visibilities, keep_flags, kernel_index, row_offset, col_offset, cell_index, tile_row, kernel_taps):
    s = lax.axis_index("au") * 8 + lax.axis_index("vert")
    ordered = sorted_blocks(
        visibilities, keep_flags, kernel_index, row_offset, col_offset, cell_index, tile_row.reshape(NB_DEV)
    )
    x_all = gathered(ordered).reshape(DEVICES, AGR, 128)
    found = x_all[:, NOTES : NOTES + 4, :NB_DEV].astype(I32)
    codes_all = ((found[:, 0] * 32 + found[:, 1]) << 14) | (found[:, 2] << 7) | found[:, 3]
    words = words_of(codes_all, s)
    taps = kernel_taps.transpose(1, 2, 0).reshape(2 * TAPS, 32)
    sent = gridded(words, codes_all, s, x_all, taps)
    got = lax.all_to_all(sent, BOTH, split_axis=0, concat_axis=0, tiled=True)
    return imaged(got)


def solution(mesh):
    in_specs = (
        P(BOTH, None, None, None),
        P(BOTH, None),
        P(BOTH, None),
        P(BOTH, None),
        P(BOTH, None),
        P(BOTH),
        P(BOTH, None),
        P(),
    )
    out_specs = P(None, BOTH, None)
    return jax.shard_map(shards, mesh=mesh, in_specs=in_specs, out_specs=out_specs, check_vma=False)
```
